512 devices in a mesh: batch: 16 (over y, x_lo, core), fsdp: 32 (over z, x_hi).
Axes of the slice: x: 4 (x_hi: 2, x_lo: 2; x = x_hi * 2 + x_lo), y: 4, z: 16, core: 2. Of those that a mesh axis runs over, the one named last changes fastest.
Arguments:
- queries: bfloat16 [1024, 4096], P(('batch', 'fsdp')), may hold values from -1 to 1
- passages: bfloat16 [1024, 4096], P(('batch', 'fsdp')), may hold values from -0.5 to 0.5
- positives: int32 [1024], P(('batch', 'fsdp')), may hold values from 0 to 1023
- hidden: bfloat16 [1024, 256, 4096], P(('batch', 'fsdp')), may hold values from -6 to 6
- norm_gain: bfloat16 [4096], replicated, may hold values from 0.5 to 1.5
- last_query: bfloat16 [1024, 2048], P(('batch', 'fsdp')), may hold values from -6 to 6
- frozen_key_weight: bfloat16 [4096, 512], P('fsdp'), may hold values from -0.09375 to 0.09375
- frozen_value_weight: bfloat16 [4096, 512], P('fsdp'), may hold values from -0.09375 to 0.09375
- key_down: bfloat16 [4096, 64], P('fsdp'), may hold values from -0.09375 to 0.09375
- key_adapter_up: bfloat16 [64, 512], replicated, may hold values from -0.75 to 0.75
- value_down: bfloat16 [4096, 64], P('fsdp'), may hold values from -0.09375 to 0.09375
- value_adapter_up: bfloat16 [64, 512], replicated, may hold values from -0.75 to 0.75
- out_weight: bfloat16 [2048, 4096], P('batch', 'fsdp'), may hold values from -0.125 to 0.125
Outputs:
- losses: float32 [1024], P(('batch', 'fsdp'))
- query_embedding_gradient: float32 [1024, 4096], P(('batch', 'fsdp'))
- passage_embedding_gradient: float32 [1024, 4096], P(('batch', 'fsdp'))
- key_down_grad: float32 [4096, 64], P(('batch', 'fsdp'))
- value_down_grad: float32 [4096, 64], P(('batch', 'fsdp'))
- key_up_grad: float32 [64, 512], replicated
- value_up_grad: float32 [64, 512], replicated
The draws below stay inside these ranges and needn't reach their ends.
All inputs are finite; a program needn't handle non-finite values.
Results may differ from the reference program's by a relative error of at most 0.02.
Values may be sent and summed in bfloat16 or wider, within the bound.
A program may use at most 64 MiB of HBM per device.

```python
import jax
import jax.numpy as jnp
from jax import lax

MODEL_WIDTH = 4096
HEAD_WIDTH = 128
HQ = 16
KEY_VALUE_HEADS = 4
ADAPTER_RANK = 64
PASS_DEV = 2
PAIR_DEV = 2
LEN = 256
PAIRS = 1024
PASS = 1024


def passage_base(key):
    inner_key = jax.random.fold_in(key, 11)
    spread = 0.0625
    return jnp.clip(jax.random.normal(inner_key, (PAIRS, MODEL_WIDTH), jnp.float32) * spread, -0.5, 0.5)


def aligned_rows(base_rows, values, low, middle, high):
    row_ids = jnp.arange(PAIRS)
    leading = base_rows[(row_ids * 7 + 3) % PAIRS]
    trailing = base_rows[(row_ids * 13 + 5) % PAIRS]
    strength = jnp.array([low, middle, high], jnp.float32)[row_ids % 3]
    aligned = 0.5 * strength[:, None] * (leading + trailing)
    chosen = (row_ids % 8 == 0)[:, None]
    return jnp.where(chosen, aligned, values)


def draw_passages(key, part):
    return passage_base(key).astype(jnp.bfloat16)


def draw_queries(key, part):
    base_rows = passage_base(key)
    key = jax.random.fold_in(key, 2)
    values = jax.random.normal(key, (PAIRS, MODEL_WIDTH), jnp.float32) * 0.0625
    values = aligned_rows(base_rows, values, 1.0, 1.25, 1.5)
    return jnp.clip(values, -1.0, 1.0).astype(jnp.bfloat16)


def set_ends(entries, stream_key, smallest, largest):
    extent = entries.shape
    place = [jax.random.randint(jax.random.fold_in(stream_key, axis), (), 0, extent[axis]) for axis in range(len(extent))]
    entries = entries.at[tuple(place)].set(smallest)
    longest = extent.index(max(extent))
    place[longest] = (place[longest] + 1) % extent[longest]
    return entries.at[tuple(place)].set(largest)


def level_of(key, extent, shards, smallest, largest):
    loudness, own = 1.0, jax.random.fold_in(key, 6)
    for dim, shards_of in shards:
        draws = jnp.exp(jax.random.uniform(jax.random.fold_in(own, dim), (shards_of,), jnp.float32, smallest / len(shards), largest / len(shards)))
        loudness = loudness * jnp.repeat(draws, extent[dim] // shards_of).reshape([-1 if axis == dim else 1 for axis in range(len(extent))])
    return loudness


def bell_draw(own_key, extent, scale, bound, shards=(), kind=jnp.bfloat16):
    result = scale * jax.random.normal(own_key, extent, jnp.float32)
    if shards:
        result = result * level_of(own_key, extent, shards, -0.22, 0.18)
    return jnp.clip(result, -bound, bound).astype(kind)


def setup_inputs(seed: int = 0) -> dict:
    key_list = jax.random.split(jax.random.key(seed), 14)
    queries = draw_queries(jax.random.fold_in(key_list[13], 71), 0)
    passages = draw_passages(jax.random.fold_in(key_list[13], 71), 0)
    positives = set_ends(jax.random.randint(key_list[2], (PAIRS,), 0, PAIRS), jax.random.fold_in(key_list[2], 1), 0, PAIRS - 1).astype(jnp.int32)
    hidden = bell_draw(key_list[3], (PASS, LEN, MODEL_WIDTH), 1.0, 6.0, ((0, 512),))
    norm_gain = jnp.clip(1.0 + 0.1 * jax.random.normal(key_list[4], (MODEL_WIDTH,), jnp.float32), 0.5, 1.5).astype(jnp.bfloat16)
    last_query = bell_draw(key_list[5], (PASS, HQ * HEAD_WIDTH), 1.0, 6.0, ((0, 512),))
    frozen_key_weight = bell_draw(key_list[6], (MODEL_WIDTH, KEY_VALUE_HEADS * HEAD_WIDTH), MODEL_WIDTH ** -0.5, 0.09375, ((0, 32),))
    frozen_value_weight = bell_draw(key_list[7], (MODEL_WIDTH, KEY_VALUE_HEADS * HEAD_WIDTH), MODEL_WIDTH ** -0.5, 0.09375, ((0, 32),))
    key_down = bell_draw(key_list[8], (MODEL_WIDTH, ADAPTER_RANK), MODEL_WIDTH ** -0.5, 0.09375, ((0, 32),))
    key_adapter_up = bell_draw(key_list[9], (ADAPTER_RANK, KEY_VALUE_HEADS * HEAD_WIDTH), ADAPTER_RANK ** -0.5, 0.75)
    value_down = bell_draw(key_list[10], (MODEL_WIDTH, ADAPTER_RANK), MODEL_WIDTH ** -0.5, 0.09375, ((0, 32),))
    value_adapter_up = bell_draw(key_list[11], (ADAPTER_RANK, KEY_VALUE_HEADS * HEAD_WIDTH), ADAPTER_RANK ** -0.5, 0.75)
    out_weight = bell_draw(key_list[12], (HQ * HEAD_WIDTH, MODEL_WIDTH), (HQ * HEAD_WIDTH) ** -0.5, 0.125, ((0, 16), (1, 32)))
    return dict(queries=queries, passages=passages, positives=positives, hidden=hidden, norm_gain=norm_gain, last_query=last_query, frozen_key_weight=frozen_key_weight, frozen_value_weight=frozen_value_weight, key_down=key_down, key_adapter_up=key_adapter_up, value_down=value_down, value_adapter_up=value_adapter_up, out_weight=out_weight)


INVERSE_TEMP_SCL = 20.0
ADAPTER_SCALE = 2.0
EPSILON = 1e-06
ROTARY_BASE = 1000000.0

def rotary_tables(length, head_size):
    half_size = head_size // 2
    position = jnp.arange(length, dtype=jnp.float32)
    frequency = ROTARY_BASE ** (-(jnp.arange(half_size, dtype=jnp.float32) * 2.0 / head_size))
    angles = position[:, None] * frequency[None, :]
    return (jnp.cos(angles)[:, None, :], jnp.sin(angles)[:, None, :])

def encode_backward(tokens, query_vec, grad_vec, norm_gain, frozen_key_weight, frozen_value_weight, key_down, key_adapter_up, value_down, value_adapter_up):
    length = tokens.shape[0]
    head_size = HEAD_WIDTH
    kv_width = frozen_key_weight.shape[1]
    groups = kv_width // head_size
    group_size = query_vec.shape[0] // kv_width
    tokens_wide = tokens.astype(jnp.float32)
    normed = (tokens_wide * lax.rsqrt(lax.optimization_barrier(jnp.mean(tokens_wide * tokens_wide, axis=-1, keepdims=True)) + EPSILON) * norm_gain.astype(jnp.float32)).astype(jnp.bfloat16)
    low_key = jnp.dot(normed, key_down, preferred_element_type=jnp.float32).astype(jnp.bfloat16)
    low_value = jnp.dot(normed, value_down, preferred_element_type=jnp.float32).astype(jnp.bfloat16)
    key_rows = jnp.dot(normed, frozen_key_weight, preferred_element_type=jnp.float32) + ADAPTER_SCALE * jnp.dot(low_key, key_adapter_up, preferred_element_type=jnp.float32)
    key_rows = key_rows.reshape(length, groups, head_size)
    cosine, sine = rotary_tables(length, head_size)
    leading = key_rows[..., :head_size // 2]
    trailing = key_rows[..., head_size // 2:]
    key_rows = jnp.concatenate([leading * cosine - trailing * sine, trailing * cosine + leading * sine], axis=-1).astype(jnp.bfloat16)
    values = (jnp.dot(normed, frozen_value_weight, preferred_element_type=jnp.float32) + ADAPTER_SCALE * jnp.dot(low_value, value_adapter_up, preferred_element_type=jnp.float32)).astype(jnp.bfloat16)
    values = values.reshape(length, groups, head_size)
    query_heads = query_vec.astype(jnp.float32).reshape(groups, group_size, head_size)
    similarity_scores = jnp.einsum('gjd,tgd->gjt', query_heads, key_rows.astype(jnp.float32)) * head_size ** (-0.5)
    attention = jax.nn.softmax(similarity_scores, axis=-1)
    grad_heads = grad_vec.astype(jnp.float32).reshape(groups, group_size, head_size)
    prob_grad = jnp.einsum('gjd,tgd->gjt', grad_heads, values.astype(jnp.float32))
    expected = lax.optimization_barrier(jnp.sum(attention * prob_grad, axis=-1, keepdims=True))
    score_grad = attention * (prob_grad - expected)
    value_grad = jnp.einsum('gjt,gjd->tgd', attention, grad_heads)
    rotated_grad = jnp.einsum('gjt,gjd->tgd', score_grad, query_heads) * head_size ** (-0.5)
    grad_lead = rotated_grad[..., :head_size // 2]
    grad_trail = rotated_grad[..., head_size // 2:]
    key_grad = jnp.concatenate([grad_lead * cosine + grad_trail * sine, grad_trail * cosine - grad_lead * sine], axis=-1)
    key_cast = key_grad.reshape(length, kv_width).astype(jnp.bfloat16)
    value_cast = value_grad.reshape(length, kv_width).astype(jnp.bfloat16)
    contract = (((0,), (0,)), ((), ()))
    up_key = ADAPTER_SCALE * lax.dot_general(low_key, key_cast, contract, preferred_element_type=jnp.float32)
    up_value = ADAPTER_SCALE * lax.dot_general(low_value, value_cast, contract, preferred_element_type=jnp.float32)
    back_key = jnp.dot(key_cast, key_adapter_up.T, preferred_element_type=jnp.float32).astype(jnp.bfloat16)
    back_value = jnp.dot(value_cast, value_adapter_up.T, preferred_element_type=jnp.float32).astype(jnp.bfloat16)
    down_key = ADAPTER_SCALE * lax.dot_general(normed, back_key, contract, preferred_element_type=jnp.float32)
    down_value = ADAPTER_SCALE * lax.dot_general(normed, back_value, contract, preferred_element_type=jnp.float32)
    return (down_key, down_value, up_key, up_value)

def reference(queries, passages, positives, hidden, norm_gain, last_query, frozen_key_weight, frozen_value_weight, key_down, key_adapter_up, value_down, value_adapter_up, out_weight):
    similarity_scores = INVERSE_TEMP_SCL * jnp.dot(queries, passages.T, preferred_element_type=jnp.float32)
    row_max = lax.optimization_barrier(jnp.max(similarity_scores, axis=1))
    exponent = jnp.exp(similarity_scores - row_max[:, None])
    denominator = lax.optimization_barrier(jnp.sum(exponent, axis=1))
    column_ids = jnp.arange(similarity_scores.shape[1], dtype=jnp.int32)
    onehot = (positives[:, None] == column_ids[None, :]).astype(jnp.float32)
    positive = lax.optimization_barrier(jnp.sum(similarity_scores * onehot, axis=1))
    losses = row_max + jnp.log(denominator) - positive
    softmax_weights = (exponent / denominator[:, None] - onehot).astype(jnp.bfloat16)
    query_embedding_gradient = INVERSE_TEMP_SCL * jnp.dot(softmax_weights, passages, preferred_element_type=jnp.float32)
    passage_embedding_gradient = INVERSE_TEMP_SCL * jnp.dot(softmax_weights.T, queries, preferred_element_type=jnp.float32)
    stride = PAIR_DEV // PASS_DEV
    cotangent = passage_embedding_gradient.reshape(PASS, stride, MODEL_WIDTH)[:, 0].astype(jnp.bfloat16)
    head_grads = lax.optimization_barrier(jnp.dot(cotangent, out_weight.T, preferred_element_type=jnp.float32).astype(jnp.bfloat16))
    kv_width = frozen_key_weight.shape[1]
    rank_size = key_down.shape[1]
    start_totals = (jnp.zeros((MODEL_WIDTH, rank_size), jnp.float32), jnp.zeros((MODEL_WIDTH, rank_size), jnp.float32), jnp.zeros((rank_size, kv_width), jnp.float32), jnp.zeros((rank_size, kv_width), jnp.float32))

    def accumulate(totals, element):
        tokens, query_vec, grad_vec = element
        terms = encode_backward(tokens, query_vec, grad_vec, norm_gain, frozen_key_weight, frozen_value_weight, key_down, key_adapter_up, value_down, value_adapter_up)
        return (tuple((total_part + term_part for total_part, term_part in zip(totals, terms))), None)
    totals, unused = lax.scan(accumulate, start_totals, (hidden, last_query, head_grads))
    return (losses, query_embedding_gradient, passage_embedding_gradient, totals[0], totals[1], totals[2], totals[3])
```

```python
import jax
import jax.numpy as jnp
from jax import lax
from jax.experimental import pallas as pl
from jax.experimental.pallas import tpu as pltpu
from jax.sharding import PartitionSpec as P

F32 = jnp.float32
BF16 = jnp.bfloat16
MESH = pl.DeviceIdType.MESH
HEAD = 128
SCALE = 20.0
EPSILON = 1e-06
ROTARY_BASE = 1000000.0
VMEM_BYTES = 56 * 1024 * 1024


def position():
    b = lax.axis_index("batch")
    f = lax.axis_index("fsdp")
    y = b // 4
    xlo = (b // 2) % 2
    c = b % 2
    z = f // 2
    xhi = f % 2
    return (b, f, y, xlo, c, z, xhi)


def remote(src, dst, send_sem, recv_sem, b, f):
    return pltpu.make_async_remote_copy(
        src_ref=src,
        dst_ref=dst,
        send_sem=send_sem,
        recv_sem=recv_sem,
        device_id=(b, f),
        device_id_type=MESH,
    )


def loop(lo, hi, body):
    def step(i, carry):
        body(i)
        return carry

    lax.fori_loop(lo, hi, step, 0)


def iota(shape, dim):
    return lax.broadcasted_iota(jnp.int32, shape, dim)


def dot(a, b, ca=1, cb=0, precision=None):
    return lax.dot_general(
        a, b, (((ca,), (cb,)), ((), ())), preferred_element_type=F32, precision=precision
    )


def gather_kernel(
    q_in,
    p_in,
    wo_in,
    wh_in,
    loss_out,
    qg_out,
    pg_out,
    head_out,
    wf,
    qs,
    ps,
    ws,
    wg,
    qwg,
    st,
    pgs,
    pgr,
    hps,
    hpr,
    qgs,
    qgx,
    qgr,
    q_send,
    q_recv,
    qx_send,
    qx_recv,
    w_send,
    w_recv,
    p_send,
    p_recv,
    w1_send,
    w1_recv,
    w2_send,
    w2_recv,
    w3_sem,
    qw_send,
    qw_recv,
    qwx_send,
    qwx_recv,
    st_send,
    st_recv,
    pg_send,
    pg_recv,
    hp_send,
    hp_recv,
    qg_send,
    qg_recv,
    qgx_sem,
    ax_send,
    ax_recv,
    ay_send,
    ay_recv,
    by_send,
    by_recv,
    bx_send,
    bx_recv,
    wx_send,
    wx_recv,
    loc_sem,
):
    b, f, y, xlo, c, z, xhi = position()
    pi = (b // 2) * 2 + xhi
    sib = b + 1 - 2 * c
    line = c * 16 + z

    def plane_dev(t):
        return ((t // 2) * 2 + c, z * 2 + t % 2)

    def line_dev(s):
        return ((b // 2) * 2 + s // 16, (s % 16) * 2 + xhi)

    barrier = pltpu.get_barrier_semaphore()

    def greet_plane(i):
        tb, tf = plane_dev((pi + i) % 16)
        pl.semaphore_signal(barrier, inc=1, device_id=(tb, tf), device_id_type=MESH)

    def greet_line(i):
        tb, tf = line_dev((line + i) % 32)
        pl.semaphore_signal(barrier, inc=1, device_id=(tb, tf), device_id_type=MESH)

    loop(1, 16, greet_plane)
    loop(1, 32, greet_line)
    qs[c, z] = q_in[...]
    ps[pi] = p_in[...]
    wf[c, z, xhi, y, xlo] = wh_in[pl.ds((y * 2 + xlo) * 16, 16), :]
    pl.semaphore_wait(barrier, 46)

    right = ((z + 1) % 16) * 2 + xhi
    left = ((z + 15) % 16) * 2 + xhi

    def q_hop(src, way, to):
        return remote(qs.at[c, src], qs.at[c, src], q_send.at[way, src], q_recv.at[src], b, to)

    def w_hop(src, way, to):
        piece = wf.at[c, src, xhi, y, xlo]
        return remote(piece, piece, w_send.at[way, src], w_recv.at[src], b, to)

    def q_cross(src):
        return remote(qs.at[c, src], qs.at[c, src], qx_send.at[src], qx_recv.at[src], sib, f)

    q_hop(z, 0, right).start()
    q_hop(z, 1, left).start()
    q_cross(z).start()
    w_hop(z, 0, right).start()
    w_hop(z, 1, left).start()

    def wo_move(zp):
        return remote(
            wo_in.at[pl.ds(zp * 16, 16), :],
            ws.at[z % 2, z // 2],
            w1_send.at[zp],
            w1_recv.at[z],
            (b // 2) * 2 + xlo,
            (2 * zp + c) * 2 + xhi,
        )

    def wo_start(zp):
        here = jnp.logical_and(c == xlo, 2 * zp + c == z)

        @pl.when(jnp.logical_not(here))
        def _():
            wo_move(zp).start()

        @pl.when(here)
        def _():
            ws[z % 2, z // 2] = wo_in[pl.ds(zp * 16, 16), :]

    loop(0, 8, wo_start)

    def p_move(i):
        t = (pi + i) % 16
        tb, tf = plane_dev(t)
        return remote(ps.at[pi], ps.at[pi], p_send.at[t], p_recv.at[pi], tb, tf)

    loop(1, 16, lambda i: p_move(i).start())

    def ring(k):
        a = (z + 16 - k) % 16
        q_hop(a, 0, right).wait_recv()

        @pl.when(k < 8)
        def _():
            q_hop(a, 0, right).start()

        q_cross(a).start()
        w_hop(a, 0, right).wait_recv()

        @pl.when(k < 8)
        def _():
            w_hop(a, 0, right).start()

        @pl.when(k < 8)
        def _():
            e = (z + k) % 16
            q_hop(e, 1, left).wait_recv()

            @pl.when(k < 7)
            def _():
                q_hop(e, 1, left).start()

            q_cross(e).start()
            w_hop(e, 1, left).wait_recv()

            @pl.when(k < 7)
            def _():
                w_hop(e, 1, left).start()

    loop(1, 4, ring)

    mine = c == xlo

    def wo_slot(t, yy):
        return wg.at[:, t, :, pl.ds((c * 4 + yy) * 16, 16), :]

    def wo_spread(i):
        t = (pi + i) % 16
        tb, tf = plane_dev(t)
        return remote(ws, wo_slot(xhi, y), w2_send.at[t], w2_recv.at[y * 2 + xhi], tb, tf)

    @pl.when(mine)
    def _():
        def wait_one(zz):
            @pl.when(jnp.logical_not(jnp.logical_and(z % 2 == c, zz == z)))
            def _():
                remote(
                    wo_in.at[pl.ds(0, 16), :],
                    ws.at[zz % 2, zz // 2],
                    w1_send.at[0],
                    w1_recv.at[zz],
                    sib,
                    f,
                ).wait_recv()

        loop(0, 16, wait_one)
        loop(1, 16, lambda i: wo_spread(i).start())
        wg[:, xhi, :, pl.ds((c * 4 + y) * 16, 16), :] = ws[...]

    loop(4, 9, ring)

    lo_z, hi_z = pl.ds(0, 8), pl.ds(8, 8)

    def x_of(i):
        return (xhi * 2 + xlo + i) % 4

    def x_dev(i):
        x = x_of(i)
        return (y * 4 + (x % 2) * 2 + c, z * 2 + x // 2)

    def y_dev(i):
        return (((y + i) % 4) * 4 + xlo * 2 + c, f)

    def ax_move(i):
        part = wf.at[c, lo_z, xhi, y, xlo]
        tb, tf = x_dev(i)
        return remote(part, part, ax_send.at[i], ax_recv.at[4 - i], tb, tf)

    def by_move(i):
        part = wf.at[c, hi_z, xhi, y, xlo]
        tb, tf = y_dev(i)
        return remote(part, part, by_send.at[i], by_recv.at[4 - i], tb, tf)

    loop(1, 4, lambda i: ax_move(i).start())
    loop(1, 4, lambda i: by_move(i).start())

    def p_wait(i):
        t = (pi + i) % 16
        remote(ps.at[t], ps.at[t], p_send.at[t], p_recv.at[t], sib, f).wait_recv()

    loop(1, 16, p_wait)

    def qx_wait(zz):
        slot = qs.at[1 - c, zz]
        remote(slot, slot, qx_send.at[zz], qx_recv.at[zz], sib, f).wait_recv()

    loop(0, 16, qx_wait)

    q_all = qs[...].reshape(512, 640)
    q_rows = q_all[:, :512]
    p_rows = ps[...].reshape(256, 512)
    wide = dot(p_rows, q_rows, 1, 1).reshape(32, 8, 512)
    same = iota((32, 8, 512), 1) == iota((32, 8, 512), 2) % 8
    folded = jnp.sum(jnp.where(same, wide, 0.0), axis=1)
    fold = (iota((512, 64), 0) // 8 == iota((512, 64), 1)).astype(F32)
    scores = SCALE * dot(folded, fold, precision=lax.Precision.HIGHEST)
    marks = dot(q_all[:, 512:], fold.astype(BF16), 0, 0)
    target = marks[0:1] * 32.0 + marks[1:2]
    pid = iota((32, 64), 0)
    ptile = pid // 2
    ids = (((ptile // 2) * 2 + c) * 32 + z * 2 + ptile % 2) * 2 + pid % 2
    hit = (ids.astype(F32) == target).astype(F32)
    top = jnp.max(scores, axis=0, keepdims=True)
    local = top + jnp.log(jnp.sum(jnp.exp(scores - top), axis=0, keepdims=True))
    st[line] = jnp.zeros((4, 128), F32)
    st[line, 0:1, 0:64] = local
    st[line, 1:2, 0:64] = jnp.sum(scores * hit, axis=0, keepdims=True)

    def st_move(i):
        s = (line + i) % 32
        tb, tf = line_dev(s)
        return remote(st.at[line], st.at[line], st_send.at[s], st_recv.at[line], tb, tf)

    loop(1, 32, lambda i: st_move(i).start())

    half = wg.at[:, :, :, pl.ds(c * 64, 64), :]
    other = wg.at[:, :, :, pl.ds((1 - c) * 64, 64), :]

    def wo_wait(s):
        @pl.when(jnp.logical_not(jnp.logical_and(mine, s == y * 2 + xhi)))
        def _():
            slot = wo_slot(s % 2, s // 2)
            remote(ws, slot, w2_send.at[0], w2_recv.at[s], sib, f).wait_recv()

    loop(0, 8, wo_wait)
    cross = remote(half, half, w3_sem.at[0], w3_sem.at[1], sib, f)
    cross.start()
    remote(other, other, w3_sem.at[0], w3_sem.at[1], sib, f).wait_recv()
    q_half = qs[c].reshape(256, 640)
    prod = jnp.zeros((256, 1024), F32)
    for a in range(4):
        prod += dot(
            q_half[:, a * 128 : (a + 1) * 128], wg[a // 2, a % 2].reshape(1024, 128), 1, 1
        )
    qw = jnp.zeros((256, 128), F32)
    chunk = iota((256, 128), 0) % 8
    for a in range(8):
        qw += jnp.where(chunk == a, prod[:, a * 128 : (a + 1) * 128], 0.0)
    qwg[z, c] = jnp.sum(qw.reshape(32, 8, 128), axis=1).astype(BF16)

    def qw_move(i):
        zz = (z + i) % 16
        return remote(
            qwg.at[z, c], qwg.at[z, c], qw_send.at[zz], qw_recv.at[z], b, zz * 2 + xhi
        )

    def qw_cross(zz):
        return remote(qwg.at[zz, c], qwg.at[zz, c], qwx_send.at[zz], qwx_recv.at[zz], sib, f)

    loop(1, 16, lambda i: qw_move(i).start())
    qw_cross(z).start()

    def ax_wait(i):
        x = x_of(i)
        part = wf.at[c, lo_z, x // 2, y, x % 2]
        remote(part, part, ax_send.at[i], ax_recv.at[i], sib, f).wait_recv()

    def by_wait(i):
        part = wf.at[c, hi_z, xhi, (y + i) % 4, xlo]
        remote(part, part, by_send.at[i], by_recv.at[i], sib, f).wait_recv()

    def ay_move(i):
        part = wf.at[c, lo_z, :, y]
        tb, tf = y_dev(i)
        return remote(part, part, ay_send.at[i], ay_recv.at[4 - i], tb, tf)

    def bx_move(i):
        part = wf.at[c, hi_z, xhi, :, xlo]
        tb, tf = x_dev(i)
        return remote(part, part, bx_send.at[i], bx_recv.at[4 - i], tb, tf)

    loop(1, 4, ax_wait)
    loop(1, 4, lambda i: ay_move(i).start())
    loop(1, 4, by_wait)
    loop(1, 4, lambda i: bx_move(i).start())

    def wx_a(yy, n):
        part = wf.at[c, lo_z, :, yy]
        return remote(part, part, wx_send.at[n], wx_recv.at[n], sib, f)

    def wx_b(x, n):
        part = wf.at[c, hi_z, x // 2, :, x % 2]
        return remote(part, part, wx_send.at[n + 4], wx_recv.at[n + 4], sib, f)

    wx_a(y, 0).start()
    wx_b(xhi * 2 + xlo, 0).start()

    def st_wait(i):
        s = (line + i) % 32
        remote(st.at[s], st.at[s], st_send.at[s], st_recv.at[s], sib, f).wait_recv()

    loop(1, 32, st_wait)
    stats = st[...]
    peak = jnp.max(stats, axis=0)
    total = peak + jnp.log(jnp.sum(jnp.exp(stats - peak[None]), axis=0))
    picked = jnp.sum(stats, axis=0)
    lse = total[0:1, :64]
    loss_out[...] = jnp.zeros_like(loss_out)
    loss_out[0:1, 0:64] = lse - picked[1:2, :64]
    weights = (jnp.exp(scores - lse) - hit).astype(BF16)

    rows8 = (iota((256, 32), 0) // 8 == iota((256, 32), 1)).astype(BF16)
    cols8 = (iota((64, 512), 1) // 8 == iota((64, 512), 0)).astype(BF16)
    spread = dot(dot(rows8, weights).astype(BF16), cols8)
    diag = iota((256, 512), 0) % 8 == iota((256, 512), 1) % 8
    spread = jnp.where(diag, spread, 0.0).astype(BF16)
    pgs[...] = (SCALE * dot(spread, q_rows)).astype(BF16).reshape(16, 16, 512)

    def pg_move(i):
        t = (pi + i) % 16
        tb, tf = plane_dev(t)
        return remote(pgs.at[t], pgr.at[pi], pg_send.at[t], pg_recv.at[pi], tb, tf)

    def hp_move(i):
        t = (pi + i) % 16
        tb, tf = plane_dev(t)
        return remote(hps.at[t], hpr.at[pi], hp_send.at[t], hp_recv.at[pi], tb, tf)

    def qw_wait(i):
        zz = (z + i) % 16
        remote(qwg.at[zz, c], qwg.at[zz, c], qw_send.at[zz], qw_recv.at[zz], sib, f).wait_recv()
        qw_cross(zz).start()

    loop(1, 16, qw_wait)

    def qwx_wait(zz):
        slot = qwg.at[zz, 1 - c]
        remote(slot, slot, qwx_send.at[zz], qwx_recv.at[zz], sib, f).wait_recv()

    loop(0, 16, qwx_wait)
    rows16 = (iota((512, 32), 0) // 16 == iota((512, 32), 1)).astype(BF16)
    cols64 = (iota((64, 1024), 1) % 64 == iota((64, 1024), 0)).astype(BF16)
    tall = dot(dot(rows16, weights).astype(BF16), cols64)
    diag = iota((512, 1024), 0) % 16 == iota((512, 1024), 1) // 64
    tall = jnp.where(diag, tall, 0.0).astype(BF16)
    hps[...] = (SCALE * dot(tall, qwg[...].reshape(1024, 128))).astype(BF16).reshape(16, 32, 128)
    loop(1, 16, lambda i: hp_move(i).start())
    loop(1, 16, lambda i: pg_move(i).start())
    hpr[pi] = hps[pi]
    pgr[pi] = pgs[pi]

    qgs[...] = (SCALE * dot(spread, p_rows, 0, 0)).astype(BF16).reshape(2, 16, 16, 512)
    swap = remote(qgs.at[1 - c], qgx, qgx_sem.at[0], qgx_sem.at[1], sib, f)
    swap.start()
    swap.wait_recv()
    qgs[c] = (qgs[c].astype(F32) + qgx[...].astype(F32)).astype(BF16)

    def qg_move(i):
        zz = (z + i) % 16
        return remote(qgs.at[c, zz], qgr.at[z], qg_send.at[zz], qg_recv.at[z], b, zz * 2 + xhi)

    loop(1, 16, lambda i: qg_move(i).start())
    qgr[z] = qgs[c, z]

    def hp_wait(i):
        t = (pi + i) % 16
        remote(hps.at[t], hpr.at[t], hp_send.at[t], hp_recv.at[t], sib, f).wait_recv()

    def pg_wait(i):
        t = (pi + i) % 16
        remote(pgs.at[t], pgr.at[t], pg_send.at[t], pg_recv.at[t], sib, f).wait_recv()

    def qg_wait(i):
        t = (z + i) % 16
        remote(qgs.at[c, t], qgr.at[t], qg_send.at[t], qg_recv.at[t], sib, f).wait_recv()

    loop(1, 16, hp_wait)
    head_out[...] = jnp.sum(hpr[...].astype(F32), axis=0)
    loop(1, 16, pg_wait)
    pg_out[...] = jnp.sum(pgr[...].astype(F32), axis=0)

    def ay_wait(i):
        part = wf.at[c, lo_z, :, (y + i) % 4]
        remote(part, part, ay_send.at[i], ay_recv.at[i], sib, f).wait_recv()
        wx_a((y + i) % 4, i).start()

    def bx_wait(i):
        x = x_of(i)
        part = wf.at[c, hi_z, x // 2, :, x % 2]
        remote(part, part, bx_send.at[i], bx_recv.at[i], sib, f).wait_recv()
        wx_b(x, i).start()

    loop(1, 4, ay_wait)
    loop(1, 4, bx_wait)
    loop(1, 16, qg_wait)
    qg_out[...] = jnp.sum(qgr[...].astype(F32), axis=0)

    def wx_wait(n):
        x = x_of(n)
        part = wf.at[1 - c, lo_z, :, (y + n) % 4]
        remote(part, part, wx_send.at[n], wx_recv.at[n], sib, f).wait_recv()
        part = wf.at[1 - c, hi_z, x // 2, :, x % 2]
        remote(part, part, wx_send.at[n + 4], wx_recv.at[n + 4], sib, f).wait_recv()

    loop(0, 4, wx_wait)

    def ring_sent(k):
        a = (z + 16 - k) % 16
        q_hop(a, 0, right).wait_send()
        w_hop(a, 0, right).wait_send()

        @pl.when(k < 7)
        def _():
            e = (z + k) % 16
            q_hop(e, 1, left).wait_send()
            w_hop(e, 1, left).wait_send()

    loop(0, 8, ring_sent)
    loop(0, 16, lambda zz: q_cross(zz).wait_send())

    def wo_sent(zp):
        @pl.when(jnp.logical_not(jnp.logical_and(mine, 2 * zp + c == z)))
        def _():
            wo_move(zp).wait_send()

    loop(0, 8, wo_sent)

    @pl.when(mine)
    def _():
        loop(1, 16, lambda i: wo_spread(i).wait_send())

    cross.wait_send()
    loop(1, 16, lambda i: p_move(i).wait_send())
    loop(1, 32, lambda i: st_move(i).wait_send())
    loop(1, 16, lambda i: qw_move(i).wait_send())
    loop(0, 16, lambda zz: qw_cross(zz).wait_send())
    loop(1, 16, lambda i: pg_move(i).wait_send())
    loop(1, 16, lambda i: hp_move(i).wait_send())
    swap.wait_send()
    loop(1, 16, lambda i: qg_move(i).wait_send())
    loop(1, 4, lambda i: ax_move(i).wait_send())
    loop(1, 4, lambda i: by_move(i).wait_send())
    loop(1, 4, lambda i: ay_move(i).wait_send())
    loop(1, 4, lambda i: bx_move(i).wait_send())

    def wx_sent(n):
        wx_a((y + n) % 4, n).wait_send()
        wx_b(x_of(n), n).wait_send()

    loop(0, 4, wx_sent)


def gather_call(q, p, wo, wh):
    dma = pltpu.SemaphoreType.DMA
    vm = pl.BlockSpec(memory_space=pltpu.VMEM)
    return pl.pallas_call(
        gather_kernel,
        out_shape=(
            jax.ShapeDtypeStruct((8, 128), F32),
            jax.ShapeDtypeStruct((16, 512), F32),
            jax.ShapeDtypeStruct((16, 512), F32),
            jax.ShapeDtypeStruct((32, 128), F32),
            jax.ShapeDtypeStruct((2, 16, 2, 4, 2, 16, 640), BF16),
        ),
        in_specs=[vm] * 4,
        out_specs=(vm,) * 5,
        scratch_shapes=[
            pltpu.VMEM((2, 16, 16, 640), BF16),
            pltpu.VMEM((16, 16, 512), BF16),
            pltpu.VMEM((2, 8, 16, 128), BF16),
            pltpu.VMEM((2, 2, 8, 128, 128), BF16),
            pltpu.VMEM((16, 2, 32, 128), BF16),
            pltpu.VMEM((32, 4, 128), F32),
            pltpu.VMEM((16, 16, 512), BF16),
            pltpu.VMEM((16, 16, 512), BF16),
            pltpu.VMEM((16, 32, 128), BF16),
            pltpu.VMEM((16, 32, 128), BF16),
            pltpu.VMEM((2, 16, 16, 512), BF16),
            pltpu.VMEM((16, 16, 512), BF16),
            pltpu.VMEM((16, 16, 512), BF16),
            dma((2, 16)),
            dma((16,)),
            dma((16,)),
            dma((16,)),
            dma((2, 16)),
            dma((16,)),
            dma((16,)),
            dma((16,)),
            dma((8,)),
            dma((16,)),
            dma((16,)),
            dma((8,)),
            dma((2,)),
            dma((16,)),
            dma((16,)),
            dma((16,)),
            dma((16,)),
            dma((32,)),
            dma((32,)),
            dma((16,)),
            dma((16,)),
            dma((16,)),
            dma((16,)),
            dma((16,)),
            dma((16,)),
            dma((2,)),
            dma((4,)),
            dma((4,)),
            dma((4,)),
            dma((4,)),
            dma((4,)),
            dma((4,)),
            dma((4,)),
            dma((4,)),
            dma((8,)),
            dma((8,)),
            dma((1,)),
        ],
        compiler_params=pltpu.CompilerParams(
            collective_id=0, has_side_effects=True, vmem_limit_bytes=VMEM_BYTES
        ),
    )(q, p, wo, wh)


def reduce_kernel(
    d_in,
    u_in,
    d_out,
    uk_out,
    uv_out,
    d1,
    r1,
    d2,
    r2,
    d3,
    u1,
    v1,
    u2,
    v3,
    u3,
    u4,
    u5,
    one_send,
    one_recv,
    d2_send,
    d2_recv,
    d3_send,
    d3_recv,
    u2_send,
    u2_recv,
    u3_send,
    u3_recv,
    u4_send,
    u4_recv,
):
    b, f, y, xlo, c, z, xhi = position()
    pi = (b // 2) * 2 + xhi
    sib = b + 1 - 2 * c

    def plane_dev(t):
        return ((t // 2) * 2 + c, z * 2 + t % 2)

    barrier = pltpu.get_barrier_semaphore()

    def greet_plane(i):
        q = ((b // 2) + i) % 8
        pl.semaphore_signal(
            barrier, inc=1, device_id=(q * 2 + c, z * 2), device_id_type=MESH
        )
        pl.semaphore_signal(
            barrier, inc=1, device_id=(q * 2 + c, z * 2 + 1), device_id_type=MESH
        )

    def greet_line(i):
        pl.semaphore_signal(barrier, inc=1, device_id=(b, (f + i) % 32), device_id_type=MESH)

    pl.semaphore_signal(barrier, inc=1, device_id=(sib, f), device_id_type=MESH)
    loop(1, 8, greet_plane)
    loop(1, 32, greet_line)
    pl.semaphore_wait(barrier, 46)

    u_swap = remote(u_in.at[1 - c], u1, one_send.at[0], one_recv.at[0], sib, f)
    d_swap = remote(d_in.at[:, 1 - c], d1, one_send.at[1], one_recv.at[1], sib, f)
    u_swap.start()
    d_swap.start()
    u_swap.wait_recv()
    v1[...] = (u_in[c].astype(F32) + u1[...].astype(F32)).astype(BF16)

    def u2_move(i):
        t = (pi + i) % 16
        tb, tf = plane_dev(t)
        return remote(v1.at[t], u2.at[pi], u2_send.at[t], u2_recv.at[pi], tb, tf)

    def d2_move(i):
        t = (pi + i) % 16
        tb, tf = plane_dev(t)
        return remote(r1.at[t], d2.at[pi], d2_send.at[t], d2_recv.at[pi], tb, tf)

    loop(1, 16, lambda i: u2_move(i).start())
    u2[pi] = v1[pi]
    d_swap.wait_recv()
    r1[...] = (
        (d_in[:, c].astype(F32) + d1[...].astype(F32)).astype(BF16).reshape(16, 128, 128)
    )
    loop(1, 16, lambda i: d2_move(i).start())
    d2[pi] = r1[pi]

    def u2_wait(i):
        t = (pi + i) % 16
        remote(v1.at[t], u2.at[t], u2_send.at[t], u2_recv.at[t], sib, f).wait_recv()

    loop(1, 16, u2_wait)
    v3[...] = jnp.sum(u2[...].astype(F32), axis=0)
    u3[z] = v3[...]

    def u3_move(i):
        zz = (z + i) % 16
        return remote(v3, u3.at[z], u3_send.at[zz], u3_recv.at[z], b, zz * 2 + xhi)

    loop(1, 16, lambda i: u3_move(i).start())

    def d2_wait(i):
        t = (pi + i) % 16
        remote(r1.at[t], d2.at[t], d2_send.at[t], d2_recv.at[t], sib, f).wait_recv()

    loop(1, 16, d2_wait)
    r2[...] = jnp.sum(d2[...].astype(F32), axis=0).reshape(16, 8, 128)

    def d3_move(k):
        return remote(
            r2.at[k], d3.at[z], d3_send.at[k], d3_recv.at[z], b, (8 * xhi + k // 2) * 2 + k % 2
        )

    own = jnp.logical_and(z // 8 == xhi, True)

    def d3_self(k):
        return (8 * xhi + k // 2) * 2 + k % 2 == f

    def d3_start(k):
        @pl.when(jnp.logical_not(d3_self(k)))
        def _():
            d3_move(k).start()

        @pl.when(d3_self(k))
        def _():
            d3[z] = r2[k]

    loop(0, 16, d3_start)

    def u3_wait(i):
        t = (z + i) % 16
        remote(v3, u3.at[t], u3_send.at[t], u3_recv.at[t], sib, f).wait_recv()

    loop(1, 16, u3_wait)
    u4[pi] = jnp.sum(u3[...], axis=0)

    def u4_move(i):
        t = (pi + i) % 16
        tb, tf = plane_dev(t)
        return remote(u4.at[pi], u4.at[pi], u4_send.at[t], u4_recv.at[pi], tb, tf)

    loop(1, 16, lambda i: u4_move(i).start())

    def d3_wait(zz):
        @pl.when(jnp.logical_not(jnp.logical_and(own, zz == z)))
        def _():
            remote(r2.at[0], d3.at[zz], d3_send.at[0], d3_recv.at[zz], sib, f).wait_recv()

    loop(0, 16, d3_wait)
    d_out[...] = jnp.sum(d3[...], axis=0)

    def u4_wait(i):
        t = (pi + i) % 16
        remote(u4.at[t], u4.at[t], u4_send.at[t], u4_recv.at[t], sib, f).wait_recv()

    loop(1, 16, u4_wait)
    back = remote(u4, u5, one_send.at[2], one_recv.at[2], sib, f)
    back.start()
    back.wait_recv()

    def put(out, src):
        full = src[...].reshape(256, 128)
        for k in range(4):
            out[:, k * 128 : (k + 1) * 128] = full[k * 64 : (k + 1) * 64]

    @pl.when(c == 0)
    def _():
        put(uk_out, u4)
        put(uv_out, u5)

    @pl.when(c == 1)
    def _():
        put(uk_out, u5)
        put(uv_out, u4)

    u_swap.wait_send()
    d_swap.wait_send()
    back.wait_send()
    loop(1, 16, lambda i: u2_move(i).wait_send())
    loop(1, 16, lambda i: d2_move(i).wait_send())
    loop(1, 16, lambda i: u3_move(i).wait_send())
    loop(1, 16, lambda i: u4_move(i).wait_send())

    def d3_sent(k):
        @pl.when(jnp.logical_not(d3_self(k)))
        def _():
            d3_move(k).wait_send()

    loop(0, 16, d3_sent)


def reduce_call(d, u):
    dma = pltpu.SemaphoreType.DMA
    vm = pl.BlockSpec(memory_space=pltpu.VMEM)
    return pl.pallas_call(
        reduce_kernel,
        out_shape=(
            jax.ShapeDtypeStruct((8, 128), F32),
            jax.ShapeDtypeStruct((64, 512), F32),
            jax.ShapeDtypeStruct((64, 512), F32),
        ),
        in_specs=[vm] * 2,
        out_specs=(vm,) * 3,
        scratch_shapes=[
            pltpu.VMEM((8, 256, 128), BF16),
            pltpu.VMEM((16, 128, 128), BF16),
            pltpu.VMEM((16, 128, 128), BF16),
            pltpu.VMEM((16, 8, 128), F32),
            pltpu.VMEM((16, 8, 128), F32),
            pltpu.VMEM((16, 16, 128), BF16),
            pltpu.VMEM((16, 16, 128), BF16),
            pltpu.VMEM((16, 16, 128), BF16),
            pltpu.VMEM((16, 128), F32),
            pltpu.VMEM((16, 16, 128), F32),
            pltpu.VMEM((16, 16, 128), F32),
            pltpu.VMEM((16, 16, 128), F32),
            dma((3,)),
            dma((3,)),
        ]
        + [dma((16,))] * 10,
        compiler_params=pltpu.CompilerParams(
            collective_id=1, has_side_effects=True, vmem_limit_bytes=VMEM_BYTES
        ),
    )(d, u)


def rotary_tables(length):
    half = HEAD // 2
    place = jnp.arange(length, dtype=F32)
    frequency = ROTARY_BASE ** (-(jnp.arange(half, dtype=F32) * 2.0 / HEAD))
    angles = place[:, None] * frequency[None, :]
    return (jnp.cos(angles)[:, None, :], jnp.sin(angles)[:, None, :])


def encode_backward(tokens, query, grad, gain, weights, key_up, value_up):
    count, length, width = tokens.shape
    groups = 4
    rows = count * length
    wide = tokens.astype(F32).reshape(rows, width)
    normed = (
        wide
        * lax.rsqrt(jnp.mean(wide * wide, axis=-1, keepdims=True) + EPSILON)
        * gain.astype(F32)
    ).astype(BF16)
    key_all = jnp.dot(normed, weights[0], preferred_element_type=F32)
    value_all = jnp.dot(normed, weights[1], preferred_element_type=F32)
    low_key = key_all[:, 512:576].astype(BF16)
    low_value = value_all[:, 512:576].astype(BF16)
    keys = key_all[:, :512] + 2.0 * jnp.dot(low_key, key_up, preferred_element_type=F32)
    values = (
        value_all[:, :512] + 2.0 * jnp.dot(low_value, value_up, preferred_element_type=F32)
    ).astype(BF16)
    keys = keys.reshape(count, length, groups, HEAD)
    cosine, sine = rotary_tables(length)
    lead, trail = keys[..., : HEAD // 2], keys[..., HEAD // 2 :]
    keys = jnp.concatenate(
        [lead * cosine - trail * sine, trail * cosine + lead * sine], axis=-1
    ).astype(BF16)
    values = values.reshape(count, length, groups, HEAD)
    q = query.reshape(count, groups, 4, HEAD)
    g = grad.reshape(count, groups, 4, HEAD)
    scores = jnp.einsum("pgjd,ptgd->pgjt", q, keys, preferred_element_type=F32) * HEAD ** (-0.5)
    attention = jax.nn.softmax(scores, axis=-1)
    prob = jnp.einsum("pgjd,ptgd->pgjt", g, values, preferred_element_type=F32)
    expected = jnp.sum(attention * prob, axis=-1, keepdims=True)
    score_grad = attention * (prob - expected)
    value_grad = jnp.einsum(
        "pgjt,pgjd->ptgd", attention.astype(BF16), g, preferred_element_type=F32
    )
    rotated = jnp.einsum(
        "pgjt,pgjd->ptgd", score_grad.astype(BF16), q, preferred_element_type=F32
    ) * HEAD ** (-0.5)
    lead, trail = rotated[..., : HEAD // 2], rotated[..., HEAD // 2 :]
    key_grad = jnp.concatenate(
        [lead * cosine + trail * sine, trail * cosine - lead * sine], axis=-1
    )
    key_cast = key_grad.reshape(rows, 512).astype(BF16)
    value_cast = value_grad.reshape(rows, 512).astype(BF16)
    up = [
        2.0 * dot(low, cast, 0, 0) for low, cast in ((low_key, key_cast), (low_value, value_cast))
    ]
    back = jnp.concatenate(
        [dot(key_cast, key_up, 1, 1), dot(value_cast, value_up, 1, 1)], axis=1
    ).astype(BF16)
    down = 2.0 * dot(normed, back, 0, 0)
    return (down, up[0], up[1])


def shards(
    queries,
    passages,
    positives,
    hidden,
    norm_gain,
    last_query,
    frozen_key_weight,
    frozen_value_weight,
    key_down,
    key_adapter_up,
    value_down,
    value_adapter_up,
    out_weight,
):
    b = lax.axis_index("batch")
    c = b % 2
    z = lax.axis_index("fsdp") // 2
    first = (jnp.arange(16) % 8 == 0)[:, None]
    spot = jnp.repeat(positives, 8)[:, None]
    lane = jnp.arange(128)[None, :]
    marks = jnp.where(lane == 0, spot // 32, jnp.where(lane == 1, spot % 32, 0))
    marks = jnp.where(first, marks, 0).astype(BF16)
    q_slab = jnp.concatenate([queries.reshape(16, 512), marks], axis=1)
    p_slab = passages.reshape(16, 512)
    pad = jnp.zeros((128, 64), BF16)
    mine = jnp.where(
        c == 0,
        jnp.concatenate([frozen_key_weight, key_down, pad], axis=1),
        jnp.concatenate([frozen_value_weight, value_down, pad], axis=1),
    )
    loss, q_grad, p_grad, head, full = gather_call(q_slab, p_slab, out_weight, mine)
    losses = lax.dynamic_slice(loss[0], ((c * 16 + z) * 2,), (2,))
    head = head.reshape(2, 8, 2, 2, 4, 16).transpose(0, 4, 3, 2, 1, 5).reshape(2, 2048)
    head = head.astype(BF16)
    down, up_key, up_value = encode_backward(
        hidden,
        last_query,
        head,
        norm_gain,
        full.reshape(2, 4096, 640),
        key_adapter_up,
        value_adapter_up,
    )
    up = jnp.stack([up_key, up_value]).reshape(2, 64, 4, 128).transpose(0, 2, 1, 3)
    grads, up_key, up_value = reduce_call(
        down.astype(BF16).reshape(8, 2, 256, 128), up.astype(BF16).reshape(2, 16, 16, 128)
    )
    return (
        losses,
        q_grad.reshape(2, 4096),
        p_grad.reshape(2, 4096),
        grads[:, :64],
        grads[:, 64:],
        up_key,
        up_value,
    )


def solution(mesh):
    rows = P(("batch", "fsdp"), None)
    placed = (
        rows,
        rows,
        P(("batch", "fsdp")),
        P(("batch", "fsdp"), None, None),
        P(),
        rows,
        P("fsdp", None),
        P("fsdp", None),
        P("fsdp", None),
        P(),
        P("fsdp", None),
        P(),
        P("batch", "fsdp"),
    )
    return jax.shard_map(
        shards,
        mesh=mesh,
        in_specs=placed,
        out_specs=(P(("batch", "fsdp")), rows, rows, rows, rows, P(), P()),
        check_vma=False,
    )
```

```python
import jax
import jax.numpy as jnp
import numpy as np
from jax import lax
from jax.experimental import pallas as pl
from jax.experimental.pallas import tpu as pltpu
from jax.sharding import PartitionSpec as P

F32 = jnp.float32
BF16 = jnp.bfloat16
MESH = pl.DeviceIdType.MESH
HEAD = 128
SCALE = 20.0
EPSILON = 1e-06
ROTARY_BASE = 1000000.0
VMEM_BYTES = 56 * 1024 * 1024
ROOT = HEAD ** (-0.5)


def position():
    b = lax.axis_index("batch")
    f = lax.axis_index("fsdp")
    y = b // 4
    xlo = (b // 2) % 2
    c = b % 2
    z = f // 2
    xhi = f % 2
    return (b, f, y, xlo, c, z, xhi)


def remote(src, dst, send_sem, recv_sem, b, f):
    return pltpu.make_async_remote_copy(
        src_ref=src,
        dst_ref=dst,
        send_sem=send_sem,
        recv_sem=recv_sem,
        device_id=(b, f),
        device_id_type=MESH,
    )


def loop(lo, hi, body):
    def step(i, carry):
        body(i)
        return carry

    lax.fori_loop(lo, hi, step, 0)


def iota(shape, dim):
    return lax.broadcasted_iota(jnp.int32, shape, dim)


def dot(a, b, ca=1, cb=0, precision=None):
    return lax.dot_general(
        a, b, (((ca,), (cb,)), ((), ())), preferred_element_type=F32, precision=precision
    )


def far_first(i):
    return 8 + (i // 2) * (2 * (i % 2) - 1)


INPUTS = (
    "q_in", "p_in", "pos_in", "hid_in", "gain_in", "lq_in", "fk_in", "fv_in",
    "kd_in", "ku_in", "vd_in", "vu_in", "wo_in", "cos_in", "sin_in",
)
OUTPUTS = ("loss_out", "qg_out", "pg_out", "dk_out", "dv_out", "uk_out", "uv_out")
BUFFERS = {
    "tmp": ((16, 512), F32),
    "lq": ((2, 16, 128), F32),
    "hid": ((512, 4096), BF16),
    "qs": ((2, 4, 4, 16, 640), BF16),
    "ps": ((16, 16, 512), BF16),
    "ws": ((2, 8, 16, 128), BF16),
    "wg": ((2, 2, 8, 128, 128), BF16),
    "qwg": ((16, 2, 32, 128), BF16),
    "st": ((32, 4, 128), F32),
    "pgs": ((16, 16, 512), BF16),
    "pgr": ((16, 16, 512), BF16),
    "hps": ((16, 32, 128), BF16),
    "hpr": ((16, 32, 128), BF16),
    "qgs": ((2, 16, 16, 512), BF16),
    "qgx": ((16, 16, 512), BF16),
    "qgr": ((16, 16, 512), BF16),
    "wk": ((4, 4, 2, 4, 2, 16, 640), BF16),
    "wv": ((4, 4, 2, 4, 2, 16, 512), BF16),
    "ku": ((128, 512), BF16),
    "vu": ((128, 512), BF16),
    "raw_k": ((512, 640), F32),
    "raw_v": ((512, 512), F32),
    "low": ((512, 128), BF16),
    "keys": ((512, 512), BF16),
    "values": ((512, 512), BF16),
    "back": ((128, 512), BF16),
    "att": ((2, 16, 256), F32),
    "dt": ((8, 2, 2, 128, 128), BF16),
    "d1": ((8, 2, 128, 128), BF16),
    "r1": ((16, 128, 128), BF16),
    "d2": ((16, 128, 128), BF16),
    "r2": ((16, 8, 128), F32),
    "d3": ((16, 8, 128), F32),
    "u0": ((2, 4, 64, 128), BF16),
    "u1": ((4, 64, 128), BF16),
    "v1": ((16, 16, 128), BF16),
    "u2": ((16, 16, 128), BF16),
    "v3": ((16, 128), F32),
    "u3": ((16, 16, 128), F32),
    "u4": ((16, 16, 128), F32),
    "u5": ((16, 16, 128), F32),
}
SEMAPHORES = {
    "hid_sem": (1,),
    "q1": (2, 4), "q2": (2, 4), "qx": (2, 4),
    "w1": (2, 4), "w2": (2, 4), "wx": (2, 8),
    "ax": (2, 4), "ay": (2, 4), "bx": (2, 4), "by": (2, 4),
    "p": (2, 16), "o1": (2, 16), "o2": (2, 16), "o3": (2,),
    "qw": (2, 16), "qwx": (2, 16), "sts": (2, 32),
    "pg": (2, 16), "hp": (2, 16), "qg": (2, 16), "qgc": (2,),
    "one": (2, 3), "sd2": (2, 16), "sd3": (2, 16),
    "su2": (2, 16), "su3": (2, 16), "su4": (2, 16),
}


class Refs:
    pass


def kernel(*refs):
    r = Refs()
    for name, ref in zip((*INPUTS, *OUTPUTS, *BUFFERS, *SEMAPHORES), refs, strict=True):
        setattr(r, name, ref)
    b, f, y, xlo, c, z, xhi = position()
    zh, zl = z // 4, z % 4
    pi = (b // 2) * 2 + xhi
    sib = b + 1 - 2 * c
    line = c * 16 + z
    OUT, IN = 0, 1

    def plane_dev(t):
        return ((t // 2) * 2 + c, z * 2 + t % 2)

    def line_dev(s):
        return ((b // 2) * 2 + s // 16, (s % 16) * 2 + xhi)

    def z_dev(zz):
        return (b, zz * 2 + xhi)

    def x_of(i):
        return (xhi * 2 + xlo + i) % 4

    def x_dev(i):
        x = x_of(i)
        return (y * 4 + (x % 2) * 2 + c, z * 2 + x // 2)

    def y_dev(i):
        return (((y + i) % 4) * 4 + xlo * 2 + c, f)

    def send(src, dst, sems, out, into, dev):
        return remote(src, dst, sems.at[OUT, out], sems.at[IN, into], dev[0], dev[1])

    def arrived(dst, sems, into):
        remote(dst, dst, sems.at[OUT, into], sems.at[IN, into], sib, f).wait_recv()

    hid_copy = pltpu.make_async_copy(r.hid_in, r.hid, r.hid_sem.at[0])
    hid_copy.start()
    barrier = pltpu.get_barrier_semaphore()

    def greet(dev):
        pl.semaphore_signal(barrier, inc=1, device_id=dev, device_id_type=MESH)

    def greet_line(i):
        zz = (z + far_first(i)) % 16
        greet(line_dev(zz))
        greet(line_dev(16 + zz))

    loop(1, 16, greet_line)
    loop(1, 16, lambda i: greet(plane_dev((pi + i) % 16)))
    greet((sib, f))

    def slab(ref):
        rows = ref[...].astype(F32)
        for j in range(2):
            for k in range(8):
                r.tmp[j * 8 + k : j * 8 + k + 1, :] = rows[j : j + 1, k * 512 : (k + 1) * 512]
        return r.tmp[...].astype(BF16)

    r.qs[c, zh, zl, :, 0:512] = slab(r.q_in)
    r.ps[pi] = slab(r.p_in)
    row, lane = iota((16, 128), 0), iota((16, 128), 1)
    mark = jnp.zeros((16, 128), F32)
    for j in range(2):
        spot = r.pos_in[j]
        high, low = (spot // 32).astype(F32), (spot % 32).astype(F32)
        mark = jnp.where((row == j * 8) & (lane == 0), high, mark)
        mark = jnp.where((row == j * 8) & (lane == 1), low, mark)
    r.qs[c, zh, zl, :, 512:640] = mark.astype(BF16)
    piece = pl.ds(pl.multiple_of((y * 2 + xlo) * 16, 16), 16)

    @pl.when(c == 0)
    def _():
        r.wk[zh, zl, xhi, y, xlo, :, 0:512] = r.fk_in[piece, :]
        r.wk[zh, zl, xhi, y, xlo, :, 512:640] = jnp.concatenate(
            [r.kd_in[piece, :], r.vd_in[piece, :]], axis=1
        )

    @pl.when(c == 1)
    def _():
        r.wv[zh, zl, xhi, y, xlo] = r.fv_in[piece, :]

    pl.semaphore_wait(barrier, 46)

    def far(i):
        return z_dev((z + 4 * i) % 16)

    def near(i):
        return z_dev((z + i - 4 * (i // 3)) % 16)

    def q1(i):
        own = r.qs.at[c, zh, zl]
        return send(own, own, r.q1, i, 4 - i, far(i))

    def q2(i):
        part = r.qs.at[c, :, zl]
        return send(part, part, r.q2, i, 4 - i, near(i))

    def qx(i):
        part = r.qs.at[c, :, (zl + i) % 4]
        return send(part, part, r.qx, i, i, (sib, f))

    loop(1, 4, lambda i: q1(i).start())

    mine = c == xlo

    def o1(zp):
        return send(
            r.wo_in.at[pl.ds(zp * 16, 16), :],
            r.ws.at[z % 2, z // 2],
            r.o1,
            zp,
            z,
            ((b // 2) * 2 + xlo, (2 * zp + c) * 2 + xhi),
        )

    def o1_start(zp):
        here = jnp.logical_and(mine, 2 * zp + c == z)

        @pl.when(jnp.logical_not(here))
        def _():
            o1(zp).start()

        @pl.when(here)
        def _():
            r.ws[z % 2, z // 2] = r.wo_in[pl.ds(zp * 16, 16), :]

    loop(0, 8, o1_start)

    def p_move(i):
        t = (pi + i) % 16
        return send(r.ps.at[pi], r.ps.at[pi], r.p, t, pi, plane_dev(t))

    def on_own(body):
        pl.when(c == 0)(lambda: body(r.wk))
        pl.when(c == 1)(lambda: body(r.wv))

    def on_other(body):
        pl.when(c == 0)(lambda: body(r.wv))
        pl.when(c == 1)(lambda: body(r.wk))

    def w1(w, i):
        own = w.at[zh, zl, xhi, y, xlo]
        return send(own, own, r.w1, i, 4 - i, far(i))

    def w2(w, i):
        part = w.at[:, zl, xhi, y, xlo]
        return send(part, part, r.w2, i, 4 - i, near(i))

    lo_z, hi_z = pl.ds(0, 2), pl.ds(2, 2)

    def ax(w, i):
        part = w.at[lo_z, :, xhi, y, xlo]
        return send(part, part, r.ax, i, 4 - i, x_dev(i))

    def by(w, i):
        part = w.at[hi_z, :, xhi, y, xlo]
        return send(part, part, r.by, i, 4 - i, y_dev(i))

    def ay(w, i):
        part = w.at[lo_z, :, :, y]
        return send(part, part, r.ay, i, 4 - i, y_dev(i))

    def bx(w, i):
        part = w.at[hi_z, :, xhi, :, xlo]
        return send(part, part, r.bx, i, 4 - i, x_dev(i))

    def wx_a(w, i):
        part = w.at[lo_z, :, :, (y + i) % 4]
        return send(part, part, r.wx, i, i, (sib, f))

    def wx_b(w, i):
        x = x_of(i)
        part = w.at[hi_z, :, x // 2, :, x % 2]
        return send(part, part, r.wx, 4 + i, 4 + i, (sib, f))

    on_own(lambda w: loop(1, 4, lambda i: w1(w, i).start()))
    loop(1, 16, lambda i: p_move(i).start())

    r.ku[0:64, :] = r.ku_in[...]
    r.ku[64:128, :] = jnp.zeros((64, 512), BF16)
    r.vu[0:64, :] = jnp.zeros((64, 512), BF16)
    r.vu[64:128, :] = r.vu_in[...]
    wide_q = r.lq_in[...].astype(F32)
    for j in range(2):
        for h in range(16):
            r.lq[j, h : h + 1, :] = wide_q[j : j + 1, h * 128 : (h + 1) * 128]

    hid_copy.wait()

    def norm(i):
        rows = pl.ds(pl.multiple_of(i * 32, 32), 32)
        x = r.hid[rows, :].astype(F32)
        scale = lax.rsqrt(jnp.mean(x * x, axis=1, keepdims=True) + EPSILON)
        r.hid[rows, :] = (x * scale * r.gain_in[...].astype(F32)).astype(BF16)

    loop(0, 8, norm)
    loop(1, 4, lambda i: arrived(r.qs.at[c, (zh + i) % 4, zl], r.q1, i))
    loop(1, 4, lambda i: q2(i).start())
    qx(0).start()

    def o2_slot(t, yy):
        return r.wg.at[:, t, :, pl.ds((c * 4 + yy) * 16, 16), :]

    def o2(i):
        t = (pi + i) % 16
        return send(r.ws, o2_slot(xhi, y), r.o2, t, y * 2 + xhi, plane_dev(t))

    @pl.when(mine)
    def _():
        def one(zz):
            @pl.when(jnp.logical_not(jnp.logical_and(z % 2 == c, zz == z)))
            def _():
                arrived(r.ws.at[zz % 2, zz // 2], r.o1, zz)

        loop(0, 16, one)
        loop(1, 16, lambda i: o2(i).start())
        r.wg[:, xhi, :, pl.ds((c * 4 + y) * 16, 16), :] = r.ws[...]

    def w1_done(w):
        loop(1, 4, lambda i: arrived(w.at[(zh + i) % 4, zl, xhi, y, xlo], r.w1, i))
        loop(1, 4, lambda i: w2(w, i).start())

    on_own(w1_done)
    loop(8, 16, norm)

    def q2_done(i):
        arrived(r.qs.at[c, :, (zl + i) % 4], r.q2, i)
        qx(i).start()

    loop(1, 4, q2_done)

    def w2_done(w):
        loop(1, 4, lambda i: arrived(w.at[:, (zl + i) % 4, xhi, y, xlo], r.w2, i))
        loop(1, 4, lambda i: ax(w, i).start())
        loop(1, 4, lambda i: by(w, i).start())

    on_own(w2_done)

    def p_done(i):
        t = (pi + i) % 16
        arrived(r.ps.at[t], r.p, t)

    loop(1, 16, p_done)
    loop(0, 4, lambda i: arrived(r.qs.at[1 - c, :, (zl + i) % 4], r.qx, i))
    q_all = r.qs[...].reshape(512, 640)
    q_rows = q_all[:, :512]
    p_rows = r.ps[...].reshape(256, 512)
    wide = dot(p_rows, q_rows, 1, 1).reshape(32, 8, 512)
    same = iota((32, 8, 512), 1) == iota((32, 8, 512), 2) % 8
    folded = jnp.sum(jnp.where(same, wide, 0.0), axis=1)
    fold = (iota((512, 64), 0) // 8 == iota((512, 64), 1)).astype(F32)
    scores = SCALE * dot(folded, fold, precision=lax.Precision.HIGHEST)
    marks = dot(q_all[:, 512:], fold.astype(BF16), 0, 0)
    target = marks[0:1] * 32.0 + marks[1:2]
    pid = iota((32, 64), 0)
    ptile = pid // 2
    ids = (((ptile // 2) * 2 + c) * 32 + z * 2 + ptile % 2) * 2 + pid % 2
    hit = (ids.astype(F32) == target).astype(F32)
    top = jnp.max(scores, axis=0, keepdims=True)
    local = top + jnp.log(jnp.sum(jnp.exp(scores - top), axis=0, keepdims=True))
    r.st[line] = jnp.zeros((4, 128), F32)
    r.st[line, 0:1, 0:64] = local
    r.st[line, 1:2, 0:64] = jnp.sum(scores * hit, axis=0, keepdims=True)

    def st_move(s):
        return send(r.st.at[line], r.st.at[line], r.sts, s, line, line_dev(s))

    def st_start(i):
        zz = (z + far_first(i)) % 16
        st_move(zz).start()
        st_move(16 + zz).start()

    loop(1, 16, st_start)
    st_move((1 - c) * 16 + z).start()

    half = r.wg.at[:, :, :, pl.ds(c * 64, 64), :]
    other = r.wg.at[:, :, :, pl.ds((1 - c) * 64, 64), :]

    def o2_done(s):
        @pl.when(jnp.logical_not(jnp.logical_and(mine, s == y * 2 + xhi)))
        def _():
            arrived(o2_slot(s % 2, s // 2), r.o2, s)

    loop(0, 8, o2_done)
    o3 = remote(half, half, r.o3.at[0], r.o3.at[1], sib, f)
    o3.start()
    remote(other, other, r.o3.at[0], r.o3.at[1], sib, f).wait_recv()
    q_half = r.qs[c].reshape(256, 640)
    prod = jnp.zeros((256, 1024), F32)
    for a in range(4):
        prod += dot(
            q_half[:, a * 128 : (a + 1) * 128], r.wg[a // 2, a % 2].reshape(1024, 128), 1, 1
        )
    qw = jnp.zeros((256, 128), F32)
    chunk = iota((256, 128), 0) % 8
    for a in range(8):
        qw += jnp.where(chunk == a, prod[:, a * 128 : (a + 1) * 128], 0.0)
    r.qwg[z, c] = jnp.sum(qw.reshape(32, 8, 128), axis=1).astype(BF16)

    def qw_move(i):
        zz = (z + far_first(i)) % 16
        return send(r.qwg.at[z, c], r.qwg.at[z, c], r.qw, zz, z, z_dev(zz))

    def qw_cross(zz):
        return send(r.qwg.at[zz, c], r.qwg.at[zz, c], r.qwx, zz, zz, (sib, f))

    loop(1, 16, lambda i: qw_move(i).start())
    qw_cross(z).start()

    def plane_done(w):
        def a_done(i):
            x = x_of(i)
            arrived(w.at[lo_z, :, x // 2, y, x % 2], r.ax, i)

        loop(1, 4, a_done)
        loop(1, 4, lambda i: ay(w, i).start())
        wx_a(w, 0).start()
        loop(1, 4, lambda i: arrived(w.at[hi_z, :, xhi, (y + i) % 4, xlo], r.by, i))
        loop(1, 4, lambda i: bx(w, i).start())
        wx_b(w, 0).start()

    on_own(plane_done)

    def st_done(i):
        s = (line + i) % 32
        arrived(r.st.at[s], r.sts, s)

    loop(1, 32, st_done)
    stats = r.st[...]
    peak = jnp.max(stats, axis=0)
    total = peak + jnp.log(jnp.sum(jnp.exp(stats - peak[None]), axis=0))
    picked = jnp.sum(stats, axis=0)
    lse = total[0:1, :64]
    weights = (jnp.exp(scores - lse) - hit).astype(BF16)

    def qw_done(i):
        zz = (z + far_first(16 - i)) % 16
        arrived(r.qwg.at[zz, c], r.qw, zz)
        qw_cross(zz).start()

    loop(1, 16, qw_done)
    loop(0, 16, lambda zz: arrived(r.qwg.at[zz, 1 - c], r.qwx, zz))
    rows16 = (iota((512, 32), 0) // 16 == iota((512, 32), 1)).astype(BF16)
    cols64 = (iota((64, 1024), 1) % 64 == iota((64, 1024), 0)).astype(BF16)
    tall = dot(dot(rows16, weights).astype(BF16), cols64)
    diag = iota((512, 1024), 0) % 16 == iota((512, 1024), 1) // 64
    tall = jnp.where(diag, tall, 0.0).astype(BF16)
    r.hps[...] = (
        (SCALE * dot(tall, r.qwg[...].reshape(1024, 128))).astype(BF16).reshape(16, 32, 128)
    )

    def hp_move(i):
        t = (pi + i) % 16
        return send(r.hps.at[t], r.hpr.at[pi], r.hp, t, pi, plane_dev(t))

    def pg_move(i):
        t = (pi + i) % 16
        return send(r.pgs.at[t], r.pgr.at[pi], r.pg, t, pi, plane_dev(t))

    loop(1, 16, lambda i: hp_move(i).start())
    r.hpr[pi] = r.hps[pi]
    rows8 = (iota((256, 32), 0) // 8 == iota((256, 32), 1)).astype(BF16)
    cols8 = (iota((64, 512), 1) // 8 == iota((64, 512), 0)).astype(BF16)
    spread = dot(dot(rows8, weights).astype(BF16), cols8)
    diag = iota((256, 512), 0) % 8 == iota((256, 512), 1) % 8
    spread = jnp.where(diag, spread, 0.0).astype(BF16)
    r.pgs[...] = (SCALE * dot(spread, q_rows)).astype(BF16).reshape(16, 16, 512)
    loop(1, 16, lambda i: pg_move(i).start())
    r.pgr[pi] = r.pgs[pi]

    r.qgs[...] = (SCALE * dot(spread, p_rows, 0, 0)).astype(BF16).reshape(2, 16, 16, 512)
    swap = remote(r.qgs.at[1 - c], r.qgx, r.qgc.at[0], r.qgc.at[1], sib, f)
    swap.start()
    loss = picked[1:2, :64]
    loss = lse - loss
    spot = iota((1, 64), 1)
    pick = [
        jnp.sum(jnp.where(spot == 2 * line + j, loss, 0.0), axis=1, keepdims=True)
        for j in range(2)
    ]
    r.loss_out[...] = jnp.where(iota((8, 128), 1) == 0, pick[0], pick[1])

    def qg_move(i):
        zz = (z + far_first(i)) % 16
        return send(r.qgs.at[c, zz], r.qgr.at[z], r.qg, zz, z, z_dev(zz))

    swap.wait_recv()
    r.qgs[c] = (r.qgs[c].astype(F32) + r.qgx[...].astype(F32)).astype(BF16)
    loop(1, 16, lambda i: qg_move(i).start())
    r.qgr[z] = r.qgs[c, z]

    def rows_done(w):
        def a_done(i):
            arrived(w.at[lo_z, :, :, (y + i) % 4], r.ay, i)
            wx_a(w, i).start()

        def b_done(i):
            x = x_of(i)
            arrived(w.at[hi_z, :, x // 2, :, x % 2], r.bx, i)
            wx_b(w, i).start()

        loop(1, 4, a_done)
        loop(1, 4, b_done)

    on_own(rows_done)

    def cross_done(w):
        def one(i):
            x = x_of(i)
            arrived(w.at[lo_z, :, :, (y + i) % 4], r.wx, i)
            arrived(w.at[hi_z, :, x // 2, :, x % 2], r.wx, 4 + i)

        loop(0, 4, one)

    on_other(cross_done)

    def project(w, raw, k):
        tokens = r.hid[:, pl.ds(pl.multiple_of(k * 1024, 1024), 1024)]
        part = dot(tokens, w[k].reshape(1024, w.shape[-1]))

        @pl.when(k == 0)
        def _():
            raw[...] = part

        @pl.when(k > 0)
        def _():
            raw[...] += part

    loop(0, 4, lambda k: project(r.wk, r.raw_k, k))
    r.low[...] = r.raw_k[:, 512:640].astype(BF16)
    adapted = dot(r.low[...], r.ku[...])
    own_group = iota((16, 512), 0) // 4 == iota((16, 512), 1) // 128

    def by_group(rows):
        return jnp.where(own_group, jnp.concatenate([rows] * 4, axis=1), 0.0).astype(BF16)

    queries = [by_group(r.lq[j]) for j in range(2)]
    for j in range(2):
        tok = slice(j * 256, (j + 1) * 256)
        for g in range(4):
            col = slice(g * 128, (g + 1) * 128)
            key = r.raw_k[tok, col] + 2.0 * adapted[tok, col]
            turned = pltpu.roll(key, 64, axis=1)
            r.keys[tok, col] = (key * r.cos_in[...] + turned * r.sin_in[...]).astype(BF16)
        sim = dot(queries[j], r.keys[tok, :], 1, 1) * ROOT
        sim = jnp.exp(sim - jnp.max(sim, axis=1, keepdims=True))
        r.att[j] = sim / jnp.sum(sim, axis=1, keepdims=True)

    loop(0, 4, lambda k: project(r.wv, r.raw_v, k))
    r.values[...] = (r.raw_v[...] + 2.0 * dot(r.low[...], r.vu[...])).astype(BF16)

    def hp_done(i):
        t = (pi + i) % 16
        arrived(r.hpr.at[t], r.hp, t)

    loop(1, 16, hp_done)
    heads = jnp.sum(r.hpr[...].astype(F32), axis=0).astype(BF16)
    row, lane = iota((128, 128), 0), iota((128, 128), 1)
    tile = (iota((128, 16), 0) % 16 == iota((128, 16), 1)).astype(BF16)
    group = (row % 16 == lane % 16).astype(BF16)
    head, src = iota((16, 128), 0), iota((16, 128), 1)
    place, at_z = src // 16, src % 16
    collect = (
        ((place % 4) * 4 + (place // 4) * 2 + at_z % 2 == head)
    ).astype(BF16)
    for j in range(2):
        tok = slice(j * 256, (j + 1) * 256)
        spread_rows = dot(tile, heads[j * 16 : (j + 1) * 16])
        spread_rows = jnp.where(lane // 16 == row // 16, spread_rows, 0.0).astype(BF16)
        copied = dot(spread_rows, group)
        copied = jnp.where(lane // 16 == (row % 16) // 2, copied, 0.0).astype(BF16)
        grads = by_group(dot(collect, copied))
        prob = dot(grads, r.values[tok, :], 1, 1)
        attention = r.att[j]
        expected = jnp.sum(attention * prob, axis=1, keepdims=True)
        score_grad = attention * (prob - expected)
        r.values[tok, :] = dot(attention.astype(BF16), grads, 0, 0).astype(BF16)
        turned_grad = dot(score_grad.astype(BF16), queries[j], 0, 0) * ROOT
        for g in range(4):
            col = slice(g * 128, (g + 1) * 128)
            part = turned_grad[:, col]
            turned = pltpu.roll(part, 64, axis=1)
            r.keys[tok, col] = (part * r.cos_in[...] - turned * r.sin_in[...]).astype(BF16)

    up_k = (2.0 * dot(r.low[...], r.keys[...], 0, 0)).astype(BF16)
    up_v = (2.0 * dot(r.low[...], r.values[...], 0, 0)).astype(BF16)
    for k in range(4):
        r.u0[0, k] = up_k[0:64, k * 128 : (k + 1) * 128]
        r.u0[1, k] = up_v[64:128, k * 128 : (k + 1) * 128]
    u_swap = send(r.u0.at[1 - c], r.u1, r.one, 0, 0, (sib, f))
    u_swap.start()
    back = dot(r.keys[...], r.ku[...], 1, 1) + dot(r.values[...], r.vu[...], 1, 1)
    r.back[...] = jnp.transpose(back.astype(BF16).astype(F32)).astype(BF16)

    def down(j, cc):
        cols = pl.ds(pl.multiple_of((j * 2 + cc) * 256, 256), 256)
        part = (2.0 * dot(r.back[...], r.hid[:, cols])).astype(BF16)
        r.dt[j, cc, 0] = part[:, :128]
        r.dt[j, cc, 1] = part[:, 128:]

    loop(0, 8, lambda j: down(j, 1 - c))
    d_swap = send(r.dt.at[:, 1 - c], r.d1, r.one, 1, 1, (sib, f))
    d_swap.start()
    u_swap.wait_recv()
    r.v1[...] = (
        (r.u0[c].astype(F32) + r.u1[...].astype(F32)).astype(BF16).reshape(16, 16, 128)
    )

    def u2_move(i):
        t = (pi + i) % 16
        return send(r.v1.at[t], r.u2.at[pi], r.su2, t, pi, plane_dev(t))

    def d2_move(i):
        t = (pi + i) % 16
        return send(r.r1.at[t], r.d2.at[pi], r.sd2, t, pi, plane_dev(t))

    loop(1, 16, lambda i: u2_move(i).start())
    r.u2[pi] = r.v1[pi]
    loop(0, 8, lambda j: down(j, c))
    d_swap.wait_recv()
    r.r1[...] = (
        (r.dt[:, c].astype(F32) + r.d1[...].astype(F32)).astype(BF16).reshape(16, 128, 128)
    )
    loop(1, 16, lambda i: d2_move(i).start())
    r.d2[pi] = r.r1[pi]

    def u2_done(i):
        t = (pi + i) % 16
        arrived(r.u2.at[t], r.su2, t)

    loop(1, 16, u2_done)
    r.v3[...] = jnp.sum(r.u2[...].astype(F32), axis=0)
    r.u3[z] = r.v3[...]

    def u3_move(i):
        zz = (z + far_first(i)) % 16
        return send(r.v3, r.u3.at[z], r.su3, zz, z, z_dev(zz))

    loop(1, 16, lambda i: u3_move(i).start())

    def d2_done(i):
        t = (pi + i) % 16
        arrived(r.d2.at[t], r.sd2, t)

    loop(1, 16, d2_done)
    r.r2[...] = jnp.transpose(jnp.sum(r.d2[...].astype(F32), axis=0)).reshape(16, 8, 128)

    def d3_move(k):
        return send(
            r.r2.at[k], r.d3.at[z], r.sd3, k, z, (b, (8 * xhi + k // 2) * 2 + k % 2)
        )

    def d3_self(k):
        return (8 * xhi + k // 2) * 2 + k % 2 == f

    def d3_start(k):
        @pl.when(jnp.logical_not(d3_self(k)))
        def _():
            d3_move(k).start()

        @pl.when(d3_self(k))
        def _():
            r.d3[z] = r.r2[k]

    loop(0, 16, d3_start)

    def put_rows(out, total):
        r.tmp[...] = total
        for j in range(2):
            for k in range(8):
                out[j : j + 1, k * 512 : (k + 1) * 512] = r.tmp[j * 8 + k : j * 8 + k + 1, :]

    def pg_done(i):
        t = (pi + i) % 16
        arrived(r.pgr.at[t], r.pg, t)

    def qg_done(i):
        t = (z + i) % 16
        arrived(r.qgr.at[t], r.qg, t)

    loop(1, 16, pg_done)
    put_rows(r.pg_out, jnp.sum(r.pgr[...].astype(F32), axis=0))
    loop(1, 16, qg_done)
    put_rows(r.qg_out, jnp.sum(r.qgr[...].astype(F32), axis=0))

    def u3_done(i):
        t = (z + i) % 16
        arrived(r.u3.at[t], r.su3, t)

    loop(1, 16, u3_done)
    r.u4[pi] = jnp.sum(r.u3[...], axis=0)

    def u4_move(i):
        t = (pi + i) % 16
        return send(r.u4.at[pi], r.u4.at[pi], r.su4, t, pi, plane_dev(t))

    loop(1, 16, lambda i: u4_move(i).start())

    def d3_done(zz):
        @pl.when(jnp.logical_not(jnp.logical_and(z // 8 == xhi, zz == z)))
        def _():
            arrived(r.d3.at[zz], r.sd3, zz)

    loop(0, 16, d3_done)
    down_total = jnp.sum(r.d3[...], axis=0)
    r.dk_out[...] = down_total[:, :64]
    r.dv_out[...] = down_total[:, 64:]

    def u4_done(i):
        t = (pi + i) % 16
        arrived(r.u4.at[t], r.su4, t)

    loop(1, 16, u4_done)
    u_back = send(r.u4, r.u5, r.one, 2, 2, (sib, f))
    u_back.start()

    def z_sent(i):
        q1(i).wait_send()
        q2(i).wait_send()

    loop(1, 4, z_sent)
    loop(0, 4, lambda i: qx(i).wait_send())

    def rows_sent(w):
        def one(i):
            w1(w, i).wait_send()
            w2(w, i).wait_send()
            ax(w, i).wait_send()
            ay(w, i).wait_send()
            bx(w, i).wait_send()
            by(w, i).wait_send()

        def two(i):
            wx_a(w, i).wait_send()
            wx_b(w, i).wait_send()

        loop(1, 4, one)
        loop(0, 4, two)

    on_own(rows_sent)

    def o1_sent(zp):
        @pl.when(jnp.logical_not(jnp.logical_and(mine, 2 * zp + c == z)))
        def _():
            o1(zp).wait_send()

    loop(0, 8, o1_sent)

    @pl.when(mine)
    def _():
        loop(1, 16, lambda i: o2(i).wait_send())

    o3.wait_send()
    swap.wait_send()
    u_swap.wait_send()
    d_swap.wait_send()

    def sixteen_sent(i):
        p_move(i).wait_send()
        qw_move(i).wait_send()
        pg_move(i).wait_send()
        hp_move(i).wait_send()
        qg_move(i).wait_send()
        u2_move(i).wait_send()
        d2_move(i).wait_send()
        u3_move(i).wait_send()
        u4_move(i).wait_send()

    loop(1, 16, sixteen_sent)

    def more_sent(k):
        qw_cross(k).wait_send()

        @pl.when(jnp.logical_not(d3_self(k)))
        def _():
            d3_move(k).wait_send()

    loop(0, 16, more_sent)
    loop(1, 32, lambda i: st_move((line + i) % 32).wait_send())

    u_back.wait_recv()

    def put(out, src):
        full = src[...].reshape(256, 128)
        for k in range(4):
            out[:, k * 128 : (k + 1) * 128] = full[k * 64 : (k + 1) * 64]

    @pl.when(c == 0)
    def _():
        put(r.uk_out, r.u4)
        put(r.uv_out, r.u5)

    @pl.when(c == 1)
    def _():
        put(r.uk_out, r.u5)
        put(r.uv_out, r.u4)

    u_back.wait_send()


def rotary_tables(length):
    half = HEAD // 2
    frequency = ROTARY_BASE ** (-(np.arange(half) * 2.0 / HEAD))
    angles = np.arange(length)[:, None] * frequency[None, :]
    cosine, sine = np.cos(angles), np.sin(angles)
    return (
        np.concatenate([cosine, cosine], axis=1).astype(np.float32),
        np.concatenate([-sine, sine], axis=1).astype(np.float32),
    )


def shards(
    queries,
    passages,
    positives,
    hidden,
    norm_gain,
    last_query,
    frozen_key_weight,
    frozen_value_weight,
    key_down,
    key_adapter_up,
    value_down,
    value_adapter_up,
    out_weight,
):
    vm = pl.BlockSpec(memory_space=pltpu.VMEM)
    specs = [vm] * len(INPUTS)
    specs[INPUTS.index("pos_in")] = pl.BlockSpec(memory_space=pltpu.SMEM)
    specs[INPUTS.index("hid_in")] = pl.BlockSpec(memory_space=pl.ANY)
    shapes = ((8, 128), (2, 4096), (2, 4096), (8, 64), (8, 64), (64, 512), (64, 512))
    cosine, sine = rotary_tables(256)
    loss, q_grad, p_grad, down_key, down_value, up_key, up_value = pl.pallas_call(
        kernel,
        out_shape=tuple(jax.ShapeDtypeStruct(shape, F32) for shape in shapes),
        in_specs=specs,
        out_specs=(vm,) * len(shapes),
        scratch_shapes=[pltpu.VMEM(shape, dtype) for shape, dtype in BUFFERS.values()]
        + [pltpu.SemaphoreType.DMA(shape) for shape in SEMAPHORES.values()],
        compiler_params=pltpu.CompilerParams(
            collective_id=0, has_side_effects=True, vmem_limit_bytes=VMEM_BYTES
        ),
    )(
        queries,
        passages,
        positives,
        hidden.reshape(512, 4096),
        norm_gain.reshape(1, 4096),
        last_query,
        frozen_key_weight,
        frozen_value_weight,
        key_down,
        key_adapter_up,
        value_down,
        value_adapter_up,
        out_weight,
        cosine,
        sine,
    )
    return (loss[0, :2], q_grad, p_grad, down_key, down_value, up_key, up_value)


def solution(mesh):
    rows = P(("batch", "fsdp"), None)
    placed = (
        rows,
        rows,
        P(("batch", "fsdp")),
        P(("batch", "fsdp"), None, None),
        P(),
        rows,
        P("fsdp", None),
        P("fsdp", None),
        P("fsdp", None),
        P(),
        P("fsdp", None),
        P(),
        P("batch", "fsdp"),
    )
    return jax.shard_map(
        shards,
        mesh=mesh,
        in_specs=placed,
        out_specs=(P(("batch", "fsdp")), rows, rows, rows, rows, P(), P()),
        check_vma=False,
    )
```

```python
import jax
import jax.numpy as jnp
import numpy as np
from jax import lax
from jax.experimental import pallas as pl
from jax.experimental.pallas import tpu as pltpu
from jax.sharding import PartitionSpec as P

F32 = jnp.float32
BF16 = jnp.bfloat16
MESH = pl.DeviceIdType.MESH
HEAD = 128
SCALE = 20.0
EPSILON = 1e-06
ROTARY_BASE = 1000000.0
VMEM_BYTES = 56 * 1024 * 1024
ROOT = HEAD ** (-0.5)


def position():
    b = lax.axis_index("batch")
    f = lax.axis_index("fsdp")
    y = b // 4
    xlo = (b // 2) % 2
    c = b % 2
    z = f // 2
    xhi = f % 2
    return (b, f, y, xlo, c, z, xhi)


def remote(src, dst, send_sem, recv_sem, b, f):
    return pltpu.make_async_remote_copy(
        src_ref=src,
        dst_ref=dst,
        send_sem=send_sem,
        recv_sem=recv_sem,
        device_id=(b, f),
        device_id_type=MESH,
    )


def loop(lo, hi, body):
    def step(i, carry):
        body(i)
        return carry

    lax.fori_loop(lo, hi, step, 0)


def iota(shape, dim):
    return lax.broadcasted_iota(jnp.int32, shape, dim)


def dot(a, b, ca=1, cb=0, precision=None):
    return lax.dot_general(
        a, b, (((ca,), (cb,)), ((), ())), preferred_element_type=F32, precision=precision
    )


def far_first(i):
    return 8 + (i // 2) * (2 * (i % 2) - 1)


INPUTS = (
    "q_in", "p_in", "pos_in", "hid_in", "gain_in", "lq_in", "fk_in", "fv_in",
    "kd_in", "ku_in", "vd_in", "vu_in", "wo_in", "cos_in", "sin_in",
)
OUTPUTS = ("loss_out", "qg_out", "pg_out", "dk_out", "dv_out", "uk_out", "uv_out")
BUFFERS = {
    "tmp": ((16, 512), F32),
    "lq": ((2, 16, 128), F32),
    "hid": ((512, 4096), BF16),
    "qs": ((2, 4, 4, 16, 640), BF16),
    "ps": ((16, 16, 512), BF16),
    "ws": ((2, 8, 16, 128), BF16),
    "wg": ((2, 2, 8, 128, 128), BF16),
    "qwg": ((16, 2, 32, 128), BF16),
    "st": ((32, 4, 128), F32),
    "pgs": ((16, 16, 512), BF16),
    "pgr": ((16, 16, 512), BF16),
    "hps": ((16, 32, 128), BF16),
    "hpr": ((16, 32, 128), BF16),
    "qgs": ((2, 16, 16, 512), BF16),
    "qgx": ((16, 16, 512), BF16),
    "qgr": ((16, 16, 512), BF16),
    "wk": ((4, 4, 2, 4, 2, 16, 640), BF16),
    "wv": ((4, 4, 2, 4, 2, 16, 512), BF16),
    "dn": ((128, 128), BF16),
    "ku": ((128, 512), BF16),
    "vu": ((128, 512), BF16),
    "raw_k": ((512, 640), F32),
    "raw_v": ((512, 512), F32),
    "low": ((512, 128), BF16),
    "keys": ((512, 512), BF16),
    "values": ((512, 512), BF16),
    "vg": ((512, 512), BF16),
    "gq": ((2, 16, 512), BF16),
    "back": ((128, 512), BF16),
    "att": ((2, 16, 256), F32),
    "dt": ((8, 2, 2, 128, 128), BF16),
    "d1": ((8, 2, 128, 128), BF16),
    "r1": ((16, 128, 128), BF16),
    "d2": ((16, 128, 128), BF16),
    "r2": ((16, 8, 128), F32),
    "d3": ((16, 8, 128), F32),
    "u0": ((2, 4, 64, 128), BF16),
    "u1": ((4, 64, 128), BF16),
    "v1": ((16, 16, 128), BF16),
    "u2": ((16, 16, 128), BF16),
    "v3": ((16, 128), F32),
    "u3": ((16, 16, 128), F32),
    "u4": ((16, 16, 128), F32),
    "u5": ((16, 16, 128), F32),
}
SEMAPHORES = {
    "hid_sem": (1,),
    "q1": (2, 4), "q2": (2, 4), "qx": (2, 4),
    "w1": (2, 4), "w2": (2, 4), "wx": (2, 8),
    "ax": (2, 4), "ay": (2, 6), "bx": (2, 6), "by": (2, 4),
    "p": (2, 16), "o1": (2, 16), "o2": (2, 16), "o3": (2,),
    "qw": (2, 16), "qwx": (2, 16), "sts": (2, 32),
    "pg": (2, 16), "hp": (2, 16), "qg": (2, 16), "qgc": (2,),
    "one": (2, 3), "sd2": (2, 16), "sd3": (2, 16),
    "su2": (2, 16), "su3": (2, 16), "su4": (2, 16),
}


class Refs:
    pass


def kernel(*refs):
    r = Refs()
    for name, ref in zip((*INPUTS, *OUTPUTS, *BUFFERS, *SEMAPHORES), refs, strict=True):
        setattr(r, name, ref)
    b, f, y, xlo, c, z, xhi = position()
    zh, zl = z // 4, z % 4
    pi = (b // 2) * 2 + xhi
    sib = b + 1 - 2 * c
    line = c * 16 + z
    OUT, IN = 0, 1

    def plane_dev(t):
        return ((t // 2) * 2 + c, z * 2 + t % 2)

    def line_dev(s):
        return ((b // 2) * 2 + s // 16, (s % 16) * 2 + xhi)

    def z_dev(zz):
        return (b, zz * 2 + xhi)

    def x_of(i):
        return (xhi * 2 + xlo + i) % 4

    def x_dev(i):
        x = x_of(i)
        return (y * 4 + (x % 2) * 2 + c, z * 2 + x // 2)

    def y_dev(i):
        return (((y + i) % 4) * 4 + xlo * 2 + c, f)

    def send(src, dst, sems, out, into, dev):
        return remote(src, dst, sems.at[OUT, out], sems.at[IN, into], dev[0], dev[1])

    def arrived(dst, sems, into):
        remote(dst, dst, sems.at[OUT, into], sems.at[IN, into], sib, f).wait_recv()

    hid_copy = pltpu.make_async_copy(r.hid_in, r.hid, r.hid_sem.at[0])
    hid_copy.start()
    barrier = pltpu.get_barrier_semaphore()

    def greet(dev):
        pl.semaphore_signal(barrier, inc=1, device_id=dev, device_id_type=MESH)

    def greet_line(i):
        zz = (z + far_first(i)) % 16
        greet(line_dev(zz))
        greet(line_dev(16 + zz))

    loop(1, 16, greet_line)
    loop(1, 16, lambda i: greet(plane_dev((pi + i) % 16)))
    greet((sib, f))

    def slab(ref):
        rows = ref[...].astype(F32)
        for j in range(2):
            for k in range(8):
                r.tmp[j * 8 + k : j * 8 + k + 1, :] = rows[j : j + 1, k * 512 : (k + 1) * 512]
        return r.tmp[...].astype(BF16)

    r.qs[c, zh, zl, :, 0:512] = slab(r.q_in)
    r.ps[pi] = slab(r.p_in)
    row, lane = iota((16, 128), 0), iota((16, 128), 1)
    mark = jnp.zeros((16, 128), F32)
    for j in range(2):
        spot = r.pos_in[j]
        high, low = (spot // 32).astype(F32), (spot % 32).astype(F32)
        mark = jnp.where((row == j * 8) & (lane == 0), high, mark)
        mark = jnp.where((row == j * 8) & (lane == 1), low, mark)
    r.qs[c, zh, zl, :, 512:640] = mark.astype(BF16)
    piece = pl.ds(pl.multiple_of((y * 2 + xlo) * 16, 16), 16)

    @pl.when(c == 0)
    def _():
        r.wk[zh, zl, xhi, y, xlo, :, 0:512] = r.fk_in[piece, :]
        downs = jnp.concatenate([r.kd_in[...], r.vd_in[...]], axis=0).astype(F32)
        r.dn[...] = jnp.transpose(downs).astype(BF16)
        r.wk[zh, zl, xhi, y, xlo, :, 512:640] = r.dn[piece, :]

    @pl.when(c == 1)
    def _():
        r.wv[zh, zl, xhi, y, xlo] = r.fv_in[piece, :]

    pl.semaphore_wait(barrier, 46)

    def far(i):
        return z_dev((z + 4 * i) % 16)

    def near(i):
        return z_dev((z + i - 4 * (i // 3)) % 16)

    def q1(i):
        own = r.qs.at[c, zh, zl]
        return send(own, own, r.q1, i, 4 - i, far(i))

    def q2(i):
        part = r.qs.at[c, :, zl]
        return send(part, part, r.q2, i, 4 - i, near(i))

    def qx(i):
        part = r.qs.at[c, :, (zl + i) % 4]
        return send(part, part, r.qx, i, i, (sib, f))

    mine = c == xlo

    def o1(zp):
        return send(
            r.wo_in.at[pl.ds(zp * 16, 16), :],
            r.ws.at[z % 2, z // 2],
            r.o1,
            zp,
            z,
            ((b // 2) * 2 + xlo, (2 * zp + c) * 2 + xhi),
        )

    def o1_start(zp):
        here = jnp.logical_and(mine, 2 * zp + c == z)

        @pl.when(jnp.logical_not(here))
        def _():
            o1(zp).start()

        @pl.when(here)
        def _():
            r.ws[z % 2, z // 2] = r.wo_in[pl.ds(zp * 16, 16), :]

    loop(0, 8, o1_start)
    loop(1, 4, lambda i: q1(i).start())

    def p_move(i):
        t = (pi + i) % 16
        return send(r.ps.at[pi], r.ps.at[pi], r.p, t, pi, plane_dev(t))

    def on_own(body):
        pl.when(c == 0)(lambda: body(r.wk))
        pl.when(c == 1)(lambda: body(r.wv))

    def on_other(body):
        pl.when(c == 0)(lambda: body(r.wv))
        pl.when(c == 1)(lambda: body(r.wk))

    def w1(w, i):
        own = w.at[zh, zl, xhi, y, xlo]
        return send(own, own, r.w1, i, 4 - i, far(i))

    def w1_start(w):
        loop(1, 4, lambda i: w1(w, i).start())

    def w2(w, i):
        part = w.at[:, zl, xhi, y, xlo]
        return send(part, part, r.w2, i, 4 - i, near(i))

    lo_z, hi_z = pl.ds(0, 2), pl.ds(2, 2)

    def ax(w, i):
        part = w.at[lo_z, :, xhi, y, xlo]
        return send(part, part, r.ax, i, 4 - i, x_dev(i))

    def by(w, i):
        part = w.at[hi_z, :, xhi, y, xlo]
        return send(part, part, r.by, i, 4 - i, y_dev(i))

    def a_part(w, i, h):
        return w.at[h, :, :, (y + i) % 4]

    def b_part(w, i, h):
        x = x_of(i)
        return w.at[2 + h, :, x // 2, :, x % 2]

    def own_on(w, part, sems, dev, d, h):
        own = part(w, 0, h)
        return send(own, own, sems, d * 2 + h, d * 2 + h, dev(1 + 2 * d))

    def pass_on(w, part, sems, dev, d):
        got = part(w, 3 - 2 * d, 1 - d)
        return send(got, got, sems, 4 + d, 4 + d, dev(1 + 2 * d))

    rings = ((a_part, r.ay, y_dev), (b_part, r.bx, x_dev))

    def wx_a(w, i):
        part = w.at[lo_z, :, :, (y + i) % 4]
        return send(part, part, r.wx, i, i, (sib, f))

    def wx_b(w, i):
        x = x_of(i)
        part = w.at[hi_z, :, x // 2, :, x % 2]
        return send(part, part, r.wx, 4 + i, 4 + i, (sib, f))

    pl.when(c == 0)(lambda: w1_start(r.wk))
    loop(1, 16, lambda i: p_move(i).start())

    r.ku[0:64, :] = r.ku_in[...]
    r.ku[64:128, :] = jnp.zeros((64, 512), BF16)
    r.vu[0:64, :] = jnp.zeros((64, 512), BF16)
    r.vu[64:128, :] = r.vu_in[...]
    wide_q = r.lq_in[...].astype(F32)
    for j in range(2):
        for h in range(16):
            r.lq[j, h : h + 1, :] = wide_q[j : j + 1, h * 128 : (h + 1) * 128]

    hid_copy.wait()

    def norm(i):
        rows = pl.ds(pl.multiple_of(i * 32, 32), 32)
        x = r.hid[rows, :].astype(F32)
        scale = lax.rsqrt(jnp.mean(x * x, axis=1, keepdims=True) + EPSILON)
        r.hid[rows, :] = (x * scale * r.gain_in[...].astype(F32)).astype(BF16)

    loop(0, 8, norm)
    loop(1, 4, lambda i: arrived(r.qs.at[c, (zh + i) % 4, zl], r.q1, i))
    loop(1, 4, lambda i: q2(i).start())
    qx(0).start()

    def o2_slot(t, yy):
        return r.wg.at[:, t, :, pl.ds((c * 4 + yy) * 16, 16), :]

    def o2(i):
        t = (pi + i) % 16
        return send(r.ws, o2_slot(xhi, y), r.o2, t, y * 2 + xhi, plane_dev(t))

    @pl.when(mine)
    def _():
        def one(zz):
            @pl.when(jnp.logical_not(jnp.logical_and(z % 2 == c, zz == z)))
            def _():
                arrived(r.ws.at[zz % 2, zz // 2], r.o1, zz)

        loop(0, 16, one)
        loop(1, 16, lambda i: o2(i).start())
        r.wg[:, xhi, :, pl.ds((c * 4 + y) * 16, 16), :] = r.ws[...]

    def w1_done(w):
        loop(1, 4, lambda i: arrived(w.at[(zh + i) % 4, zl, xhi, y, xlo], r.w1, i))
        loop(1, 4, lambda i: w2(w, i).start())

    pl.when(c == 0)(lambda: w1_done(r.wk))
    pl.when(c == 1)(lambda: w1_start(r.wv))
    loop(8, 16, norm)

    def q2_done(i):
        arrived(r.qs.at[c, :, (zl + i) % 4], r.q2, i)
        qx(i).start()

    loop(1, 4, q2_done)

    def w2_done(w):
        loop(1, 4, lambda i: arrived(w.at[:, (zl + i) % 4, xhi, y, xlo], r.w2, i))

    def first_start(w):
        loop(1, 4, lambda i: ax(w, i).start())
        loop(1, 4, lambda i: by(w, i).start())

    def first_done(w):
        def a_done(i):
            x = x_of(i)
            arrived(w.at[lo_z, :, x // 2, y, x % 2], r.ax, i)

        loop(1, 4, a_done)
        loop(1, 4, lambda i: arrived(w.at[hi_z, :, xhi, (y + i) % 4, xlo], r.by, i))

    def second_start(w):
        for part, sems, dev in rings:
            own_on(w, part, sems, dev, 0, 1).start()
            own_on(w, part, sems, dev, 1, 0).start()
        for part, sems, dev in rings:
            own_on(w, part, sems, dev, 0, 0).start()
            own_on(w, part, sems, dev, 1, 1).start()
        wx_a(w, 0).start()
        wx_b(w, 0).start()

    def second_pass(w):
        for part, sems, dev in rings:
            arrived(part(w, 3, 1), sems, 1)
            pass_on(w, part, sems, dev, 0).start()
            arrived(part(w, 1, 0), sems, 2)
            pass_on(w, part, sems, dev, 1).start()

    def second_done(w):
        for (part, sems, dev), cross in zip(rings, (wx_a, wx_b)):
            arrived(part(w, 3, 0), sems, 0)
            cross(w, 3).start()
            arrived(part(w, 1, 1), sems, 3)
            cross(w, 1).start()
        for (part, sems, dev), cross in zip(rings, (wx_a, wx_b)):
            arrived(part(w, 2, 1), sems, 4)
            arrived(part(w, 2, 0), sems, 5)
            cross(w, 2).start()

    def cross_a_done(w):
        loop(0, 4, lambda i: arrived(w.at[lo_z, :, :, (y + i) % 4], r.wx, i))

    def cross_b_done(w):
        def one(i):
            x = x_of(i)
            arrived(w.at[hi_z, :, x // 2, :, x % 2], r.wx, 4 + i)

        loop(0, 4, one)

    def keys_core(body):
        pl.when(c == 0)(lambda: body(r.wk))

    def values_core(body):
        pl.when(c == 1)(lambda: body(r.wv))

    keys_core(w2_done)
    keys_core(first_start)
    values_core(w1_done)

    def p_done(i):
        t = (pi + i) % 16
        arrived(r.ps.at[t], r.p, t)

    loop(1, 16, p_done)
    loop(0, 4, lambda i: arrived(r.qs.at[1 - c, :, (zl + i) % 4], r.qx, i))
    q_all = r.qs[...].reshape(512, 640)
    q_rows = q_all[:, :512]
    p_rows = r.ps[...].reshape(256, 512)
    wide = dot(p_rows, q_rows, 1, 1).reshape(32, 8, 512)
    same = iota((32, 8, 512), 1) == iota((32, 8, 512), 2) % 8
    folded = jnp.sum(jnp.where(same, wide, 0.0), axis=1)
    fold = (iota((512, 64), 0) // 8 == iota((512, 64), 1)).astype(F32)
    scores = SCALE * dot(folded, fold, precision=lax.Precision.HIGHEST)
    marks = dot(q_all[:, 512:], fold.astype(BF16), 0, 0)
    target = marks[0:1] * 32.0 + marks[1:2]
    pid = iota((32, 64), 0)
    ptile = pid // 2
    ids = (((ptile // 2) * 2 + c) * 32 + z * 2 + ptile % 2) * 2 + pid % 2
    hit = (ids.astype(F32) == target).astype(F32)
    top = jnp.max(scores, axis=0, keepdims=True)
    local = top + jnp.log(jnp.sum(jnp.exp(scores - top), axis=0, keepdims=True))
    r.st[line] = jnp.zeros((4, 128), F32)
    r.st[line, 0:1, 0:64] = local
    r.st[line, 1:2, 0:64] = jnp.sum(scores * hit, axis=0, keepdims=True)

    def st_move(s):
        return send(r.st.at[line], r.st.at[line], r.sts, s, line, line_dev(s))

    def st_start(i):
        zz = (z + far_first(i)) % 16
        st_move(zz).start()
        st_move(16 + zz).start()

    loop(1, 16, st_start)
    st_move((1 - c) * 16 + z).start()

    half = r.wg.at[:, :, :, pl.ds(c * 64, 64), :]
    other = r.wg.at[:, :, :, pl.ds((1 - c) * 64, 64), :]

    def o2_done(s):
        @pl.when(jnp.logical_not(jnp.logical_and(mine, s == y * 2 + xhi)))
        def _():
            arrived(o2_slot(s % 2, s // 2), r.o2, s)

    loop(0, 8, o2_done)
    o3 = remote(half, half, r.o3.at[0], r.o3.at[1], sib, f)
    o3.start()
    keys_core(first_done)
    keys_core(second_start)
    values_core(w2_done)
    values_core(first_start)
    remote(other, other, r.o3.at[0], r.o3.at[1], sib, f).wait_recv()
    q_half = r.qs[c].reshape(256, 640)
    prod = jnp.zeros((256, 1024), F32)
    for a in range(4):
        prod += dot(
            q_half[:, a * 128 : (a + 1) * 128], r.wg[a // 2, a % 2].reshape(1024, 128), 1, 1
        )
    qw = jnp.zeros((256, 128), F32)
    chunk = iota((256, 128), 0) % 8
    for a in range(8):
        qw += jnp.where(chunk == a, prod[:, a * 128 : (a + 1) * 128], 0.0)
    r.qwg[z, c] = jnp.sum(qw.reshape(32, 8, 128), axis=1).astype(BF16)

    def qw_move(i):
        zz = (z + far_first(i)) % 16
        return send(r.qwg.at[z, c], r.qwg.at[z, c], r.qw, zz, z, z_dev(zz))

    def qw_cross(zz):
        return send(r.qwg.at[zz, c], r.qwg.at[zz, c], r.qwx, zz, zz, (sib, f))

    loop(1, 16, lambda i: qw_move(i).start())
    qw_cross(z).start()

    keys_core(second_pass)
    def st_done(i):
        s = (line + i) % 32
        arrived(r.st.at[s], r.sts, s)

    loop(1, 32, st_done)
    stats = r.st[...]
    peak = jnp.max(stats, axis=0)
    total = peak + jnp.log(jnp.sum(jnp.exp(stats - peak[None]), axis=0))
    picked = jnp.sum(stats, axis=0)
    lse = total[0:1, :64]
    weights = (jnp.exp(scores - lse) - hit).astype(BF16)

    def qw_done(i):
        zz = (z + far_first(16 - i)) % 16
        arrived(r.qwg.at[zz, c], r.qw, zz)
        qw_cross(zz).start()

    loop(1, 16, qw_done)
    loop(0, 16, lambda zz: arrived(r.qwg.at[zz, 1 - c], r.qwx, zz))
    rows16 = (iota((512, 32), 0) // 16 == iota((512, 32), 1)).astype(BF16)
    cols64 = (iota((64, 1024), 1) % 64 == iota((64, 1024), 0)).astype(BF16)
    tall = dot(dot(rows16, weights).astype(BF16), cols64)
    diag = iota((512, 1024), 0) % 16 == iota((512, 1024), 1) // 64
    tall = jnp.where(diag, tall, 0.0).astype(BF16)
    r.hps[...] = (
        (SCALE * dot(tall, r.qwg[...].reshape(1024, 128))).astype(BF16).reshape(16, 32, 128)
    )

    def hp_move(i):
        t = (pi + i) % 16
        return send(r.hps.at[t], r.hpr.at[pi], r.hp, t, pi, plane_dev(t))

    def pg_move(i):
        t = (pi + i) % 16
        return send(r.pgs.at[t], r.pgr.at[pi], r.pg, t, pi, plane_dev(t))

    loop(1, 16, lambda i: hp_move(i).start())
    r.hpr[pi] = r.hps[pi]
    values_core(first_done)
    values_core(second_start)
    rows8 = (iota((256, 32), 0) // 8 == iota((256, 32), 1)).astype(BF16)
    cols8 = (iota((64, 512), 1) // 8 == iota((64, 512), 0)).astype(BF16)
    spread = dot(dot(rows8, weights).astype(BF16), cols8)
    diag = iota((256, 512), 0) % 8 == iota((256, 512), 1) % 8
    spread = jnp.where(diag, spread, 0.0).astype(BF16)
    r.pgs[...] = (SCALE * dot(spread, q_rows)).astype(BF16).reshape(16, 16, 512)
    loop(1, 16, lambda i: pg_move(i).start())
    r.pgr[pi] = r.pgs[pi]

    r.qgs[...] = (SCALE * dot(spread, p_rows, 0, 0)).astype(BF16).reshape(2, 16, 16, 512)
    swap = remote(r.qgs.at[1 - c], r.qgx, r.qgc.at[0], r.qgc.at[1], sib, f)
    swap.start()
    loss = picked[1:2, :64]
    loss = lse - loss
    spot = iota((1, 64), 1)
    for j in range(2):
        r.loss_out[j] = jnp.sum(jnp.where(spot == 2 * line + j, loss, 0.0))

    def qg_move(i):
        zz = (z + far_first(i)) % 16
        return send(r.qgs.at[c, zz], r.qgr.at[z], r.qg, zz, z, z_dev(zz))

    keys_core(second_done)
    values_core(second_pass)
    swap.wait_recv()
    r.qgs[c] = (r.qgs[c].astype(F32) + r.qgx[...].astype(F32)).astype(BF16)
    loop(1, 16, lambda i: qg_move(i).start())
    r.qgr[z] = r.qgs[c, z]

    pl.when(c == 1)(lambda: cross_a_done(r.wk))
    pl.when(c == 1)(lambda: cross_b_done(r.wk))
    def project(w, raw, k):
        tokens = r.hid[:, pl.ds(pl.multiple_of(k * 1024, 1024), 1024)]
        part = dot(tokens, w[k].reshape(1024, w.shape[-1]))

        @pl.when(k == 0)
        def _():
            raw[...] = part

        @pl.when(k > 0)
        def _():
            raw[...] += part

    loop(0, 4, lambda k: project(r.wk, r.raw_k, k))
    r.low[...] = r.raw_k[:, 512:640].astype(BF16)
    adapted = dot(r.low[...], r.ku[...])
    own_group = iota((16, 512), 0) // 4 == iota((16, 512), 1) // 128

    def by_group(rows):
        return jnp.where(own_group, jnp.concatenate([rows] * 4, axis=1), 0.0).astype(BF16)

    queries = [by_group(r.lq[j]) for j in range(2)]
    for j in range(2):
        tok = slice(j * 256, (j + 1) * 256)
        for g in range(4):
            col = slice(g * 128, (g + 1) * 128)
            key = r.raw_k[tok, col] + 2.0 * adapted[tok, col]
            turned = pltpu.roll(key, 64, axis=1)
            r.keys[tok, col] = (key * r.cos_in[...] + turned * r.sin_in[...]).astype(BF16)
        sim = dot(queries[j], r.keys[tok, :], 1, 1) * ROOT
        sim = jnp.exp(sim - jnp.max(sim, axis=1, keepdims=True))
        r.att[j] = sim / jnp.sum(sim, axis=1, keepdims=True)

    values_core(second_done)
    def hp_done(i):
        t = (pi + i) % 16
        arrived(r.hpr.at[t], r.hp, t)

    loop(1, 16, hp_done)
    heads = jnp.sum(r.hpr[...].astype(F32), axis=0).astype(BF16)
    row, lane = iota((128, 128), 0), iota((128, 128), 1)
    tile = (iota((128, 16), 0) % 16 == iota((128, 16), 1)).astype(BF16)
    group = (row % 16 == lane % 16).astype(BF16)
    head, src = iota((16, 128), 0), iota((16, 128), 1)
    place, at_z = src // 16, src % 16
    collect = (
        ((place % 4) * 4 + (place // 4) * 2 + at_z % 2 == head)
    ).astype(BF16)
    for j in range(2):
        tok = slice(j * 256, (j + 1) * 256)
        spread_rows = dot(tile, heads[j * 16 : (j + 1) * 16])
        spread_rows = jnp.where(lane // 16 == row // 16, spread_rows, 0.0).astype(BF16)
        copied = dot(spread_rows, group)
        copied = jnp.where(lane // 16 == (row % 16) // 2, copied, 0.0).astype(BF16)
        r.gq[j] = by_group(dot(collect, copied))
        r.vg[tok, :] = dot(r.att[j].astype(BF16), r.gq[j], 0, 0).astype(BF16)
    up_v = (2.0 * dot(r.low[...], r.vg[...], 0, 0)).astype(BF16)
    for k in range(4):
        r.u0[1, k] = up_v[64:128, k * 128 : (k + 1) * 128]
    r.raw_v[...] = 2.0 * dot(r.low[...], r.vu[...])

    def project_values(k):
        tokens = r.hid[:, pl.ds(pl.multiple_of(k * 1024, 1024), 1024)]
        r.raw_v[...] += dot(tokens, r.wv[k].reshape(1024, 512))

    pl.when(c == 0)(lambda: cross_a_done(r.wv))
    loop(0, 2, project_values)
    pl.when(c == 0)(lambda: cross_b_done(r.wv))
    loop(2, 4, project_values)
    r.values[...] = r.raw_v[...].astype(BF16)
    for j in range(2):
        tok = slice(j * 256, (j + 1) * 256)
        prob = dot(r.gq[j], r.values[tok, :], 1, 1)
        attention = r.att[j]
        expected = jnp.sum(attention * prob, axis=1, keepdims=True)
        score_grad = attention * (prob - expected)
        turned_grad = dot(score_grad.astype(BF16), queries[j], 0, 0) * ROOT
        for g in range(4):
            col = slice(g * 128, (g + 1) * 128)
            part = turned_grad[:, col]
            turned = pltpu.roll(part, 64, axis=1)
            r.keys[tok, col] = (part * r.cos_in[...] - turned * r.sin_in[...]).astype(BF16)

    up_k = (2.0 * dot(r.low[...], r.keys[...], 0, 0)).astype(BF16)
    for k in range(4):
        r.u0[0, k] = up_k[0:64, k * 128 : (k + 1) * 128]
    u_swap = send(r.u0.at[1 - c], r.u1, r.one, 0, 0, (sib, f))
    u_swap.start()
    back = dot(r.keys[...], r.ku[...], 1, 1) + dot(r.vg[...], r.vu[...], 1, 1)
    r.back[...] = jnp.transpose(back.astype(BF16).astype(F32)).astype(BF16)

    def down(j, cc):
        cols = pl.ds(pl.multiple_of((j * 2 + cc) * 256, 256), 256)
        part = (2.0 * dot(r.back[...], r.hid[:, cols])).astype(BF16)
        r.dt[j, cc, 0] = part[:, :128]
        r.dt[j, cc, 1] = part[:, 128:]

    loop(0, 8, lambda j: down(j, 1 - c))
    d_swap = send(r.dt.at[:, 1 - c], r.d1, r.one, 1, 1, (sib, f))
    d_swap.start()
    u_swap.wait_recv()
    r.v1[...] = (
        (r.u0[c].astype(F32) + r.u1[...].astype(F32)).astype(BF16).reshape(16, 16, 128)
    )

    def u2_move(i):
        t = (pi + i) % 16
        return send(r.v1.at[t], r.u2.at[pi], r.su2, t, pi, plane_dev(t))

    def d2_move(i):
        t = (pi + i) % 16
        return send(r.r1.at[t], r.d2.at[pi], r.sd2, t, pi, plane_dev(t))

    loop(1, 16, lambda i: u2_move(i).start())
    r.u2[pi] = r.v1[pi]
    loop(0, 8, lambda j: down(j, c))
    d_swap.wait_recv()
    r.r1[...] = (
        (r.dt[:, c].astype(F32) + r.d1[...].astype(F32)).astype(BF16).reshape(16, 128, 128)
    )
    loop(1, 16, lambda i: d2_move(i).start())
    r.d2[pi] = r.r1[pi]

    def u2_done(i):
        t = (pi + i) % 16
        arrived(r.u2.at[t], r.su2, t)

    loop(1, 16, u2_done)
    r.v3[...] = jnp.sum(r.u2[...].astype(F32), axis=0)
    r.u3[z] = r.v3[...]

    def u3_move(i):
        zz = (z + far_first(i)) % 16
        return send(r.v3, r.u3.at[z], r.su3, zz, z, z_dev(zz))

    loop(1, 16, lambda i: u3_move(i).start())

    def d2_done(i):
        t = (pi + i) % 16
        arrived(r.d2.at[t], r.sd2, t)

    loop(1, 16, d2_done)
    r.r2[...] = jnp.transpose(jnp.sum(r.d2[...].astype(F32), axis=0)).reshape(16, 8, 128)

    def d3_move(k):
        return send(
            r.r2.at[k], r.d3.at[z], r.sd3, k, z, (b, (8 * xhi + k // 2) * 2 + k % 2)
        )

    def d3_self(k):
        return (8 * xhi + k // 2) * 2 + k % 2 == f

    def d3_start(k):
        @pl.when(jnp.logical_not(d3_self(k)))
        def _():
            d3_move(k).start()

        @pl.when(d3_self(k))
        def _():
            r.d3[z] = r.r2[k]

    loop(0, 16, d3_start)

    def put_rows(out, total):
        r.tmp[...] = total
        for j in range(2):
            for k in range(8):
                out[j : j + 1, k * 512 : (k + 1) * 512] = r.tmp[j * 8 + k : j * 8 + k + 1, :]

    def pg_done(i):
        t = (pi + i) % 16
        arrived(r.pgr.at[t], r.pg, t)

    def qg_done(i):
        t = (z + i) % 16
        arrived(r.qgr.at[t], r.qg, t)

    loop(1, 16, pg_done)
    put_rows(r.pg_out, jnp.sum(r.pgr[...].astype(F32), axis=0))
    loop(1, 16, qg_done)
    put_rows(r.qg_out, jnp.sum(r.qgr[...].astype(F32), axis=0))

    def u3_done(i):
        t = (z + i) % 16
        arrived(r.u3.at[t], r.su3, t)

    loop(1, 16, u3_done)
    r.u4[pi] = jnp.sum(r.u3[...], axis=0)

    def u4_move(i):
        t = (pi + i) % 16
        return send(r.u4.at[pi], r.u4.at[pi], r.su4, t, pi, plane_dev(t))

    loop(1, 16, lambda i: u4_move(i).start())

    def d3_done(zz):
        @pl.when(jnp.logical_not(jnp.logical_and(z // 8 == xhi, zz == z)))
        def _():
            arrived(r.d3.at[zz], r.sd3, zz)

    loop(0, 16, d3_done)
    down_total = jnp.sum(r.d3[...], axis=0)
    r.dk_out[...] = down_total[:, :64]
    r.dv_out[...] = down_total[:, 64:]

    def u4_done(i):
        t = (pi + i) % 16
        arrived(r.u4.at[t], r.su4, t)

    loop(1, 16, u4_done)
    u_back = send(r.u4, r.u5, r.one, 2, 2, (sib, f))
    u_back.start()

    def z_sent(i):
        q1(i).wait_send()
        q2(i).wait_send()

    loop(1, 4, z_sent)
    loop(0, 4, lambda i: qx(i).wait_send())

    def rows_sent(w):
        def one(i):
            w1(w, i).wait_send()
            w2(w, i).wait_send()
            ax(w, i).wait_send()
            by(w, i).wait_send()

        def two(i):
            wx_a(w, i).wait_send()
            wx_b(w, i).wait_send()

        loop(1, 4, one)
        loop(0, 4, two)
        for part, sems, dev in rings:
            for d in range(2):
                for h in range(2):
                    own_on(w, part, sems, dev, d, h).wait_send()
                pass_on(w, part, sems, dev, d).wait_send()

    on_own(rows_sent)

    def o1_sent(zp):
        @pl.when(jnp.logical_not(jnp.logical_and(mine, 2 * zp + c == z)))
        def _():
            o1(zp).wait_send()

    loop(0, 8, o1_sent)

    @pl.when(mine)
    def _():
        loop(1, 16, lambda i: o2(i).wait_send())

    o3.wait_send()
    swap.wait_send()
    u_swap.wait_send()
    d_swap.wait_send()

    def sixteen_sent(i):
        p_move(i).wait_send()
        qw_move(i).wait_send()
        pg_move(i).wait_send()
        hp_move(i).wait_send()
        qg_move(i).wait_send()
        u2_move(i).wait_send()
        d2_move(i).wait_send()
        u3_move(i).wait_send()
        u4_move(i).wait_send()

    loop(1, 16, sixteen_sent)

    def more_sent(k):
        qw_cross(k).wait_send()

        @pl.when(jnp.logical_not(d3_self(k)))
        def _():
            d3_move(k).wait_send()

    loop(0, 16, more_sent)
    loop(1, 32, lambda i: st_move((line + i) % 32).wait_send())

    u_back.wait_recv()

    def put(out, src):
        full = src[...].reshape(256, 128)
        for k in range(4):
            out[:, k * 128 : (k + 1) * 128] = full[k * 64 : (k + 1) * 64]

    @pl.when(c == 0)
    def _():
        put(r.uk_out, r.u4)
        put(r.uv_out, r.u5)

    @pl.when(c == 1)
    def _():
        put(r.uk_out, r.u5)
        put(r.uv_out, r.u4)

    u_back.wait_send()


def hand_over(*refs):
    half = len(refs) // 2
    for src, out in zip(refs[:half], refs[half:], strict=True):
        if len(src.shape) == 1:
            for j in range(src.shape[0]):
                out[j] = src[j]
        else:
            out[...] = src[...]


def rotary_tables(length):
    half = HEAD // 2
    frequency = ROTARY_BASE ** (-(np.arange(half) * 2.0 / HEAD))
    angles = np.arange(length)[:, None] * frequency[None, :]
    cosine, sine = np.cos(angles), np.sin(angles)
    return (
        np.concatenate([cosine, cosine], axis=1).astype(np.float32),
        np.concatenate([-sine, sine], axis=1).astype(np.float32),
    )


def shards(
    queries,
    passages,
    positives,
    hidden,
    norm_gain,
    last_query,
    frozen_key_weight,
    frozen_value_weight,
    key_down,
    key_adapter_up,
    value_down,
    value_adapter_up,
    out_weight,
):
    vm = pl.BlockSpec(memory_space=pltpu.VMEM)
    specs = [vm] * len(INPUTS)
    specs[INPUTS.index("pos_in")] = pl.BlockSpec(memory_space=pltpu.SMEM)
    specs[INPUTS.index("hid_in")] = pl.BlockSpec(memory_space=pl.ANY)
    shapes = ((2,), (2, 4096), (2, 4096), (8, 64), (8, 64), (64, 512), (64, 512))
    cosine, sine = rotary_tables(256)
    outs = (vm,) * len(shapes)
    outs = (pl.BlockSpec(memory_space=pltpu.SMEM), *outs[1:])
    results = pl.pallas_call(
        kernel,
        out_shape=tuple(jax.ShapeDtypeStruct(shape, F32) for shape in shapes),
        in_specs=specs,
        out_specs=outs,
        scratch_shapes=[pltpu.VMEM(shape, dtype) for shape, dtype in BUFFERS.values()]
        + [pltpu.SemaphoreType.DMA(shape) for shape in SEMAPHORES.values()],
        compiler_params=pltpu.CompilerParams(
            collective_id=0, has_side_effects=True, vmem_limit_bytes=VMEM_BYTES
        ),
    )(
        queries,
        passages,
        positives,
        hidden.reshape(512, 4096),
        norm_gain.reshape(1, 4096),
        last_query,
        frozen_key_weight,
        frozen_value_weight,
        key_down.T,
        key_adapter_up,
        value_down.T,
        value_adapter_up,
        out_weight,
        cosine,
        sine,
    )
    return pl.pallas_call(
        hand_over,
        out_shape=tuple(jax.ShapeDtypeStruct(shape, F32) for shape in shapes),
        in_specs=outs,
        out_specs=outs,
    )(*results)


def solution(mesh):
    rows = P(("batch", "fsdp"), None)
    placed = (
        rows,
        rows,
        P(("batch", "fsdp")),
        P(("batch", "fsdp"), None, None),
        P(),
        rows,
        P("fsdp", None),
        P("fsdp", None),
        P("fsdp", None),
        P(),
        P("fsdp", None),
        P(),
        P("batch", "fsdp"),
    )
    return jax.shard_map(
        shards,
        mesh=mesh,
        in_specs=placed,
        out_specs=(P(("batch", "fsdp")), rows, rows, rows, rows, P(), P()),
        check_vma=False,
    )
```

```python
import jax
import jax.numpy as jnp
import numpy as np
from jax import lax
from jax.experimental import pallas as pl
from jax.experimental.pallas import tpu as pltpu
from jax.sharding import PartitionSpec as P

F32 = jnp.float32
BF16 = jnp.bfloat16
MESH = pl.DeviceIdType.MESH
HEAD = 128
SCALE = 20.0
EPSILON = 1e-06
ROTARY_BASE = 1000000.0
VMEM_BYTES = 56 * 1024 * 1024
ROOT = HEAD ** (-0.5)


def position():
    b = lax.axis_index("batch")
    f = lax.axis_index("fsdp")
    y = b // 4
    xlo = (b // 2) % 2
    c = b % 2
    z = f // 2
    xhi = f % 2
    return (b, f, y, xlo, c, z, xhi)


def remote(src, dst, send_sem, recv_sem, b, f):
    return pltpu.make_async_remote_copy(
        src_ref=src,
        dst_ref=dst,
        send_sem=send_sem,
        recv_sem=recv_sem,
        device_id=(b, f),
        device_id_type=MESH,
    )


def loop(lo, hi, body):
    def step(i, carry):
        body(i)
        return carry

    lax.fori_loop(lo, hi, step, 0)


def iota(shape, dim):
    return lax.broadcasted_iota(jnp.int32, shape, dim)


def dot(a, b, ca=1, cb=0, precision=None):
    return lax.dot_general(
        a, b, (((ca,), (cb,)), ((), ())), preferred_element_type=F32, precision=precision
    )


def far_first(i):
    return 8 + (i // 2) * (2 * (i % 2) - 1)


INPUTS = (
    "q_in", "p_in", "pos_in", "hid_in", "gain_in", "lq_in", "fk_in", "fv_in",
    "kd_in", "ku_in", "vd_in", "vu_in", "wo_in", "cos_in", "sin_in",
)
OUTPUTS = ("loss_out", "qg_out", "pg_out", "dk_out", "dv_out", "uk_out", "uv_out")
BUFFERS = {
    "q_v": ((2, 4096), BF16),
    "p_v": ((2, 4096), BF16),
    "gain_v": ((4096,), BF16),
    "lq_v": ((2, 2048), BF16),
    "downs_v": ((2, 64, 128), BF16),
    "wo_v": ((128, 128), BF16),
    "cos_v": ((256, 128), F32),
    "sin_v": ((256, 128), F32),
    "tmp": ((16, 512), F32),
    "lq": ((2, 16, 128), F32),
    "hid": ((512, 4096), BF16),
    "qs": ((2, 4, 4, 16, 640), BF16),
    "ps": ((16, 16, 512), BF16),
    "ws": ((2, 8, 16, 128), BF16),
    "wg": ((2, 2, 8, 128, 128), BF16),
    "qwg": ((16, 2, 32, 128), BF16),
    "st": ((32, 4, 128), F32),
    "pgs": ((16, 16, 512), BF16),
    "pgr": ((16, 16, 512), BF16),
    "hps": ((16, 32, 128), BF16),
    "hpr": ((16, 32, 128), BF16),
    "qgs": ((2, 16, 16, 512), BF16),
    "qgx": ((16, 16, 512), BF16),
    "qgr": ((16, 16, 512), BF16),
    "wk": ((4, 4, 2, 4, 2, 16, 640), BF16),
    "wv": ((4, 4, 2, 4, 2, 16, 512), BF16),
    "dn": ((128, 128), BF16),
    "ku": ((128, 512), BF16),
    "vu": ((128, 512), BF16),
    "raw_k": ((512, 640), F32),
    "raw_v": ((512, 512), F32),
    "low": ((512, 128), BF16),
    "keys": ((512, 512), BF16),
    "values": ((512, 512), BF16),
    "vg": ((512, 512), BF16),
    "gq": ((2, 16, 512), BF16),
    "back": ((128, 512), BF16),
    "att": ((2, 16, 256), F32),
    "dt": ((8, 2, 2, 128, 128), BF16),
    "d1": ((8, 2, 128, 128), BF16),
    "r1": ((16, 128, 128), BF16),
    "d2": ((16, 128, 128), BF16),
    "r2": ((16, 8, 128), F32),
    "d3": ((16, 8, 128), F32),
    "u0": ((2, 4, 64, 128), BF16),
    "u1": ((4, 64, 128), BF16),
    "v1": ((16, 16, 128), BF16),
    "u2": ((16, 16, 128), BF16),
    "v3": ((16, 128), F32),
    "u3": ((16, 16, 128), F32),
    "u4": ((16, 16, 128), F32),
    "u5": ((16, 16, 128), F32),
}
SEMAPHORES = {
    "loc": (13,),
    "q1": (2, 4), "q2": (2, 4), "qx": (2, 4),
    "w1": (2, 4), "w2": (2, 4), "wx": (2, 16),
    "ax": (2, 8), "ay": (2, 12), "bx": (2, 12), "by": (2, 8),
    "p": (2, 16), "o1": (2, 16), "o2": (2, 16), "o3": (2,),
    "qw": (2, 16), "qwx": (2, 16), "sts": (2, 32),
    "pg": (2, 16), "hp": (2, 16), "qg": (2, 16), "qgc": (2,),
    "one": (2, 3), "sd2": (2, 16), "sd3": (2, 16),
    "su2": (2, 16), "su3": (2, 16), "su4": (2, 16),
}


class Refs:
    pass


def kernel(*refs):
    r = Refs()
    for name, ref in zip((*INPUTS, *OUTPUTS, *BUFFERS, *SEMAPHORES), refs, strict=True):
        setattr(r, name, ref)
    b, f, y, xlo, c, z, xhi = position()
    zh, zl = z // 4, z % 4
    pi = (b // 2) * 2 + xhi
    sib = b + 1 - 2 * c
    line = c * 16 + z
    OUT, IN = 0, 1

    def plane_dev(t):
        return ((t // 2) * 2 + c, z * 2 + t % 2)

    def line_dev(s):
        return ((b // 2) * 2 + s // 16, (s % 16) * 2 + xhi)

    def z_dev(zz):
        return (b, zz * 2 + xhi)

    def x_of(i):
        return (xhi * 2 + xlo + i) % 4

    def x_dev(i):
        x = x_of(i)
        return (y * 4 + (x % 2) * 2 + c, z * 2 + x // 2)

    def y_dev(i):
        return (((y + i) % 4) * 4 + xlo * 2 + c, f)

    def send(src, dst, sems, out, into, dev):
        return remote(src, dst, sems.at[OUT, out], sems.at[IN, into], dev[0], dev[1])

    def arrived(dst, sems, into):
        remote(dst, dst, sems.at[OUT, into], sems.at[IN, into], sib, f).wait_recv()

    piece = pl.ds(pl.multiple_of((y * 2 + xlo) * 16, 16), 16)
    fetch = [
        pltpu.make_async_copy(src, dst, r.loc.at[n])
        for n, (src, dst) in enumerate(
            (
                (r.fk_in.at[piece, :], r.wk.at[zh, 0, xhi, y, xlo, :, 0:512]),
                (r.fv_in.at[piece, :], r.wv.at[zh, 0, xhi, y, xlo]),
                (r.q_in, r.q_v),
                (r.p_in, r.p_v),
                (r.kd_in, r.downs_v.at[0]),
                (r.vd_in, r.downs_v.at[1]),
                (r.wo_in, r.wo_v),
                (r.hid_in, r.hid),
                (r.gain_in, r.gain_v),
                (r.lq_in, r.lq_v),
                (r.cos_in, r.cos_v),
                (r.sin_in, r.sin_v),
            )
        )
    ]

    @pl.when(c == 0)
    def _():
        fetch[0].start()

    @pl.when(c == 1)
    def _():
        fetch[1].start()

    for copy in fetch[2:]:
        copy.start()
    barrier = pltpu.get_barrier_semaphore()

    def greet(dev):
        pl.semaphore_signal(barrier, inc=1, device_id=dev, device_id_type=MESH)

    def greet_line(i):
        zz = (z + far_first(i)) % 16
        greet(line_dev(zz))
        greet(line_dev(16 + zz))

    loop(1, 16, greet_line)
    loop(1, 16, lambda i: greet(plane_dev((pi + i) % 16)))
    greet((sib, f))

    def slab(ref):
        rows = ref[...].astype(F32)
        for j in range(2):
            for k in range(8):
                r.tmp[j * 8 + k : j * 8 + k + 1, :] = rows[j : j + 1, k * 512 : (k + 1) * 512]
        return r.tmp[...].astype(BF16)

    fetch[2].wait()
    r.qs[c, zh, zl, :, 0:512] = slab(r.q_v)
    fetch[3].wait()
    r.ps[pi] = slab(r.p_v)
    fetch[4].wait()
    fetch[5].wait()
    fetch[6].wait()
    row, lane = iota((16, 128), 0), iota((16, 128), 1)
    mark = jnp.zeros((16, 128), F32)
    for j in range(2):
        spot = r.pos_in[j]
        high, low = (spot // 32).astype(F32), (spot % 32).astype(F32)
        mark = jnp.where((row == j * 8) & (lane == 0), high, mark)
        mark = jnp.where((row == j * 8) & (lane == 1), low, mark)
    r.qs[c, zh, zl, :, 512:640] = mark.astype(BF16)
    @pl.when(c == 0)
    def _():
        fetch[0].wait()
        downs = r.downs_v[...].reshape(128, 128).astype(F32)
        r.dn[...] = jnp.transpose(downs).astype(BF16)
        r.wk[zh, 0, xhi, y, xlo, :, 512:640] = r.dn[piece, :]

    @pl.when(c == 1)
    def _():
        fetch[1].wait()

    pl.semaphore_wait(barrier, 46)

    def far(i):
        return z_dev((z + 4 * i) % 16)

    def near(i):
        return z_dev((z + i - 4 * (i // 3)) % 16)

    def q1(i):
        own = r.qs.at[c, zh, zl]
        return send(own, own, r.q1, i, 4 - i, far(i))

    def q2(i):
        part = r.qs.at[c, :, zl]
        return send(part, part, r.q2, i, 4 - i, near(i))

    def qx(i):
        part = r.qs.at[c, :, (zl + i) % 4]
        return send(part, part, r.qx, i, i, (sib, f))

    mine = c == xlo

    def o1(zp):
        return send(
            r.wo_v.at[pl.ds(zp * 16, 16), :],
            r.ws.at[z % 2, z // 2],
            r.o1,
            zp,
            z,
            ((b // 2) * 2 + xlo, (2 * zp + c) * 2 + xhi),
        )

    def o1_start(zp):
        here = jnp.logical_and(mine, 2 * zp + c == z)

        @pl.when(jnp.logical_not(here))
        def _():
            o1(zp).start()

        @pl.when(here)
        def _():
            r.ws[z % 2, z // 2] = r.wo_v[pl.ds(zp * 16, 16), :]

    loop(0, 8, o1_start)
    loop(1, 4, lambda i: q1(i).start())

    def p_move(i):
        t = (pi + i) % 16
        return send(r.ps.at[pi], r.ps.at[pi], r.p, t, pi, plane_dev(t))

    def on_own(body):
        pl.when(c == 0)(lambda: body(r.wk))
        pl.when(c == 1)(lambda: body(r.wv))

    def on_other(body):
        pl.when(c == 0)(lambda: body(r.wv))
        pl.when(c == 1)(lambda: body(r.wk))

    def w1(w, i):
        own = w.at[zh, 0, xhi, y, xlo]
        return send(own, own, r.w1, i, 4 - i, far(i))

    def w1_start(w):
        loop(1, 4, lambda i: w1(w, i).start())

    def w2(w, i):
        part = w.at[:, 0, xhi, y, xlo]
        return send(part, w.at[:, 4 - i, xhi, y, xlo], r.w2, i, 4 - i, near(i))

    lo_z, hi_z = pl.ds(0, 2), pl.ds(2, 2)

    near_z = (pl.ds(0, 1), pl.ds(1, 3))

    def ax(w, g, i):
        part = w.at[lo_z, near_z[g], xhi, y, xlo]
        return send(part, part, r.ax, 4 * g + i, 4 * g + 4 - i, x_dev(i))

    def by(w, g, i):
        part = w.at[hi_z, near_z[g], xhi, y, xlo]
        return send(part, part, r.by, 4 * g + i, 4 * g + 4 - i, y_dev(i))

    def a_part(w, g, i, h):
        return w.at[h, near_z[g], :, (y + i) % 4]

    def b_part(w, g, i, h):
        x = x_of(i)
        return w.at[2 + h, near_z[g], x // 2, :, x % 2]

    def own_on(w, g, part, sems, dev, d, h):
        own = part(w, g, 0, h)
        n = 6 * g + d * 2 + h
        return send(own, own, sems, n, n, dev(1 + 2 * d))

    def pass_on(w, g, part, sems, dev, d):
        got = part(w, g, 3 - 2 * d, 1 - d)
        n = 6 * g + 4 + d
        return send(got, got, sems, n, n, dev(1 + 2 * d))

    rings = ((a_part, r.ay, y_dev), (b_part, r.bx, x_dev))

    def wx_a(w, g, i):
        part = w.at[lo_z, near_z[g], :, (y + i) % 4]
        return send(part, part, r.wx, 8 * g + i, 8 * g + i, (sib, f))

    def wx_b(w, g, i):
        x = x_of(i)
        part = w.at[hi_z, near_z[g], x // 2, :, x % 2]
        return send(part, part, r.wx, 8 * g + 4 + i, 8 * g + 4 + i, (sib, f))

    def first_start(w, g):
        loop(1, 4, lambda i: ax(w, g, i).start())
        loop(1, 4, lambda i: by(w, g, i).start())

    def first_done(w, g):
        def a_done(i):
            x = x_of(i)
            arrived(w.at[lo_z, near_z[g], x // 2, y, x % 2], r.ax, 4 * g + i)

        def b_done(i):
            part = w.at[hi_z, near_z[g], xhi, (y + i) % 4, xlo]
            arrived(part, r.by, 4 * g + i)

        loop(1, 4, a_done)
        loop(1, 4, b_done)

    def second_start(w, g):
        for part, sems, dev in rings:
            own_on(w, g, part, sems, dev, 0, 1).start()
            own_on(w, g, part, sems, dev, 1, 0).start()
        for part, sems, dev in rings:
            own_on(w, g, part, sems, dev, 0, 0).start()
            own_on(w, g, part, sems, dev, 1, 1).start()
        wx_a(w, g, 0).start()
        wx_b(w, g, 0).start()

    def second_pass(w, g):
        for part, sems, dev in rings:
            arrived(part(w, g, 3, 1), sems, 6 * g + 1)
            pass_on(w, g, part, sems, dev, 0).start()
            arrived(part(w, g, 1, 0), sems, 6 * g + 2)
            pass_on(w, g, part, sems, dev, 1).start()

    def second_done(w, g):
        for (part, sems, dev), cross in zip(rings, (wx_a, wx_b)):
            arrived(part(w, g, 3, 0), sems, 6 * g)
            cross(w, g, 3).start()
            arrived(part(w, g, 1, 1), sems, 6 * g + 3)
            cross(w, g, 1).start()
        for (part, sems, dev), cross in zip(rings, (wx_a, wx_b)):
            arrived(part(w, g, 2, 1), sems, 6 * g + 4)
            arrived(part(w, g, 2, 0), sems, 6 * g + 5)
            cross(w, g, 2).start()

    def cross_a_done(w):
        for g in range(2):
            loop(
                0,
                4,
                lambda i: arrived(
                    w.at[lo_z, near_z[g], :, (y + i) % 4], r.wx, 8 * g + i
                ),
            )

    def cross_b_done(w):
        for g in range(2):

            def one(i):
                x = x_of(i)
                part = w.at[hi_z, near_z[g], x // 2, :, x % 2]
                arrived(part, r.wx, 8 * g + 4 + i)

            loop(0, 4, one)

    def keys_core(body, g):
        pl.when(c == 0)(lambda: body(r.wk, g))

    def values_core(body, g):
        pl.when(c == 1)(lambda: body(r.wv, g))

    def each_core(body, g):
        keys_core(body, g)
        values_core(body, g)

    on_own(w1_start)
    loop(1, 16, lambda i: p_move(i).start())

    r.ku[0:64, :] = r.ku_in[...]
    r.ku[64:128, :] = jnp.zeros((64, 512), BF16)
    r.vu[0:64, :] = jnp.zeros((64, 512), BF16)
    r.vu[64:128, :] = r.vu_in[...]
    fetch[9].wait()
    wide_q = r.lq_v[...].astype(F32)
    for j in range(2):
        for h in range(16):
            r.lq[j, h : h + 1, :] = wide_q[j : j + 1, h * 128 : (h + 1) * 128]

    fetch[7].wait()
    fetch[8].wait()

    def norm(i):
        rows = pl.ds(pl.multiple_of(i * 32, 32), 32)
        x = r.hid[rows, :].astype(F32)
        scale = lax.rsqrt(jnp.mean(x * x, axis=1, keepdims=True) + EPSILON)
        r.hid[rows, :] = (x * scale * r.gain_v[...].astype(F32).reshape(1, 4096)).astype(BF16)

    loop(0, 8, norm)
    loop(1, 4, lambda i: arrived(r.qs.at[c, (zh + i) % 4, zl], r.q1, i))
    loop(1, 4, lambda i: q2(i).start())
    qx(0).start()

    def o2_slot(t, yy):
        return r.wg.at[:, t, :, pl.ds((c * 4 + yy) * 16, 16), :]

    def o2(i):
        t = (pi + i) % 16
        return send(r.ws, o2_slot(xhi, y), r.o2, t, y * 2 + xhi, plane_dev(t))

    @pl.when(mine)
    def _():
        def one(zz):
            @pl.when(jnp.logical_not(jnp.logical_and(z % 2 == c, zz == z)))
            def _():
                arrived(r.ws.at[zz % 2, zz // 2], r.o1, zz)

        loop(0, 16, one)
        loop(1, 16, lambda i: o2(i).start())
        r.wg[:, xhi, :, pl.ds((c * 4 + y) * 16, 16), :] = r.ws[...]

    def w1_done(w):
        loop(1, 4, lambda i: arrived(w.at[(zh + i) % 4, 0, xhi, y, xlo], r.w1, i))
        loop(1, 4, lambda i: w2(w, i).start())

    on_own(w1_done)
    each_core(first_start, 0)
    loop(8, 16, norm)

    def q2_done(i):
        arrived(r.qs.at[c, :, (zl + i) % 4], r.q2, i)
        qx(i).start()

    loop(1, 4, q2_done)

    def w2_done(w):
        loop(1, 4, lambda i: arrived(w.at[:, i, xhi, y, xlo], r.w2, i))

    each_core(first_done, 0)
    each_core(second_start, 0)
    on_own(w2_done)
    keys_core(first_start, 1)

    def p_done(i):
        t = (pi + i) % 16
        arrived(r.ps.at[t], r.p, t)

    loop(1, 16, p_done)
    loop(0, 4, lambda i: arrived(r.qs.at[1 - c, :, (zl + i) % 4], r.qx, i))
    q_all = r.qs[...].reshape(512, 640)
    q_rows = q_all[:, :512]
    p_rows = r.ps[...].reshape(256, 512)
    wide = dot(p_rows, q_rows, 1, 1).reshape(32, 8, 512)
    same = iota((32, 8, 512), 1) == iota((32, 8, 512), 2) % 8
    folded = jnp.sum(jnp.where(same, wide, 0.0), axis=1)
    fold = (iota((512, 64), 0) // 8 == iota((512, 64), 1)).astype(F32)
    scores = SCALE * dot(folded, fold, precision=lax.Precision.HIGHEST)
    marks = dot(q_all[:, 512:], fold.astype(BF16), 0, 0)
    target = marks[0:1] * 32.0 + marks[1:2]
    pid = iota((32, 64), 0)
    ptile = pid // 2
    ids = (((ptile // 2) * 2 + c) * 32 + z * 2 + ptile % 2) * 2 + pid % 2
    hit = (ids.astype(F32) == target).astype(F32)
    top = jnp.max(scores, axis=0, keepdims=True)
    local = top + jnp.log(jnp.sum(jnp.exp(scores - top), axis=0, keepdims=True))
    r.st[line] = jnp.zeros((4, 128), F32)
    r.st[line, 0:1, 0:64] = local
    r.st[line, 1:2, 0:64] = jnp.sum(scores * hit, axis=0, keepdims=True)

    def st_move(s):
        return send(r.st.at[line], r.st.at[line], r.sts, s, line, line_dev(s))

    def st_start(i):
        zz = (z + far_first(i)) % 16
        st_move(zz).start()
        st_move(16 + zz).start()

    loop(1, 16, st_start)
    st_move((1 - c) * 16 + z).start()

    half = r.wg.at[:, :, :, pl.ds(c * 64, 64), :]
    other = r.wg.at[:, :, :, pl.ds((1 - c) * 64, 64), :]

    def o2_done(s):
        @pl.when(jnp.logical_not(jnp.logical_and(mine, s == y * 2 + xhi)))
        def _():
            arrived(o2_slot(s % 2, s // 2), r.o2, s)

    loop(0, 8, o2_done)
    o3 = remote(half, half, r.o3.at[0], r.o3.at[1], sib, f)
    o3.start()
    each_core(second_pass, 0)
    keys_core(first_done, 1)
    keys_core(second_start, 1)
    values_core(first_start, 1)
    remote(other, other, r.o3.at[0], r.o3.at[1], sib, f).wait_recv()
    q_half = r.qs[c].reshape(256, 640)
    prod = jnp.zeros((256, 1024), F32)
    for a in range(4):
        prod += dot(
            q_half[:, a * 128 : (a + 1) * 128], r.wg[a // 2, a % 2].reshape(1024, 128), 1, 1
        )
    qw = jnp.zeros((256, 128), F32)
    chunk = iota((256, 128), 0) % 8
    for a in range(8):
        qw += jnp.where(chunk == a, prod[:, a * 128 : (a + 1) * 128], 0.0)
    r.qwg[z, c] = jnp.sum(qw.reshape(32, 8, 128), axis=1).astype(BF16)

    def qw_move(i):
        zz = (z + far_first(i)) % 16
        return send(r.qwg.at[z, c], r.qwg.at[z, c], r.qw, zz, z, z_dev(zz))

    def qw_cross(zz):
        return send(r.qwg.at[zz, c], r.qwg.at[zz, c], r.qwx, zz, zz, (sib, f))

    loop(1, 16, lambda i: qw_move(i).start())
    qw_cross(z).start()

    each_core(second_done, 0)
    keys_core(second_pass, 1)
    def st_done(i):
        s = (line + i) % 32
        arrived(r.st.at[s], r.sts, s)

    loop(1, 32, st_done)
    stats = r.st[...]
    peak = jnp.max(stats, axis=0)
    total = peak + jnp.log(jnp.sum(jnp.exp(stats - peak[None]), axis=0))
    picked = jnp.sum(stats, axis=0)
    lse = total[0:1, :64]
    weights = (jnp.exp(scores - lse) - hit).astype(BF16)

    def qw_done(i):
        zz = (z + far_first(16 - i)) % 16
        arrived(r.qwg.at[zz, c], r.qw, zz)
        qw_cross(zz).start()

    loop(1, 16, qw_done)
    loop(0, 16, lambda zz: arrived(r.qwg.at[zz, 1 - c], r.qwx, zz))
    rows16 = (iota((512, 32), 0) // 16 == iota((512, 32), 1)).astype(BF16)
    cols64 = (iota((64, 1024), 1) % 64 == iota((64, 1024), 0)).astype(BF16)
    tall = dot(dot(rows16, weights).astype(BF16), cols64)
    diag = iota((512, 1024), 0) % 16 == iota((512, 1024), 1) // 64
    tall = jnp.where(diag, tall, 0.0).astype(BF16)
    r.hps[...] = (
        (SCALE * dot(tall, r.qwg[...].reshape(1024, 128))).astype(BF16).reshape(16, 32, 128)
    )

    def hp_move(i):
        t = (pi + i) % 16
        return send(r.hps.at[t], r.hpr.at[pi], r.hp, t, pi, plane_dev(t))

    def pg_move(i):
        t = (pi + i) % 16
        return send(r.pgs.at[t], r.pgr.at[pi], r.pg, t, pi, plane_dev(t))

    loop(1, 16, lambda i: hp_move(i).start())
    r.hpr[pi] = r.hps[pi]
    values_core(first_done, 1)
    values_core(second_start, 1)
    rows8 = (iota((256, 32), 0) // 8 == iota((256, 32), 1)).astype(BF16)
    cols8 = (iota((64, 512), 1) // 8 == iota((64, 512), 0)).astype(BF16)
    spread = dot(dot(rows8, weights).astype(BF16), cols8)
    diag = iota((256, 512), 0) % 8 == iota((256, 512), 1) % 8
    spread = jnp.where(diag, spread, 0.0).astype(BF16)
    r.pgs[...] = (SCALE * dot(spread, q_rows)).astype(BF16).reshape(16, 16, 512)
    r.pgr[pi] = r.pgs[pi]

    r.qgs[...] = (SCALE * dot(spread, p_rows, 0, 0)).astype(BF16).reshape(2, 16, 16, 512)
    swap = remote(r.qgs.at[1 - c], r.qgx, r.qgc.at[0], r.qgc.at[1], sib, f)
    swap.start()
    loss = picked[1:2, :64]
    loss = lse - loss
    spot = iota((1, 64), 1)
    for j in range(2):
        r.loss_out[j] = jnp.sum(jnp.where(spot == 2 * line + j, loss, 0.0))

    def qg_move(i):
        zz = (z + far_first(i)) % 16
        return send(r.qgs.at[c, zz], r.qgr.at[z], r.qg, zz, z, z_dev(zz))

    keys_core(second_done, 1)
    values_core(second_pass, 1)
    swap.wait_recv()
    r.qgs[c] = (r.qgs[c].astype(F32) + r.qgx[...].astype(F32)).astype(BF16)
    loop(1, 16, lambda i: qg_move(i).start())
    r.qgr[z] = r.qgs[c, z]

    pl.when(c == 1)(lambda: cross_a_done(r.wk))
    pl.when(c == 1)(lambda: cross_b_done(r.wk))
    def tokens_of(k):
        cols = [pl.multiple_of((k * 4 + (zl + j) % 4) * 256, 256) for j in range(4)]
        return jnp.concatenate([r.hid[:, pl.ds(col, 256)] for col in cols], axis=1)

    def project(w, raw, k):
        tokens = tokens_of(k)
        part = dot(tokens, w[k].reshape(1024, w.shape[-1]))

        @pl.when(k == 0)
        def _():
            raw[...] = part

        @pl.when(k > 0)
        def _():
            raw[...] += part

    loop(0, 4, lambda k: project(r.wk, r.raw_k, k))
    r.low[...] = r.raw_k[:, 512:640].astype(BF16)
    adapted = dot(r.low[...], r.ku[...])
    fetch[10].wait()
    fetch[11].wait()
    own_group = iota((16, 512), 0) // 4 == iota((16, 512), 1) // 128

    def by_group(rows):
        return jnp.where(own_group, jnp.concatenate([rows] * 4, axis=1), 0.0).astype(BF16)

    queries = [by_group(r.lq[j]) for j in range(2)]
    for j in range(2):
        tok = slice(j * 256, (j + 1) * 256)
        for g in range(4):
            col = slice(g * 128, (g + 1) * 128)
            key = r.raw_k[tok, col] + 2.0 * adapted[tok, col]
            turned = pltpu.roll(key, 64, axis=1)
            r.keys[tok, col] = (key * r.cos_v[...] + turned * r.sin_v[...]).astype(BF16)
        sim = dot(queries[j], r.keys[tok, :], 1, 1) * ROOT
        sim = jnp.exp(sim - jnp.max(sim, axis=1, keepdims=True))
        r.att[j] = sim / jnp.sum(sim, axis=1, keepdims=True)

    values_core(second_done, 1)
    loop(1, 16, lambda i: pg_move(i).start())
    def hp_done(i):
        t = (pi + i) % 16
        arrived(r.hpr.at[t], r.hp, t)

    loop(1, 16, hp_done)
    heads = jnp.sum(r.hpr[...].astype(F32), axis=0).astype(BF16)
    row, lane = iota((128, 128), 0), iota((128, 128), 1)
    tile = (iota((128, 16), 0) % 16 == iota((128, 16), 1)).astype(BF16)
    group = (row % 16 == lane % 16).astype(BF16)
    head, src = iota((16, 128), 0), iota((16, 128), 1)
    place, at_z = src // 16, src % 16
    collect = (
        ((place % 4) * 4 + (place // 4) * 2 + at_z % 2 == head)
    ).astype(BF16)
    for j in range(2):
        tok = slice(j * 256, (j + 1) * 256)
        spread_rows = dot(tile, heads[j * 16 : (j + 1) * 16])
        spread_rows = jnp.where(lane // 16 == row // 16, spread_rows, 0.0).astype(BF16)
        copied = dot(spread_rows, group)
        copied = jnp.where(lane // 16 == (row % 16) // 2, copied, 0.0).astype(BF16)
        r.gq[j] = by_group(dot(collect, copied))
        r.vg[tok, :] = dot(r.att[j].astype(BF16), r.gq[j], 0, 0).astype(BF16)
    up_v = (2.0 * dot(r.low[...], r.vg[...], 0, 0)).astype(BF16)
    for k in range(4):
        r.u0[1, k] = up_v[64:128, k * 128 : (k + 1) * 128]
    r.raw_v[...] = 2.0 * dot(r.low[...], r.vu[...])

    def project_values(k):
        tokens = tokens_of(k)
        r.raw_v[...] += dot(tokens, r.wv[k].reshape(1024, 512))

    pl.when(c == 0)(lambda: cross_a_done(r.wv))
    loop(0, 2, project_values)
    pl.when(c == 0)(lambda: cross_b_done(r.wv))
    loop(2, 4, project_values)
    r.values[...] = r.raw_v[...].astype(BF16)
    for j in range(2):
        tok = slice(j * 256, (j + 1) * 256)
        prob = dot(r.gq[j], r.values[tok, :], 1, 1)
        attention = r.att[j]
        expected = jnp.sum(attention * prob, axis=1, keepdims=True)
        score_grad = attention * (prob - expected)
        turned_grad = dot(score_grad.astype(BF16), queries[j], 0, 0) * ROOT
        for g in range(4):
            col = slice(g * 128, (g + 1) * 128)
            part = turned_grad[:, col]
            turned = pltpu.roll(part, 64, axis=1)
            r.keys[tok, col] = (part * r.cos_v[...] - turned * r.sin_v[...]).astype(BF16)

    up_k = (2.0 * dot(r.low[...], r.keys[...], 0, 0)).astype(BF16)
    for k in range(4):
        r.u0[0, k] = up_k[0:64, k * 128 : (k + 1) * 128]
    u_swap = send(r.u0.at[1 - c], r.u1, r.one, 0, 0, (sib, f))
    u_swap.start()
    back = dot(r.keys[...], r.ku[...], 1, 1) + dot(r.vg[...], r.vu[...], 1, 1)
    r.back[...] = jnp.transpose(back.astype(BF16).astype(F32)).astype(BF16)

    def down(j, cc):
        cols = pl.ds(pl.multiple_of((j * 2 + cc) * 256, 256), 256)
        part = (2.0 * dot(r.back[...], r.hid[:, cols])).astype(BF16)
        r.dt[j, cc, 0] = part[:, :128]
        r.dt[j, cc, 1] = part[:, 128:]

    loop(0, 8, lambda j: down(j, 1 - c))
    d_swap = send(r.dt.at[:, 1 - c], r.d1, r.one, 1, 1, (sib, f))
    d_swap.start()
    u_swap.wait_recv()
    r.v1[...] = (
        (r.u0[c].astype(F32) + r.u1[...].astype(F32)).astype(BF16).reshape(16, 16, 128)
    )

    def u2_move(i):
        t = (pi + i) % 16
        return send(r.v1.at[t], r.u2.at[pi], r.su2, t, pi, plane_dev(t))

    def d2_move(i):
        t = (pi + i) % 16
        return send(r.r1.at[t], r.d2.at[pi], r.sd2, t, pi, plane_dev(t))

    loop(1, 16, lambda i: u2_move(i).start())
    r.u2[pi] = r.v1[pi]
    loop(0, 8, lambda j: down(j, c))
    d_swap.wait_recv()
    r.r1[...] = (
        (r.dt[:, c].astype(F32) + r.d1[...].astype(F32)).astype(BF16).reshape(16, 128, 128)
    )
    loop(1, 16, lambda i: d2_move(i).start())
    r.d2[pi] = r.r1[pi]

    def u2_done(i):
        t = (pi + i) % 16
        arrived(r.u2.at[t], r.su2, t)

    loop(1, 16, u2_done)
    r.v3[...] = jnp.sum(r.u2[...].astype(F32), axis=0)
    r.u3[z] = r.v3[...]

    def u3_move(i):
        zz = (z + far_first(i)) % 16
        return send(r.v3, r.u3.at[z], r.su3, zz, z, z_dev(zz))

    loop(1, 16, lambda i: u3_move(i).start())

    def d2_done(i):
        t = (pi + i) % 16
        arrived(r.d2.at[t], r.sd2, t)

    loop(1, 16, d2_done)
    r.r2[...] = jnp.transpose(jnp.sum(r.d2[...].astype(F32), axis=0)).reshape(16, 8, 128)

    def d3_move(k):
        return send(
            r.r2.at[k], r.d3.at[z], r.sd3, k, z, (b, (8 * xhi + k // 2) * 2 + k % 2)
        )

    def d3_self(k):
        return (8 * xhi + k // 2) * 2 + k % 2 == f

    def d3_start(k):
        @pl.when(jnp.logical_not(d3_self(k)))
        def _():
            d3_move(k).start()

        @pl.when(d3_self(k))
        def _():
            r.d3[z] = r.r2[k]

    loop(0, 16, d3_start)

    def put_rows(out, total):
        r.tmp[...] = total
        for j in range(2):
            for k in range(8):
                out[j : j + 1, k * 512 : (k + 1) * 512] = r.tmp[j * 8 + k : j * 8 + k + 1, :]

    def pg_done(i):
        t = (pi + i) % 16
        arrived(r.pgr.at[t], r.pg, t)

    def qg_done(i):
        t = (z + i) % 16
        arrived(r.qgr.at[t], r.qg, t)

    loop(1, 16, pg_done)
    put_rows(r.pg_out, jnp.sum(r.pgr[...].astype(F32), axis=0))
    loop(1, 16, qg_done)
    put_rows(r.qg_out, jnp.sum(r.qgr[...].astype(F32), axis=0))

    def u3_done(i):
        t = (z + i) % 16
        arrived(r.u3.at[t], r.su3, t)

    loop(1, 16, u3_done)
    r.u4[pi] = jnp.sum(r.u3[...], axis=0)

    def u4_move(i):
        t = (pi + i) % 16
        return send(r.u4.at[pi], r.u4.at[pi], r.su4, t, pi, plane_dev(t))

    loop(1, 16, lambda i: u4_move(i).start())

    def d3_done(zz):
        @pl.when(jnp.logical_not(jnp.logical_and(z // 8 == xhi, zz == z)))
        def _():
            arrived(r.d3.at[zz], r.sd3, zz)

    loop(0, 16, d3_done)
    down_total = jnp.sum(r.d3[...], axis=0)
    r.dk_out[...] = down_total[:, :64]
    r.dv_out[...] = down_total[:, 64:]

    def u4_done(i):
        t = (pi + i) % 16
        arrived(r.u4.at[t], r.su4, t)

    loop(1, 16, u4_done)
    u_back = send(r.u4, r.u5, r.one, 2, 2, (sib, f))
    u_back.start()

    def z_sent(i):
        q1(i).wait_send()
        q2(i).wait_send()

    loop(1, 4, z_sent)
    loop(0, 4, lambda i: qx(i).wait_send())

    def rows_sent(w):
        def one(i):
            w1(w, i).wait_send()
            w2(w, i).wait_send()
            for g in range(2):
                ax(w, g, i).wait_send()
                by(w, g, i).wait_send()

        def two(i):
            for g in range(2):
                wx_a(w, g, i).wait_send()
                wx_b(w, g, i).wait_send()

        loop(1, 4, one)
        loop(0, 4, two)
        for part, sems, dev in rings:
            for g, d in ((0, 0), (0, 1), (1, 0), (1, 1)):
                for h in range(2):
                    own_on(w, g, part, sems, dev, d, h).wait_send()
                pass_on(w, g, part, sems, dev, d).wait_send()

    on_own(rows_sent)

    def o1_sent(zp):
        @pl.when(jnp.logical_not(jnp.logical_and(mine, 2 * zp + c == z)))
        def _():
            o1(zp).wait_send()

    loop(0, 8, o1_sent)

    @pl.when(mine)
    def _():
        loop(1, 16, lambda i: o2(i).wait_send())

    o3.wait_send()
    swap.wait_send()
    u_swap.wait_send()
    d_swap.wait_send()

    def sixteen_sent(i):
        p_move(i).wait_send()
        qw_move(i).wait_send()
        pg_move(i).wait_send()
        hp_move(i).wait_send()
        qg_move(i).wait_send()
        u2_move(i).wait_send()
        d2_move(i).wait_send()
        u3_move(i).wait_send()
        u4_move(i).wait_send()

    loop(1, 16, sixteen_sent)

    def more_sent(k):
        qw_cross(k).wait_send()

        @pl.when(jnp.logical_not(d3_self(k)))
        def _():
            d3_move(k).wait_send()

    loop(0, 16, more_sent)
    loop(1, 32, lambda i: st_move((line + i) % 32).wait_send())

    u_back.wait_recv()

    def put(out, src):
        full = src[...].reshape(256, 128)
        for k in range(4):
            out[:, k * 128 : (k + 1) * 128] = full[k * 64 : (k + 1) * 64]

    @pl.when(c == 0)
    def _():
        put(r.uk_out, r.u4)
        put(r.uv_out, r.u5)

    @pl.when(c == 1)
    def _():
        put(r.uk_out, r.u5)
        put(r.uv_out, r.u4)

    u_back.wait_send()


def hand_over(*refs):
    half = len(refs) // 2
    for src, out in zip(refs[:half], refs[half:], strict=True):
        if len(src.shape) == 1:
            for j in range(src.shape[0]):
                out[j] = src[j]
        else:
            out[...] = src[...]


def rotary_tables(length):
    half = HEAD // 2
    frequency = ROTARY_BASE ** (-(np.arange(half) * 2.0 / HEAD))
    angles = np.arange(length)[:, None] * frequency[None, :]
    cosine, sine = np.cos(angles), np.sin(angles)
    return (
        np.concatenate([cosine, cosine], axis=1).astype(np.float32),
        np.concatenate([-sine, sine], axis=1).astype(np.float32),
    )


def shards(
    queries,
    passages,
    positives,
    hidden,
    norm_gain,
    last_query,
    frozen_key_weight,
    frozen_value_weight,
    key_down,
    key_adapter_up,
    value_down,
    value_adapter_up,
    out_weight,
):
    vm = pl.BlockSpec(memory_space=pltpu.VMEM)
    specs = [pl.BlockSpec(memory_space=pl.ANY)] * len(INPUTS)
    specs[INPUTS.index("pos_in")] = pl.BlockSpec(memory_space=pltpu.SMEM)
    for name in ("ku_in", "vu_in"):
        specs[INPUTS.index(name)] = vm
    shapes = ((2,), (2, 4096), (2, 4096), (8, 64), (8, 64), (64, 512), (64, 512))
    cosine, sine = rotary_tables(256)
    outs = (vm,) * len(shapes)
    outs = (pl.BlockSpec(memory_space=pltpu.SMEM), *outs[1:])
    results = pl.pallas_call(
        kernel,
        out_shape=tuple(jax.ShapeDtypeStruct(shape, F32) for shape in shapes),
        in_specs=specs,
        out_specs=outs,
        scratch_shapes=[pltpu.VMEM(shape, dtype) for shape, dtype in BUFFERS.values()]
        + [pltpu.SemaphoreType.DMA(shape) for shape in SEMAPHORES.values()],
        compiler_params=pltpu.CompilerParams(
            collective_id=0, has_side_effects=True, vmem_limit_bytes=VMEM_BYTES
        ),
    )(
        queries,
        passages,
        positives,
        hidden.reshape(512, 4096),
        norm_gain,
        last_query,
        frozen_key_weight,
        frozen_value_weight,
        key_down.T,
        key_adapter_up,
        value_down.T,
        value_adapter_up,
        out_weight,
        cosine,
        sine,
    )
    return pl.pallas_call(
        hand_over,
        out_shape=tuple(jax.ShapeDtypeStruct(shape, F32) for shape in shapes),
        in_specs=outs,
        out_specs=outs,
    )(*results)


def solution(mesh):
    rows = P(("batch", "fsdp"), None)
    placed = (
        rows,
        rows,
        P(("batch", "fsdp")),
        P(("batch", "fsdp"), None, None),
        P(),
        rows,
        P("fsdp", None),
        P("fsdp", None),
        P("fsdp", None),
        P(),
        P("fsdp", None),
        P(),
        P("batch", "fsdp"),
    )
    return jax.shard_map(
        shards,
        mesh=mesh,
        in_specs=placed,
        out_specs=(P(("batch", "fsdp")), rows, rows, rows, rows, P(), P()),
        check_vma=False,
    )
```

```python
import jax
import jax.numpy as jnp
import numpy as np
from jax import lax
from jax.experimental import pallas as pl
from jax.experimental.pallas import tpu as pltpu
from jax.sharding import PartitionSpec as P

F32 = jnp.float32
BF16 = jnp.bfloat16
MESH = pl.DeviceIdType.MESH
HEAD = 128
SCALE = 20.0
EPSILON = 1e-06
ROTARY_BASE = 1000000.0
VMEM_BYTES = 56 * 1024 * 1024
ROOT = HEAD ** (-0.5)


def position():
    b = lax.axis_index("batch")
    f = lax.axis_index("fsdp")
    y = b // 4
    xlo = (b // 2) % 2
    c = b % 2
    z = f // 2
    xhi = f % 2
    return (b, f, y, xlo, c, z, xhi)


def remote(src, dst, send_sem, recv_sem, b, f):
    return pltpu.make_async_remote_copy(
        src_ref=src,
        dst_ref=dst,
        send_sem=send_sem,
        recv_sem=recv_sem,
        device_id=(b, f),
        device_id_type=MESH,
    )


def loop(lo, hi, body):
    def step(i, carry):
        body(i)
        return carry

    lax.fori_loop(lo, hi, step, 0)


def iota(shape, dim):
    return lax.broadcasted_iota(jnp.int32, shape, dim)


def dot(a, b, ca=1, cb=0, precision=None):
    return lax.dot_general(
        a, b, (((ca,), (cb,)), ((), ())), preferred_element_type=F32, precision=precision
    )


def far_first(i):
    return 8 + (i // 2) * (2 * (i % 2) - 1)


INPUTS = (
    "q_in", "p_in", "pos_in", "hid_in", "gain_in", "lq_in", "fk_in", "fv_in",
    "kd_in", "ku_in", "vd_in", "vu_in", "wo_in", "cos_in", "sin_in",
)
OUTPUTS = ("loss_out", "qg_out", "pg_out", "dk_out", "dv_out", "uk_out", "uv_out")
BUFFERS = {
    "q_v": ((2, 4096), BF16),
    "p_v": ((2, 4096), BF16),
    "gain_v": ((4096,), BF16),
    "lq_v": ((2, 2048), BF16),
    "downs_v": ((2, 64, 128), BF16),
    "wo_v": ((128, 128), BF16),
    "cos_v": ((256, 128), F32),
    "sin_v": ((256, 128), F32),
    "tmp": ((16, 512), F32),
    "lq": ((2, 16, 128), F32),
    "hid": ((512, 4096), BF16),
    "qs": ((2, 4, 4, 16, 640), BF16),
    "ps": ((16, 16, 512), BF16),
    "ws": ((2, 8, 16, 128), BF16),
    "wg": ((2, 2, 8, 128, 128), BF16),
    "qwg": ((16, 2, 32, 128), BF16),
    "st": ((32, 4, 128), F32),
    "pgs": ((16, 16, 512), BF16),
    "pgr": ((16, 16, 512), BF16),
    "hps": ((16, 32, 128), BF16),
    "hpr": ((16, 32, 128), BF16),
    "qgs": ((2, 16, 16, 512), BF16),
    "qgx": ((16, 16, 512), BF16),
    "qgr": ((16, 16, 512), BF16),
    "wk": ((4, 4, 2, 4, 2, 16, 640), BF16),
    "wv": ((4, 4, 2, 4, 2, 16, 512), BF16),
    "dn": ((128, 128), BF16),
    "ku": ((128, 512), BF16),
    "vu": ((128, 512), BF16),
    "raw_k": ((512, 640), F32),
    "raw_v": ((512, 512), F32),
    "low": ((512, 128), BF16),
    "keys": ((512, 512), BF16),
    "values": ((512, 512), BF16),
    "vg": ((512, 512), BF16),
    "gq": ((2, 16, 512), BF16),
    "back": ((128, 512), BF16),
    "att": ((2, 16, 256), F32),
    "dt": ((8, 2, 2, 128, 128), BF16),
    "d1": ((8, 2, 128, 128), BF16),
    "r1": ((16, 128, 128), BF16),
    "d2": ((16, 128, 128), BF16),
    "r2": ((16, 8, 128), F32),
    "d3": ((16, 8, 128), F32),
    "u0": ((2, 4, 64, 128), BF16),
    "u1": ((4, 64, 128), BF16),
    "v1": ((16, 16, 128), BF16),
    "u2": ((16, 16, 128), BF16),
    "v3": ((16, 128), F32),
    "u3": ((16, 16, 128), F32),
    "u4": ((32, 16, 128), F32),
}
SEMAPHORES = {
    "loc": (13,),
    "q1": (2, 4), "q2": (2, 4), "qx": (2, 4),
    "w1": (2, 4), "w2": (2, 4), "wx": (2, 16),
    "ax": (2, 8), "ay": (2, 12), "bx": (2, 12), "by": (2, 8),
    "p": (2, 16), "o1": (2, 16), "o2": (2, 16), "o3": (2,),
    "qw": (2, 16), "qwx": (2, 16), "sts": (2, 32),
    "pg": (2, 16), "hp": (2, 16), "qg": (2, 16), "qgc": (2,),
    "one": (2, 3), "sd2": (2, 16), "sd3": (2, 16),
    "su2": (2, 16), "su3": (2, 16), "su4": (2, 32),
}


class Refs:
    pass


def kernel(*refs):
    r = Refs()
    for name, ref in zip((*INPUTS, *OUTPUTS, *BUFFERS, *SEMAPHORES), refs, strict=True):
        setattr(r, name, ref)
    b, f, y, xlo, c, z, xhi = position()
    zh, zl = z // 4, z % 4
    pi = (b // 2) * 2 + xhi
    sib = b + 1 - 2 * c
    line = c * 16 + z
    OUT, IN = 0, 1

    def plane_dev(t):
        return ((t // 2) * 2 + c, z * 2 + t % 2)

    def line_dev(s):
        return ((b // 2) * 2 + s // 16, (s % 16) * 2 + xhi)

    def z_dev(zz):
        return (b, zz * 2 + xhi)

    def x_of(i):
        return (xhi * 2 + xlo + i) % 4

    def x_dev(i):
        x = x_of(i)
        return (y * 4 + (x % 2) * 2 + c, z * 2 + x // 2)

    def y_dev(i):
        return (((y + i) % 4) * 4 + xlo * 2 + c, f)

    def send(src, dst, sems, out, into, dev):
        return remote(src, dst, sems.at[OUT, out], sems.at[IN, into], dev[0], dev[1])

    def arrived(dst, sems, into):
        remote(dst, dst, sems.at[OUT, into], sems.at[IN, into], sib, f).wait_recv()

    piece = pl.ds(pl.multiple_of((y * 2 + xlo) * 16, 16), 16)
    fetch = [
        pltpu.make_async_copy(src, dst, r.loc.at[n])
        for n, (src, dst) in enumerate(
            (
                (r.fk_in.at[piece, :], r.wk.at[zh, 0, xhi, y, xlo, :, 0:512]),
                (r.fv_in.at[piece, :], r.wv.at[zh, 0, xhi, y, xlo]),
                (r.q_in, r.q_v),
                (r.p_in, r.p_v),
                (r.kd_in, r.downs_v.at[0]),
                (r.vd_in, r.downs_v.at[1]),
                (r.wo_in, r.wo_v),
                (r.hid_in, r.hid),
                (r.gain_in, r.gain_v),
                (r.lq_in, r.lq_v),
                (r.cos_in, r.cos_v),
                (r.sin_in, r.sin_v),
            )
        )
    ]

    @pl.when(c == 0)
    def _():
        fetch[0].start()

    @pl.when(c == 1)
    def _():
        fetch[1].start()

    for copy in fetch[2:]:
        copy.start()
    barrier = pltpu.get_barrier_semaphore()

    def greet(dev):
        pl.semaphore_signal(barrier, inc=1, device_id=dev, device_id_type=MESH)

    def greet_line(i):
        zz = (z + far_first(i)) % 16
        greet(line_dev(zz))
        greet(line_dev(16 + zz))

    loop(1, 16, greet_line)
    def greet_plane(i):
        tb, tf = plane_dev((pi + i) % 16)
        greet((tb, tf))
        greet((tb + 1 - 2 * c, tf))

    loop(1, 16, greet_plane)
    greet((sib, f))

    def slab(ref):
        rows = ref[...].astype(F32)
        for j in range(2):
            for k in range(8):
                r.tmp[j * 8 + k : j * 8 + k + 1, :] = rows[j : j + 1, k * 512 : (k + 1) * 512]
        return r.tmp[...].astype(BF16)

    fetch[2].wait()
    r.qs[c, zh, zl, :, 0:512] = slab(r.q_v)
    fetch[3].wait()
    r.ps[pi] = slab(r.p_v)
    fetch[4].wait()
    fetch[5].wait()
    fetch[6].wait()
    row, lane = iota((16, 128), 0), iota((16, 128), 1)
    mark = jnp.zeros((16, 128), F32)
    for j in range(2):
        spot = r.pos_in[j]
        high, low = (spot // 32).astype(F32), (spot % 32).astype(F32)
        mark = jnp.where((row == j * 8) & (lane == 0), high, mark)
        mark = jnp.where((row == j * 8) & (lane == 1), low, mark)
    r.qs[c, zh, zl, :, 512:640] = mark.astype(BF16)
    @pl.when(c == 0)
    def _():
        fetch[0].wait()
        downs = r.downs_v[...].reshape(128, 128).astype(F32)
        r.dn[...] = jnp.transpose(downs).astype(BF16)
        r.wk[zh, 0, xhi, y, xlo, :, 512:640] = r.dn[piece, :]

    @pl.when(c == 1)
    def _():
        fetch[1].wait()

    pl.semaphore_wait(barrier, 61)

    def far(i):
        return z_dev((z + 4 * i) % 16)

    def near(i):
        return z_dev((z + i - 4 * (i // 3)) % 16)

    def q1(i):
        own = r.qs.at[c, zh, zl]
        return send(own, own, r.q1, i, 4 - i, far(i))

    def q2(i):
        part = r.qs.at[c, :, zl]
        return send(part, part, r.q2, i, 4 - i, near(i))

    def qx(i):
        part = r.qs.at[c, :, (zl + i) % 4]
        return send(part, part, r.qx, i, i, (sib, f))

    mine = c == xlo

    def o1(zp):
        return send(
            r.wo_v.at[pl.ds(zp * 16, 16), :],
            r.ws.at[z % 2, z // 2],
            r.o1,
            zp,
            z,
            ((b // 2) * 2 + xlo, (2 * zp + c) * 2 + xhi),
        )

    def o1_start(zp):
        here = jnp.logical_and(mine, 2 * zp + c == z)

        @pl.when(jnp.logical_not(here))
        def _():
            o1(zp).start()

        @pl.when(here)
        def _():
            r.ws[z % 2, z // 2] = r.wo_v[pl.ds(zp * 16, 16), :]

    loop(0, 8, o1_start)
    loop(1, 4, lambda i: q1(i).start())

    def p_move(i):
        t = (pi + i) % 16
        return send(r.ps.at[pi], r.ps.at[pi], r.p, t, pi, plane_dev(t))

    def on_own(body):
        pl.when(c == 0)(lambda: body(r.wk))
        pl.when(c == 1)(lambda: body(r.wv))

    def on_other(body):
        pl.when(c == 0)(lambda: body(r.wv))
        pl.when(c == 1)(lambda: body(r.wk))

    def w1(w, i):
        own = w.at[zh, 0, xhi, y, xlo]
        return send(own, own, r.w1, i, 4 - i, far(i))

    def w1_start(w):
        loop(1, 4, lambda i: w1(w, i).start())

    def w2(w, i):
        part = w.at[:, 0, xhi, y, xlo]
        return send(part, w.at[:, 4 - i, xhi, y, xlo], r.w2, i, 4 - i, near(i))

    lo_z, hi_z = pl.ds(0, 2), pl.ds(2, 2)

    near_z = (pl.ds(0, 1), pl.ds(1, 3))

    def ax(w, g, i):
        part = w.at[lo_z, near_z[g], xhi, y, xlo]
        return send(part, part, r.ax, 4 * g + i, 4 * g + 4 - i, x_dev(i))

    def by(w, g, i):
        part = w.at[hi_z, near_z[g], xhi, y, xlo]
        return send(part, part, r.by, 4 * g + i, 4 * g + 4 - i, y_dev(i))

    def a_part(w, g, i, h):
        return w.at[h, near_z[g], :, (y + i) % 4]

    def b_part(w, g, i, h):
        x = x_of(i)
        return w.at[2 + h, near_z[g], x // 2, :, x % 2]

    def own_on(w, g, part, sems, dev, d, h):
        own = part(w, g, 0, h)
        n = 6 * g + d * 2 + h
        return send(own, own, sems, n, n, dev(1 + 2 * d))

    def pass_on(w, g, part, sems, dev, d):
        got = part(w, g, 3 - 2 * d, 1 - d)
        n = 6 * g + 4 + d
        return send(got, got, sems, n, n, dev(1 + 2 * d))

    rings = ((a_part, r.ay, y_dev), (b_part, r.bx, x_dev))

    def wx_a(w, g, i):
        part = w.at[lo_z, near_z[g], :, (y + i) % 4]
        return send(part, part, r.wx, 8 * g + i, 8 * g + i, (sib, f))

    def wx_b(w, g, i):
        x = x_of(i)
        part = w.at[hi_z, near_z[g], x // 2, :, x % 2]
        return send(part, part, r.wx, 8 * g + 4 + i, 8 * g + 4 + i, (sib, f))

    def first_start(w, g):
        loop(1, 4, lambda i: ax(w, g, i).start())
        loop(1, 4, lambda i: by(w, g, i).start())

    def first_done(w, g):
        def a_done(i):
            x = x_of(i)
            arrived(w.at[lo_z, near_z[g], x // 2, y, x % 2], r.ax, 4 * g + i)

        def b_done(i):
            part = w.at[hi_z, near_z[g], xhi, (y + i) % 4, xlo]
            arrived(part, r.by, 4 * g + i)

        loop(1, 4, a_done)
        loop(1, 4, b_done)

    def second_start(w, g):
        for part, sems, dev in rings:
            own_on(w, g, part, sems, dev, 0, 1).start()
            own_on(w, g, part, sems, dev, 1, 0).start()
        for part, sems, dev in rings:
            own_on(w, g, part, sems, dev, 0, 0).start()
            own_on(w, g, part, sems, dev, 1, 1).start()
        wx_a(w, g, 0).start()
        wx_b(w, g, 0).start()

    def second_pass(w, g):
        for part, sems, dev in rings:
            arrived(part(w, g, 3, 1), sems, 6 * g + 1)
            pass_on(w, g, part, sems, dev, 0).start()
            arrived(part(w, g, 1, 0), sems, 6 * g + 2)
            pass_on(w, g, part, sems, dev, 1).start()

    def second_done(w, g):
        for (part, sems, dev), cross in zip(rings, (wx_a, wx_b)):
            arrived(part(w, g, 3, 0), sems, 6 * g)
            cross(w, g, 3).start()
            arrived(part(w, g, 1, 1), sems, 6 * g + 3)
            cross(w, g, 1).start()
        for (part, sems, dev), cross in zip(rings, (wx_a, wx_b)):
            arrived(part(w, g, 2, 1), sems, 6 * g + 4)
            arrived(part(w, g, 2, 0), sems, 6 * g + 5)
            cross(w, g, 2).start()

    def cross_a_done(w):
        for g in range(2):
            loop(
                0,
                4,
                lambda i: arrived(
                    w.at[lo_z, near_z[g], :, (y + i) % 4], r.wx, 8 * g + i
                ),
            )

    def cross_b_done(w):
        for g in range(2):

            def one(i):
                x = x_of(i)
                part = w.at[hi_z, near_z[g], x // 2, :, x % 2]
                arrived(part, r.wx, 8 * g + 4 + i)

            loop(0, 4, one)

    def keys_core(body, g):
        pl.when(c == 0)(lambda: body(r.wk, g))

    def values_core(body, g):
        pl.when(c == 1)(lambda: body(r.wv, g))

    def each_core(body, g):
        keys_core(body, g)
        values_core(body, g)

    on_own(w1_start)
    loop(1, 16, lambda i: p_move(i).start())

    r.ku[0:64, :] = r.ku_in[...]
    r.ku[64:128, :] = jnp.zeros((64, 512), BF16)
    r.vu[0:64, :] = jnp.zeros((64, 512), BF16)
    r.vu[64:128, :] = r.vu_in[...]
    fetch[9].wait()
    wide_q = r.lq_v[...].astype(F32)
    for j in range(2):
        for h in range(16):
            r.lq[j, h : h + 1, :] = wide_q[j : j + 1, h * 128 : (h + 1) * 128]

    fetch[7].wait()
    fetch[8].wait()

    def norm(i):
        rows = pl.ds(pl.multiple_of(i * 32, 32), 32)
        x = r.hid[rows, :].astype(F32)
        scale = lax.rsqrt(jnp.mean(x * x, axis=1, keepdims=True) + EPSILON)
        r.hid[rows, :] = (x * scale * r.gain_v[...].astype(F32).reshape(1, 4096)).astype(BF16)

    loop(0, 8, norm)
    loop(1, 4, lambda i: arrived(r.qs.at[c, (zh + i) % 4, zl], r.q1, i))
    loop(1, 4, lambda i: q2(i).start())
    qx(0).start()

    def o2_slot(t, yy):
        return r.wg.at[:, t, :, pl.ds((c * 4 + yy) * 16, 16), :]

    def o2(i):
        t = (pi + i) % 16
        return send(r.ws, o2_slot(xhi, y), r.o2, t, y * 2 + xhi, plane_dev(t))

    @pl.when(mine)
    def _():
        def one(zz):
            @pl.when(jnp.logical_not(jnp.logical_and(z % 2 == c, zz == z)))
            def _():
                arrived(r.ws.at[zz % 2, zz // 2], r.o1, zz)

        loop(0, 16, one)
        loop(1, 16, lambda i: o2(i).start())
        r.wg[:, xhi, :, pl.ds((c * 4 + y) * 16, 16), :] = r.ws[...]

    def w1_done(w):
        loop(1, 4, lambda i: arrived(w.at[(zh + i) % 4, 0, xhi, y, xlo], r.w1, i))
        loop(1, 4, lambda i: w2(w, i).start())

    on_own(w1_done)
    each_core(first_start, 0)
    loop(8, 16, norm)

    def q2_done(i):
        arrived(r.qs.at[c, :, (zl + i) % 4], r.q2, i)
        qx(i).start()

    loop(1, 4, q2_done)

    def w2_done(w):
        loop(1, 4, lambda i: arrived(w.at[:, i, xhi, y, xlo], r.w2, i))

    each_core(first_done, 0)
    each_core(second_start, 0)
    on_own(w2_done)
    keys_core(first_start, 1)

    def p_done(i):
        t = (pi + i) % 16
        arrived(r.ps.at[t], r.p, t)

    loop(1, 16, p_done)
    loop(0, 4, lambda i: arrived(r.qs.at[1 - c, :, (zl + i) % 4], r.qx, i))
    q_all = r.qs[...].reshape(512, 640)
    q_rows = q_all[:, :512]
    p_rows = r.ps[...].reshape(256, 512)
    wide = dot(p_rows, q_rows, 1, 1).reshape(32, 8, 512)
    same = iota((32, 8, 512), 1) == iota((32, 8, 512), 2) % 8
    folded = jnp.sum(jnp.where(same, wide, 0.0), axis=1)
    fold = (iota((512, 64), 0) // 8 == iota((512, 64), 1)).astype(F32)
    scores = SCALE * dot(folded, fold, precision=lax.Precision.HIGHEST)
    marks = dot(q_all[:, 512:], fold.astype(BF16), 0, 0)
    target = marks[0:1] * 32.0 + marks[1:2]
    pid = iota((32, 64), 0)
    ptile = pid // 2
    ids = (((ptile // 2) * 2 + c) * 32 + z * 2 + ptile % 2) * 2 + pid % 2
    hit = (ids.astype(F32) == target).astype(F32)
    top = jnp.max(scores, axis=0, keepdims=True)
    local = top + jnp.log(jnp.sum(jnp.exp(scores - top), axis=0, keepdims=True))
    r.st[line] = jnp.zeros((4, 128), F32)
    r.st[line, 0:1, 0:64] = local
    r.st[line, 1:2, 0:64] = jnp.sum(scores * hit, axis=0, keepdims=True)

    def st_move(s):
        return send(r.st.at[line], r.st.at[line], r.sts, s, line, line_dev(s))

    def st_start(i):
        zz = (z + far_first(i)) % 16
        st_move(zz).start()
        st_move(16 + zz).start()

    loop(1, 16, st_start)
    st_move((1 - c) * 16 + z).start()

    half = r.wg.at[:, :, :, pl.ds(c * 64, 64), :]
    other = r.wg.at[:, :, :, pl.ds((1 - c) * 64, 64), :]

    def o2_done(s):
        @pl.when(jnp.logical_not(jnp.logical_and(mine, s == y * 2 + xhi)))
        def _():
            arrived(o2_slot(s % 2, s // 2), r.o2, s)

    loop(0, 8, o2_done)
    o3 = remote(half, half, r.o3.at[0], r.o3.at[1], sib, f)
    o3.start()
    each_core(second_pass, 0)
    keys_core(first_done, 1)
    keys_core(second_start, 1)
    values_core(first_start, 1)
    remote(other, other, r.o3.at[0], r.o3.at[1], sib, f).wait_recv()
    q_half = r.qs[c].reshape(256, 640)
    prod = jnp.zeros((256, 1024), F32)
    for a in range(4):
        prod += dot(
            q_half[:, a * 128 : (a + 1) * 128], r.wg[a // 2, a % 2].reshape(1024, 128), 1, 1
        )
    qw = jnp.zeros((256, 128), F32)
    chunk = iota((256, 128), 0) % 8
    for a in range(8):
        qw += jnp.where(chunk == a, prod[:, a * 128 : (a + 1) * 128], 0.0)
    r.qwg[z, c] = jnp.sum(qw.reshape(32, 8, 128), axis=1).astype(BF16)

    def qw_move(i):
        zz = (z + far_first(i)) % 16
        return send(r.qwg.at[z, c], r.qwg.at[z, c], r.qw, zz, z, z_dev(zz))

    def qw_cross(zz):
        return send(r.qwg.at[zz, c], r.qwg.at[zz, c], r.qwx, zz, zz, (sib, f))

    loop(1, 16, lambda i: qw_move(i).start())
    qw_cross(z).start()

    each_core(second_done, 0)
    keys_core(second_pass, 1)
    def st_done(i):
        s = (line + i) % 32
        arrived(r.st.at[s], r.sts, s)

    loop(1, 32, st_done)
    stats = r.st[...]
    peak = jnp.max(stats, axis=0)
    total = peak + jnp.log(jnp.sum(jnp.exp(stats - peak[None]), axis=0))
    picked = jnp.sum(stats, axis=0)
    lse = total[0:1, :64]
    weights = (jnp.exp(scores - lse) - hit).astype(BF16)

    def qw_done(i):
        zz = (z + far_first(16 - i)) % 16
        arrived(r.qwg.at[zz, c], r.qw, zz)
        qw_cross(zz).start()

    loop(1, 16, qw_done)
    loop(0, 16, lambda zz: arrived(r.qwg.at[zz, 1 - c], r.qwx, zz))
    rows16 = (iota((512, 32), 0) // 16 == iota((512, 32), 1)).astype(BF16)
    cols64 = (iota((64, 1024), 1) % 64 == iota((64, 1024), 0)).astype(BF16)
    tall = dot(dot(rows16, weights).astype(BF16), cols64)
    diag = iota((512, 1024), 0) % 16 == iota((512, 1024), 1) // 64
    tall = jnp.where(diag, tall, 0.0).astype(BF16)
    r.hps[...] = (
        (SCALE * dot(tall, r.qwg[...].reshape(1024, 128))).astype(BF16).reshape(16, 32, 128)
    )

    def hp_move(i):
        t = (pi + i) % 16
        return send(r.hps.at[t], r.hpr.at[pi], r.hp, t, pi, plane_dev(t))

    def pg_move(i):
        t = (pi + i) % 16
        return send(r.pgs.at[t], r.pgr.at[pi], r.pg, t, pi, plane_dev(t))

    loop(1, 16, lambda i: hp_move(i).start())
    r.hpr[pi] = r.hps[pi]
    values_core(first_done, 1)
    values_core(second_start, 1)
    rows8 = (iota((256, 32), 0) // 8 == iota((256, 32), 1)).astype(BF16)
    cols8 = (iota((64, 512), 1) // 8 == iota((64, 512), 0)).astype(BF16)
    spread = dot(dot(rows8, weights).astype(BF16), cols8)
    diag = iota((256, 512), 0) % 8 == iota((256, 512), 1) % 8
    spread = jnp.where(diag, spread, 0.0).astype(BF16)
    r.pgs[...] = (SCALE * dot(spread, q_rows)).astype(BF16).reshape(16, 16, 512)
    r.pgr[pi] = r.pgs[pi]

    r.qgs[...] = (SCALE * dot(spread, p_rows, 0, 0)).astype(BF16).reshape(2, 16, 16, 512)
    swap = remote(r.qgs.at[1 - c], r.qgx, r.qgc.at[0], r.qgc.at[1], sib, f)
    swap.start()
    loss = picked[1:2, :64]
    loss = lse - loss
    spot = iota((1, 64), 1)
    for j in range(2):
        r.loss_out[j] = jnp.sum(jnp.where(spot == 2 * line + j, loss, 0.0))

    def qg_move(i):
        zz = (z + far_first(i)) % 16
        return send(r.qgs.at[c, zz], r.qgr.at[z], r.qg, zz, z, z_dev(zz))

    keys_core(second_done, 1)
    values_core(second_pass, 1)

    pl.when(c == 1)(lambda: cross_a_done(r.wk))
    pl.when(c == 1)(lambda: cross_b_done(r.wk))
    def tokens_of(k):
        cols = [pl.multiple_of((k * 4 + (zl + j) % 4) * 256, 256) for j in range(4)]
        return jnp.concatenate([r.hid[:, pl.ds(col, 256)] for col in cols], axis=1)

    def project(w, raw, k):
        tokens = tokens_of(k)
        part = dot(tokens, w[k].reshape(1024, w.shape[-1]))

        @pl.when(k == 0)
        def _():
            raw[...] = part

        @pl.when(k > 0)
        def _():
            raw[...] += part

    loop(0, 4, lambda k: project(r.wk, r.raw_k, k))
    r.low[...] = r.raw_k[:, 512:640].astype(BF16)
    adapted = dot(r.low[...], r.ku[...])
    fetch[10].wait()
    fetch[11].wait()
    own_group = iota((16, 512), 0) // 4 == iota((16, 512), 1) // 128

    def by_group(rows):
        return jnp.where(own_group, jnp.concatenate([rows] * 4, axis=1), 0.0).astype(BF16)

    queries = [by_group(r.lq[j]) for j in range(2)]
    for j in range(2):
        tok = slice(j * 256, (j + 1) * 256)
        for g in range(4):
            col = slice(g * 128, (g + 1) * 128)
            key = r.raw_k[tok, col] + 2.0 * adapted[tok, col]
            turned = pltpu.roll(key, 64, axis=1)
            r.keys[tok, col] = (key * r.cos_v[...] + turned * r.sin_v[...]).astype(BF16)
        sim = dot(queries[j], r.keys[tok, :], 1, 1) * ROOT
        sim = jnp.exp(sim - jnp.max(sim, axis=1, keepdims=True))
        r.att[j] = sim / jnp.sum(sim, axis=1, keepdims=True)

    swap.wait_recv()
    r.qgs[c] = (r.qgs[c].astype(F32) + r.qgx[...].astype(F32)).astype(BF16)
    loop(1, 16, lambda i: qg_move(i).start())
    r.qgr[z] = r.qgs[c, z]
    values_core(second_done, 1)
    loop(1, 16, lambda i: pg_move(i).start())
    def hp_done(i):
        t = (pi + i) % 16
        arrived(r.hpr.at[t], r.hp, t)

    loop(1, 16, hp_done)
    heads = jnp.sum(r.hpr[...].astype(F32), axis=0).astype(BF16)
    row, lane = iota((128, 128), 0), iota((128, 128), 1)
    tile = (iota((128, 16), 0) % 16 == iota((128, 16), 1)).astype(BF16)
    group = (row % 16 == lane % 16).astype(BF16)
    head, src = iota((16, 128), 0), iota((16, 128), 1)
    place, at_z = src // 16, src % 16
    collect = (
        ((place % 4) * 4 + (place // 4) * 2 + at_z % 2 == head)
    ).astype(BF16)
    for j in range(2):
        tok = slice(j * 256, (j + 1) * 256)
        spread_rows = dot(tile, heads[j * 16 : (j + 1) * 16])
        spread_rows = jnp.where(lane // 16 == row // 16, spread_rows, 0.0).astype(BF16)
        copied = dot(spread_rows, group)
        copied = jnp.where(lane // 16 == (row % 16) // 2, copied, 0.0).astype(BF16)
        r.gq[j] = by_group(dot(collect, copied))
        r.vg[tok, :] = dot(r.att[j].astype(BF16), r.gq[j], 0, 0).astype(BF16)
    up_v = (2.0 * dot(r.low[...], r.vg[...], 0, 0)).astype(BF16)
    for k in range(4):
        r.u0[1, k] = up_v[64:128, k * 128 : (k + 1) * 128]
    r.raw_v[...] = 2.0 * dot(r.low[...], r.vu[...])

    def project_values(k):
        tokens = tokens_of(k)
        r.raw_v[...] += dot(tokens, r.wv[k].reshape(1024, 512))

    pl.when(c == 0)(lambda: cross_a_done(r.wv))
    loop(0, 2, project_values)
    pl.when(c == 0)(lambda: cross_b_done(r.wv))
    loop(2, 4, project_values)
    r.values[...] = r.raw_v[...].astype(BF16)
    for j in range(2):
        tok = slice(j * 256, (j + 1) * 256)
        prob = dot(r.gq[j], r.values[tok, :], 1, 1)
        attention = r.att[j]
        expected = jnp.sum(attention * prob, axis=1, keepdims=True)
        score_grad = attention * (prob - expected)
        turned_grad = dot(score_grad.astype(BF16), queries[j], 0, 0) * ROOT
        for g in range(4):
            col = slice(g * 128, (g + 1) * 128)
            part = turned_grad[:, col]
            turned = pltpu.roll(part, 64, axis=1)
            r.keys[tok, col] = (part * r.cos_v[...] - turned * r.sin_v[...]).astype(BF16)

    up_k = (2.0 * dot(r.low[...], r.keys[...], 0, 0)).astype(BF16)
    for k in range(4):
        r.u0[0, k] = up_k[0:64, k * 128 : (k + 1) * 128]
    u_swap = send(r.u0.at[1 - c], r.u1, r.one, 0, 0, (sib, f))
    u_swap.start()
    back = dot(r.keys[...], r.ku[...], 1, 1) + dot(r.vg[...], r.vu[...], 1, 1)
    r.back[...] = jnp.transpose(back.astype(BF16).astype(F32)).astype(BF16)

    def down(j, cc):
        cols = pl.ds(pl.multiple_of((j * 2 + cc) * 256, 256), 256)
        part = (2.0 * dot(r.back[...], r.hid[:, cols])).astype(BF16)
        r.dt[j, cc, 0] = part[:, :128]
        r.dt[j, cc, 1] = part[:, 128:]

    loop(0, 8, lambda j: down(j, 1 - c))
    d_swap = send(r.dt.at[:, 1 - c], r.d1, r.one, 1, 1, (sib, f))
    d_swap.start()
    u_swap.wait_recv()
    r.v1[...] = (
        (r.u0[c].astype(F32) + r.u1[...].astype(F32)).astype(BF16).reshape(16, 16, 128)
    )

    def u2_move(i):
        t = (pi + i) % 16
        return send(r.v1.at[t], r.u2.at[pi], r.su2, t, pi, plane_dev(t))

    def d2_move(i):
        t = (pi + i) % 16
        return send(r.r1.at[t], r.d2.at[pi], r.sd2, t, pi, plane_dev(t))

    loop(1, 16, lambda i: u2_move(i).start())
    r.u2[pi] = r.v1[pi]
    loop(0, 8, lambda j: down(j, c))
    d_swap.wait_recv()
    r.r1[...] = (
        (r.dt[:, c].astype(F32) + r.d1[...].astype(F32)).astype(BF16).reshape(16, 128, 128)
    )
    loop(1, 16, lambda i: d2_move(i).start())
    r.d2[pi] = r.r1[pi]

    def u2_done(i):
        t = (pi + i) % 16
        arrived(r.u2.at[t], r.su2, t)

    loop(1, 16, u2_done)
    r.v3[...] = jnp.sum(r.u2[...].astype(F32), axis=0)
    r.u3[z] = r.v3[...]

    def u3_move(i):
        zz = (z + far_first(i)) % 16
        return send(r.v3, r.u3.at[z], r.su3, zz, z, z_dev(zz))

    loop(1, 16, lambda i: u3_move(i).start())

    def d2_done(i):
        t = (pi + i) % 16
        arrived(r.d2.at[t], r.sd2, t)

    loop(1, 16, d2_done)
    r.r2[...] = jnp.transpose(jnp.sum(r.d2[...].astype(F32), axis=0)).reshape(16, 8, 128)

    def d3_move(k):
        return send(
            r.r2.at[k], r.d3.at[z], r.sd3, k, z, (b, (8 * xhi + k // 2) * 2 + k % 2)
        )

    def d3_self(k):
        return (8 * xhi + k // 2) * 2 + k % 2 == f

    def d3_start(k):
        @pl.when(jnp.logical_not(d3_self(k)))
        def _():
            d3_move(k).start()

        @pl.when(d3_self(k))
        def _():
            r.d3[z] = r.r2[k]

    loop(0, 16, d3_start)

    def put_rows(out, total):
        r.tmp[...] = total
        for j in range(2):
            for k in range(8):
                out[j : j + 1, k * 512 : (k + 1) * 512] = r.tmp[j * 8 + k : j * 8 + k + 1, :]

    def pg_done(i):
        t = (pi + i) % 16
        arrived(r.pgr.at[t], r.pg, t)

    def qg_done(i):
        t = (z + i) % 16
        arrived(r.qgr.at[t], r.qg, t)

    loop(1, 16, pg_done)
    put_rows(r.pg_out, jnp.sum(r.pgr[...].astype(F32), axis=0))
    loop(1, 16, qg_done)
    put_rows(r.qg_out, jnp.sum(r.qgr[...].astype(F32), axis=0))

    def u3_done(i):
        t = (z + i) % 16
        arrived(r.u3.at[t], r.su3, t)

    loop(1, 16, u3_done)
    up_own = c * 16 + pi
    r.u4[up_own] = jnp.sum(r.u3[...], axis=0)

    def u4_move(i):
        t = (up_own + i) % 32
        dev = (((t % 16) // 2) * 2 + t // 16, z * 2 + t % 2)
        return send(r.u4.at[up_own], r.u4.at[up_own], r.su4, t, up_own, dev)

    loop(1, 32, lambda i: u4_move(i).start())

    def d3_done(zz):
        @pl.when(jnp.logical_not(jnp.logical_and(z // 8 == xhi, zz == z)))
        def _():
            arrived(r.d3.at[zz], r.sd3, zz)

    loop(0, 16, d3_done)
    down_total = jnp.sum(r.d3[...], axis=0)
    r.dk_out[...] = down_total[:, :64]
    r.dv_out[...] = down_total[:, 64:]

    def z_sent(i):
        q1(i).wait_send()
        q2(i).wait_send()

    loop(1, 4, z_sent)
    loop(0, 4, lambda i: qx(i).wait_send())

    def rows_sent(w):
        def one(i):
            w1(w, i).wait_send()
            w2(w, i).wait_send()
            for g in range(2):
                ax(w, g, i).wait_send()
                by(w, g, i).wait_send()

        def two(i):
            for g in range(2):
                wx_a(w, g, i).wait_send()
                wx_b(w, g, i).wait_send()

        loop(1, 4, one)
        loop(0, 4, two)
        for part, sems, dev in rings:
            for g, d in ((0, 0), (0, 1), (1, 0), (1, 1)):
                for h in range(2):
                    own_on(w, g, part, sems, dev, d, h).wait_send()
                pass_on(w, g, part, sems, dev, d).wait_send()

    on_own(rows_sent)

    def o1_sent(zp):
        @pl.when(jnp.logical_not(jnp.logical_and(mine, 2 * zp + c == z)))
        def _():
            o1(zp).wait_send()

    loop(0, 8, o1_sent)

    @pl.when(mine)
    def _():
        loop(1, 16, lambda i: o2(i).wait_send())

    o3.wait_send()
    swap.wait_send()
    u_swap.wait_send()
    d_swap.wait_send()

    def sixteen_sent(i):
        p_move(i).wait_send()
        qw_move(i).wait_send()
        pg_move(i).wait_send()
        hp_move(i).wait_send()
        qg_move(i).wait_send()
        u2_move(i).wait_send()
        d2_move(i).wait_send()
        u3_move(i).wait_send()

    loop(1, 16, sixteen_sent)

    def more_sent(k):
        qw_cross(k).wait_send()

        @pl.when(jnp.logical_not(d3_self(k)))
        def _():
            d3_move(k).wait_send()

    loop(0, 16, more_sent)
    loop(1, 32, lambda i: st_move((line + i) % 32).wait_send())

    loop(1, 32, lambda i: u4_move(i).wait_send())

    def u4_done(i):
        t = (up_own + i) % 32
        arrived(r.u4.at[t], r.su4, t)

    loop(1, 32, u4_done)
    ups = r.u4[...].reshape(512, 128)
    for k in range(4):
        col = slice(k * 128, (k + 1) * 128)
        r.uk_out[:, col] = ups[k * 64 : (k + 1) * 64]
        r.uv_out[:, col] = ups[256 + k * 64 : 256 + (k + 1) * 64]


def hand_over(*refs):
    half = len(refs) // 2
    for src, out in zip(refs[:half], refs[half:], strict=True):
        if len(src.shape) == 1:
            for j in range(src.shape[0]):
                out[j] = src[j]
        else:
            out[...] = src[...]


def rotary_tables(length):
    half = HEAD // 2
    frequency = ROTARY_BASE ** (-(np.arange(half) * 2.0 / HEAD))
    angles = np.arange(length)[:, None] * frequency[None, :]
    cosine, sine = np.cos(angles), np.sin(angles)
    return (
        np.concatenate([cosine, cosine], axis=1).astype(np.float32),
        np.concatenate([-sine, sine], axis=1).astype(np.float32),
    )


def shards(
    queries,
    passages,
    positives,
    hidden,
    norm_gain,
    last_query,
    frozen_key_weight,
    frozen_value_weight,
    key_down,
    key_adapter_up,
    value_down,
    value_adapter_up,
    out_weight,
):
    vm = pl.BlockSpec(memory_space=pltpu.VMEM)
    specs = [pl.BlockSpec(memory_space=pl.ANY)] * len(INPUTS)
    specs[INPUTS.index("pos_in")] = pl.BlockSpec(memory_space=pltpu.SMEM)
    for name in ("ku_in", "vu_in"):
        specs[INPUTS.index(name)] = vm
    shapes = ((2,), (2, 4096), (2, 4096), (8, 64), (8, 64), (64, 512), (64, 512))
    cosine, sine = rotary_tables(256)
    outs = (vm,) * len(shapes)
    outs = (pl.BlockSpec(memory_space=pltpu.SMEM), *outs[1:])
    results = pl.pallas_call(
        kernel,
        out_shape=tuple(jax.ShapeDtypeStruct(shape, F32) for shape in shapes),
        in_specs=specs,
        out_specs=outs,
        scratch_shapes=[pltpu.VMEM(shape, dtype) for shape, dtype in BUFFERS.values()]
        + [pltpu.SemaphoreType.DMA(shape) for shape in SEMAPHORES.values()],
        compiler_params=pltpu.CompilerParams(
            collective_id=0, has_side_effects=True, vmem_limit_bytes=VMEM_BYTES
        ),
    )(
        queries,
        passages,
        positives,
        hidden.reshape(512, 4096),
        norm_gain,
        last_query,
        frozen_key_weight,
        frozen_value_weight,
        key_down.T,
        key_adapter_up,
        value_down.T,
        value_adapter_up,
        out_weight,
        cosine,
        sine,
    )
    return pl.pallas_call(
        hand_over,
        out_shape=tuple(jax.ShapeDtypeStruct(shape, F32) for shape in shapes),
        in_specs=outs,
        out_specs=outs,
    )(*results)


def solution(mesh):
    rows = P(("batch", "fsdp"), None)
    placed = (
        rows,
        rows,
        P(("batch", "fsdp")),
        P(("batch", "fsdp"), None, None),
        P(),
        rows,
        P("fsdp", None),
        P("fsdp", None),
        P("fsdp", None),
        P(),
        P("fsdp", None),
        P(),
        P("batch", "fsdp"),
    )
    return jax.shard_map(
        shards,
        mesh=mesh,
        in_specs=placed,
        out_specs=(P(("batch", "fsdp")), rows, rows, rows, rows, P(), P()),
        check_vma=False,
    )
```
